512 devices in a mesh: row: 64 (over x, z, core), col: 8 (over y).
Axes of the slice: x: 4, y: 8, z: 8, core: 2. Of those that a mesh axis runs over, the one named last changes fastest.
Arguments:
- panel: float32 [32768, 256], P('row', 'col'), may hold values from -0.375 to 0.375
- trailing: float32 [32768, 8192], P('row', 'col'), may hold values from -6 to 6
- pivots: int32 [256], replicated, may hold values from 0 to 32767, as said below
Outputs:
- updated: float32 [32768, 8192], P('row', 'col')
The draws below stay inside these ranges and needn't reach their ends.
Inputs may be any that keep to these rules, and one draw needn't show every extreme that they name: pivots[i] is a row index from i to 32767.
All inputs are finite; a program needn't handle non-finite values.
Results may differ from the reference program's by a relative error of at most 0.000058.
Values sent between devices are 32-bit elements; how exact they have to be, the bound alone decides.
No kernel may reach another device: no remote copies, remote signals or barrier semaphores. Data moves between devices by JAX's collectives and lax.ppermute only.
A program may use at most 64 MiB of HBM per device.

```python
import jax
import jax.numpy as jnp
from jax import lax

NB = 256
ORDER = 32768
TRAIL = 8192


def draw_pivots(key, part):
    key = jax.random.fold_in(key, 11)
    first_key, second_key = jax.random.split(key)
    lowest = jnp.arange(NB, dtype=jnp.int32)
    picks = jax.random.randint(first_key, (NB,), lowest, ORDER, dtype=jnp.int32)
    marked = jax.random.randint(second_key, (), 1, NB, dtype=jnp.int32)
    picks = jnp.where(lowest == 0, 0, picks)
    return jnp.where(lowest == marked, ORDER - 1, picks).astype(jnp.int32)


def steps_of(own_key, extent, pieces, smallest, largest):
    gain = 1.0
    for position, parts in pieces:
        draws = jax.random.uniform(jax.random.fold_in(jax.random.fold_in(own_key, 6), position), (parts,), jnp.float32, smallest / len(pieces), largest / len(pieces))
        gain = gain * jnp.repeat(jnp.exp(draws), extent[position] // parts).reshape((-1,) + (1,) * (len(extent) - 1 - position))
    return gain


def normal_values(key, dims, spread, most, shards=(), held_as=jnp.bfloat16):
    loudness = steps_of(key, dims, shards, -0.22, 0.18) if shards else 1.0
    array = jax.random.normal(key, dims, jnp.float32) * spread * loudness
    return jnp.minimum(jnp.maximum(array, -most), most).astype(held_as)


def setup_inputs(seed: int = 0) -> dict:
    key_list = jax.random.split(jax.random.key(seed), 4)
    return {
        "panel": normal_values(key_list[0], (ORDER, NB), NB ** -0.5, 0.375, ((0, 64), (1, 8)), jnp.float32),
        "trailing": normal_values(key_list[1], (ORDER, TRAIL), 1.0, 6.0, ((0, 64), (1, 8)), jnp.float32),
        "pivots": draw_pivots(jax.random.fold_in(key_list[3], 71), 0),
    }


def row_sequence(pivots, order_total):
    sequence = jnp.arange(order_total, dtype=jnp.int32)

    def exchange_step(step_index, current):
        pivot_row = pivots[step_index].astype(jnp.int32)
        left_row = current[step_index]
        right_row = current[pivot_row]
        return current.at[step_index].set(right_row).at[pivot_row].set(left_row)
    return lax.fori_loop(0, pivots.shape[0], exchange_step, sequence)

def reference(panel, trailing, pivots):
    panel_width = panel.shape[1]
    sequence = row_sequence(pivots, trailing.shape[0])
    swapped = trailing[sequence]
    l_block = jnp.tril(panel[:panel_width], -1) + jnp.eye(panel_width, dtype=panel.dtype)
    u_block = lax.linalg.triangular_solve(l_block, swapped[:panel_width], left_side=True, lower=True)
    below = swapped[panel_width:] - jnp.dot(panel[panel_width:], u_block, precision=lax.Precision.HIGHEST)
    return jnp.concatenate([u_block, below], axis=0)
```

```python
import functools

import jax
import jax.numpy as jnp
from jax import lax
from jax.experimental import pallas as pl
from jax.experimental.pallas import tpu as pltpu
from jax.sharding import Mesh, PartitionSpec as P

NB = 256
ORDER = 32768
LANES = 128
X, Z, C, Y = 4, 8, 2, 8
BLOCKS = X * C
ROWS = ORDER // (X * Z * C)
COLS = BLOCKS * LANES
NARROW = 64
HIGHEST = lax.Precision.HIGHEST
VMEM = pl.BlockSpec(memory_space=pltpu.VMEM)
SMEM = pl.BlockSpec(memory_space=pltpu.SMEM)
PARAMS = pltpu.CompilerParams(vmem_limit_bytes=48 * 1024 * 1024)


def loop(count, body, unroll=1):
    def step(i, carry):
        body(i)
        return carry

    lax.fori_loop(0, count, step, 0, unroll=unroll)


def tile_of(row):
    return pl.ds(pl.multiple_of(lax.div(row, 8) * 8, 8), 8)


def picked(row, width):
    return lax.broadcasted_iota(jnp.int32, (8, width), 0) == lax.rem(row, 8)


def load_row(ref, row):
    tile = ref[tile_of(row), :]
    return jnp.sum(jnp.where(picked(row, tile.shape[1]), tile, 0.0), axis=0, keepdims=True)


def store_row(ref, row, values):
    at = tile_of(row)
    tile = ref[at, :]
    ref[at, :] = jnp.where(picked(row, tile.shape[1]), values, tile)


def plan_kernel(pivots, source, filler, place, slot_of, count, most, content):
    def start(i):
        content[pivots[i]] = pivots[i]

    def start_top(i):
        content[i] = i

    def exchange(i):
        at = pivots[i]
        left, right = content[i], content[at]
        content[i] = right
        content[at] = left

    loop(NB, start, 8)
    loop(NB, start_top, 8)
    loop(NB, exchange, 4)
    for z in range(Z):
        count[z] = 0

    def rank(i):
        origin = content[i]
        source[i] = origin
        filler[i] = jnp.where(origin >= NB, content[origin], 0)
        plane = lax.rem(lax.div(origin, ROWS * C), Z)
        have = count[plane]
        place[i] = plane * NB + have
        slot_of[plane * NB + have] = i
        count[plane] = have + 1

    loop(NB, rank, 4)
    peak = count[0]
    for z in range(1, Z):
        peak = jnp.maximum(peak, count[z])
    most[0] = peak


def make_plan(pivots):
    shape = lambda n: jax.ShapeDtypeStruct((n,), jnp.int32)
    return pl.pallas_call(
        plan_kernel,
        out_shape=[shape(NB), shape(NB), shape(NB), shape(Z * NB), shape(Z), shape(1)],
        in_specs=[SMEM],
        out_specs=[SMEM] * 6,
        scratch_shapes=[pltpu.SMEM((ORDER,), jnp.int32)],
        name="plan",
    )(pivots)


def first_row():
    return ((lax.axis_index("x") * Z + lax.axis_index("z")) * C + lax.axis_index("c")) * ROWS


def pack_kernel(cap, source, slot_of, count, trailing, panel_t, out):
    z = lax.axis_index("z")
    first = first_row()
    for b in range(BLOCKS):
        out[b, :cap, :] = jnp.zeros((cap, LANES), jnp.float32)
        out[b, cap : cap + NB, :] = trailing[:NB, b * LANES : (b + 1) * LANES]
        q, h = b // 2, b % 2
        out[b, cap + NB :, :] = panel_t[8 * q : 8 * q + 8, h * LANES : (h + 1) * LANES]

    def put(r):
        local = source[slot_of[z * NB + r]] - first

        @pl.when((local >= 0) & (local < ROWS))
        def _():
            row = load_row(trailing, local)
            for b in range(BLOCKS):
                out[b, pl.ds(r, 1), :] = row[:, b * LANES : (b + 1) * LANES]

    loop(count[z], put)


def spread_kernel(cap, filler, place, got, out):
    rows = got[0, :cap, :]
    for s in range(1, BLOCKS):
        rows = rows + got[s, :cap, :]
    for z in range(Z):
        out[z, :cap, :] = rows
        out[z, 2 * cap :, :] = got[0, cap + NB :, :]

    def put(i):
        where = place[i]
        plane, rank = lax.div(where, NB), lax.rem(where, NB)
        out[plane, pl.ds(cap + rank, 1), :] = got[0, pl.ds(cap + filler[i], 1), :]

    loop(NB, put, 8)


def collect_kernel(cap, place, got, out, lower):
    def take(i):
        where = place[i]
        plane, rank = lax.div(where, NB), lax.rem(where, NB)
        out[0, pl.ds(i, 1), :] = got[plane, pl.ds(rank, 1), :]

    loop(NB, take, 8)
    out[0, NB:, :] = got[0, cap : 2 * cap, :]
    for x in range(1, X):
        out[x] = out[0]
    piece = got[0, 2 * cap :, :]
    for k in range(BLOCKS * Y):
        lower[k] = piece


def invert_kernel(pieces, out, upper):
    for b in range(BLOCKS):
        q, h = b // 2, b % 2
        for y in range(Y):
            at = 32 * y + 8 * q
            upper[at : at + 8, h * LANES : (h + 1) * LANES] = pieces[b * Y + y]
    rows = lax.broadcasted_iota(jnp.int32, (NB, NB), 0)
    cols = lax.broadcasted_iota(jnp.int32, (NB, NB), 1)
    values = upper[...]
    dot = functools.partial(jnp.dot, precision=HIGHEST, preferred_element_type=jnp.float32)
    inverse = jnp.where(rows == cols, 1.0, 0.0)
    inverse = inverse - jnp.where((cols == rows + 1) & (rows % 2 == 0), values, 0.0)
    size = 2
    while size < NB:
        mask = (rows // (2 * size) == cols // (2 * size)) & (rows // size < cols // size)
        inverse = inverse - dot(dot(inverse, jnp.where(mask, values, 0.0)), inverse)
        size *= 2
    out[...] = inverse.T


def finish_kernel(cap, source, slot_of, count, own, other, inverse, panel_t, trailing, out,
                  top, upper, current, multipliers):
    c = lax.axis_index("c")
    z = lax.axis_index("z")
    first = first_row()
    for x in range(X):
        for side, ref in ((c, own), (1 - c, other)):
            lanes = pl.ds(pl.multiple_of((x * C + side) * LANES, LANES), LANES)
            top[:, lanes] = ref[x]
    upper[...] = jnp.dot(inverse[...], top[:NB], precision=HIGHEST, preferred_element_type=jnp.float32)
    multipliers[...] = panel_t[...].T
    current[...] = trailing[...]

    def put(r):
        local = source[slot_of[z * NB + r]] - first

        @pl.when((local >= 0) & (local < ROWS))
        def _():
            store_row(current, local, load_row(top, NB + r))

    loop(count[z], put)
    step = 128

    def rows(k):
        at = pl.ds(pl.multiple_of(k * step, step), step)
        out[at, :] = current[at, :] - jnp.dot(
            multipliers[at, :], upper[...], precision=HIGHEST, preferred_element_type=jnp.float32
        )

    loop(ROWS // step, rows)

    @pl.when(first == 0)
    def _():
        out[:NB, :] = upper[...]


def call(kernel, out_shape, smem, vmem, scratch=(), name=None):
    single = not isinstance(out_shape, list)
    shapes = [out_shape] if single else out_shape
    got = pl.pallas_call(
        kernel,
        out_shape=[jax.ShapeDtypeStruct(s, jnp.float32) for s in shapes],
        in_specs=[SMEM] * len(smem) + [VMEM] * len(vmem),
        out_specs=[VMEM] * len(shapes),
        scratch_shapes=list(scratch),
        compiler_params=PARAMS,
        name=name,
    )(*smem, *vmem)
    return got[0] if single else got


def step(cap, panel_t, trailing, source, filler, place, slot_of, count):
    spread = functools.partial(lax.all_to_all, split_axis=0, concat_axis=0, tiled=True)
    whole_t = spread(jnp.broadcast_to(panel_t[None], (Y,) + panel_t.shape), "y").reshape(NB, ROWS)
    packed = call(functools.partial(pack_kernel, cap), (BLOCKS, cap + NB + 8, LANES),
                  (source, slot_of, count), (trailing, panel_t), name="pack")
    packed = spread(packed, ("x", "c"))
    planes = call(functools.partial(spread_kernel, cap), (Z, 2 * cap + 8, LANES),
                  (filler, place), (packed,), name="spread")
    planes = spread(planes, "z")
    blocks, pieces = call(functools.partial(collect_kernel, cap),
                          [(X, NB + cap, LANES), (BLOCKS * Y, 8, LANES)],
                          (place,), (planes,), name="collect")
    pieces = spread(pieces, ("x", "c", "y"))
    own = spread(blocks, "x")
    other = lax.ppermute(own, "c", [(0, 1), (1, 0)])
    inverse = call(invert_kernel, (NB, NB), (), (pieces,),
                   [pltpu.VMEM((NB, NB), jnp.float32)], name="invert")
    scratch = [pltpu.VMEM(s, jnp.float32)
               for s in ((NB + cap, COLS), (NB, COLS), (ROWS, COLS), (ROWS, NB))]
    return call(functools.partial(finish_kernel, cap), (ROWS, COLS), (source, slot_of, count),
                (own, other, inverse, whole_t, trailing), scratch, name="finish")


def shards(panel, trailing, pivots):
    source, filler, place, slot_of, count, most = make_plan(pivots)
    return lax.cond(
        most[0] <= NARROW,
        functools.partial(step, NARROW),
        functools.partial(step, NB),
        panel.T, trailing, source, filler, place, slot_of, count,
    )


def solution(mesh):
    fine = Mesh(mesh.devices.reshape(X, Z, C, Y), ("x", "z", "c", "y"))
    split = P(("x", "z", "c"), "y")
    return jax.shard_map(shards, mesh=fine, in_specs=(split, split, P()), out_specs=split, check_vma=False)
```

```python
import functools

import jax
import jax.numpy as jnp
from jax import lax
from jax.experimental import pallas as pl
from jax.experimental.pallas import tpu as pltpu
from jax.sharding import Mesh, PartitionSpec as P

NB = 256
ORDER = 32768
LANES = 128
X, Z, C, Y = 4, 8, 2, 8
BLOCKS = X * C
ROWS = ORDER // (X * Z * C)
COLS = BLOCKS * LANES
NARROW = 64
HIGHEST = lax.Precision.HIGHEST
VMEM = pl.BlockSpec(memory_space=pltpu.VMEM)
SMEM = pl.BlockSpec(memory_space=pltpu.SMEM)
PARAMS = pltpu.CompilerParams(vmem_limit_bytes=48 * 1024 * 1024)


def loop(count, body, unroll=1):
    def step(i, carry):
        body(i)
        return carry

    lax.fori_loop(0, count, step, 0, unroll=unroll)


def tile_of(row):
    return pl.ds(pl.multiple_of(lax.div(row, 8) * 8, 8), 8)


def picked(row, width):
    return lax.broadcasted_iota(jnp.int32, (8, width), 0) == lax.rem(row, 8)


def load_row(ref, row):
    tile = ref[tile_of(row), :]
    return jnp.sum(jnp.where(picked(row, tile.shape[1]), tile, 0.0), axis=0, keepdims=True)


def store_row(ref, row, values):
    at = tile_of(row)
    tile = ref[at, :]
    ref[at, :] = jnp.where(picked(row, tile.shape[1]), values, tile)


def plane_of(row):
    return lax.rem(lax.div(row, ROWS * C), Z)


def plan_kernel(pivots, source, filler, place, slot_of, count, most, content):
    def start(i):
        content[pivots[i]] = pivots[i]

    def start_top(i):
        content[i] = i

    def exchange(i):
        at = pivots[i]
        left, right = content[i], content[at]
        content[i] = right
        content[at] = left

    loop(NB, start, 8)
    loop(NB, start_top, 8)
    loop(NB, exchange, 4)
    for z in range(Z):
        count[z] = 0

    def rank(i):
        origin = content[i]
        source[i] = origin
        filler[i] = jnp.where(origin >= NB, content[origin], 0)
        plane = plane_of(origin)
        have = count[plane]
        place[i] = plane * NB + have
        slot_of[plane * NB + have] = i
        count[plane] = have + 1

    loop(NB, rank, 4)
    peak = count[0]
    for z in range(1, Z):
        peak = jnp.maximum(peak, count[z])
    most[0] = peak


def make_plan(pivots):
    shape = lambda n: jax.ShapeDtypeStruct((n,), jnp.int32)
    return pl.pallas_call(
        plan_kernel,
        out_shape=[shape(NB), shape(NB), shape(NB), shape(Z * NB), shape(Z), shape(1)],
        in_specs=[SMEM],
        out_specs=[SMEM] * 6,
        scratch_shapes=[pltpu.SMEM((ORDER,), jnp.int32)],
        cost_estimate=pl.CostEstimate(flops=0, bytes_accessed=16 * 1024 * 1024, transcendentals=0),
        name="plan",
    )(pivots)


def first_row():
    return ((lax.axis_index("x") * Z + lax.axis_index("z")) * C + lax.axis_index("c")) * ROWS


def pack_kernel(cap, pivots, trailing, panel_t, out, seen):
    z = lax.axis_index("z")
    first = first_row()
    for b in range(BLOCKS):
        out[b, :cap, :] = jnp.zeros((cap, LANES), jnp.float32)
        out[b, cap : cap + NB, :] = trailing[:NB, b * LANES : (b + 1) * LANES]
        q, h = b // 2, b % 2
        out[b, cap + NB :, :] = panel_t[8 * q : 8 * q + 8, h * LANES : (h + 1) * LANES]

    def clear(i):
        seen[pivots[i]] = 0

    loop(NB, clear, 8)

    def put(i, rank):
        row = pivots[i]
        again = seen[row]
        seen[row] = 1
        local = row - first

        @pl.when((again == 0) & (local >= 0) & (local < ROWS))
        def _():
            values = load_row(trailing, local)
            at = pl.ds(jnp.minimum(rank, cap - 1), 1)
            for b in range(BLOCKS):
                out[b, at, :] = values[:, b * LANES : (b + 1) * LANES]

        plane = jnp.where(again == 1, 0, plane_of(row))
        return rank + (plane == z).astype(jnp.int32)

    lax.fori_loop(0, NB, put, jnp.int32(0), unroll=4)


def spread_kernel(cap, source, filler, place, slot_of, count, got, out):
    for z in range(Z):
        out[z, 2 * cap :, :] = got[0, cap + NB :, :]
    rows = got[0, :cap, :]
    for s in range(1, BLOCKS):
        rows = rows + got[s, :cap, :]
    out[0, :cap, :] = rows

    @pl.when(lax.axis_index("z") == 0)
    def _():
        def top(r):
            origin = source[slot_of[r]]

            @pl.when(origin < NB)
            def _():
                out[0, pl.ds(r, 1), :] = got[0, pl.ds(cap + origin, 1), :]

        loop(jnp.minimum(count[0], cap), top)

        def put(i):
            where = place[i]
            plane, rank = lax.div(where, NB), jnp.minimum(lax.rem(where, NB), cap - 1)
            out[plane, pl.ds(cap + rank, 1), :] = got[0, pl.ds(cap + filler[i], 1), :]

        loop(NB, put, 8)

    for z in range(1, Z):
        out[z, :cap, :] = out[0, :cap, :]


def collect_kernel(cap, place, got, pieces, out):
    def take(i):
        where = place[i]
        plane, rank = lax.div(where, NB), jnp.minimum(lax.rem(where, NB), cap - 1)
        out[0, pl.ds(i, 1), :] = got[plane, pl.ds(rank, 1), :]

    loop(NB, take, 8)
    out[0, NB : NB + cap, :] = got[0, cap : 2 * cap, :]
    for y in range(Y):
        out[0, NB + cap + 8 * y : NB + cap + 8 * y + 8, :] = pieces[y]
    for x in range(1, X):
        out[x] = out[0]


def invert_kernel(cap, own, other, out, upper):
    c = lax.axis_index("c")
    for x in range(X):
        for side, ref in ((c, own), (1 - c, other)):
            lanes = pl.ds(pl.multiple_of(side * LANES, LANES), LANES)
            for y in range(Y):
                at = 32 * y + 8 * x
                upper[at : at + 8, lanes] = ref[x, NB + cap + 8 * y : NB + cap + 8 * y + 8, :]
    rows = lax.broadcasted_iota(jnp.int32, (NB, NB), 0)
    cols = lax.broadcasted_iota(jnp.int32, (NB, NB), 1)
    values = upper[...]
    dot = functools.partial(jnp.dot, precision=HIGHEST, preferred_element_type=jnp.float32)
    inverse = jnp.where(rows == cols, 1.0, 0.0)
    inverse = inverse - jnp.where((cols == rows + 1) & (rows % 2 == 0), values, 0.0)
    size = 2
    while size < NB:
        mask = (rows // (2 * size) == cols // (2 * size)) & (rows // size < cols // size)
        inverse = inverse - dot(dot(inverse, jnp.where(mask, values, 0.0)), inverse)
        size *= 2
    out[...] = inverse.T


def finish_kernel(cap, source, slot_of, count, own, other, inverse, whole_t, trailing, out,
                  top, upper, current, multipliers, sem):
    copy = pltpu.make_async_copy(trailing, current, sem)
    copy.start()
    c = lax.axis_index("c")
    z = lax.axis_index("z")
    first = first_row()
    for x in range(X):
        for side, ref in ((c, own), (1 - c, other)):
            lanes = pl.ds(pl.multiple_of((x * C + side) * LANES, LANES), LANES)
            top[:, lanes] = ref[x, : NB + cap]
    upper[...] = jnp.dot(inverse[...], top[:NB], precision=HIGHEST, preferred_element_type=jnp.float32)
    for y in range(Y):
        multipliers[:, 32 * y : 32 * y + 32] = whole_t[y, c].T
    copy.wait()

    def put(r):
        local = source[slot_of[z * NB + r]] - first

        @pl.when((local >= 0) & (local < ROWS))
        def _():
            store_row(current, local, load_row(top, NB + r))

    loop(jnp.minimum(count[z], cap), put)
    step = 128

    def rows(k):
        at = pl.ds(pl.multiple_of(k * step, step), step)
        out[at, :] = current[at, :] - jnp.dot(
            multipliers[at, :], upper[...], precision=HIGHEST, preferred_element_type=jnp.float32
        )

    loop(ROWS // step, rows)

    @pl.when(first == 0)
    def _():
        out[:NB, :] = upper[...]


def call(kernel, shape, smem, vmem, scratch=(), name=None, last=VMEM, busy=2):
    return pl.pallas_call(
        kernel,
        out_shape=jax.ShapeDtypeStruct(shape, jnp.float32),
        in_specs=[SMEM] * len(smem) + [VMEM] * (len(vmem) - 1) + [last],
        out_specs=VMEM,
        scratch_shapes=list(scratch),
        compiler_params=PARAMS,
        cost_estimate=pl.CostEstimate(flops=0, bytes_accessed=busy * 2**20, transcendentals=0),
        name=name,
    )(*smem, *vmem)


def exchange(cap, panel_t, trailing, pivots, plan):
    source, filler, place, slot_of, count = plan
    spread = functools.partial(lax.all_to_all, split_axis=0, concat_axis=0, tiled=True)
    packed = call(functools.partial(pack_kernel, cap), (BLOCKS, cap + NB + 8, LANES),
                  (pivots,), (trailing, panel_t), [pltpu.SMEM((ORDER,), jnp.int32)], name="pack")
    packed = spread(packed, ("x", "c"))
    planes = call(functools.partial(spread_kernel, cap), (Z, 2 * cap + 8, LANES),
                  (source, filler, place, slot_of, count), (packed,), name="spread")
    planes = spread(planes, "z")
    pieces = spread(jnp.broadcast_to(planes[:1, 2 * cap :], (Y, 8, LANES)), "y")
    blocks = call(functools.partial(collect_kernel, cap), (X, NB + cap + 8 * Y, LANES),
                  (place,), (planes, pieces), name="collect")
    own = spread(blocks, "x")
    other = lax.ppermute(own, "c", [(0, 1), (1, 0)])
    inverse = call(functools.partial(invert_kernel, cap), (NB, NB), (), (own, other),
                   [pltpu.VMEM((NB, NB), jnp.float32)], name="invert", busy=16)
    return own, other, inverse


def finish(cap, own, other, inverse, whole_t, trailing, plan):
    source, _, _, slot_of, count = plan
    scratch = [pltpu.VMEM(s, jnp.float32)
               for s in ((NB + cap, COLS), (NB, COLS), (ROWS, COLS), (ROWS, NB))]
    return call(functools.partial(finish_kernel, cap), (ROWS, COLS), (source, slot_of, count),
                (own, other, inverse, whole_t, trailing), scratch + [pltpu.SemaphoreType.DMA],
                name="finish", last=pl.BlockSpec(memory_space=pl.ANY), busy=16)


def shards(panel, trailing, pivots):
    panel_t = panel.T
    whole_t = lax.all_gather(panel_t, ("y", "c"), axis=0).reshape(Y, C, 32, ROWS)
    *plan, most = make_plan(pivots)
    ready = exchange(NARROW, panel_t, trailing, pivots, plan)

    def narrow(ready, panel_t, whole_t, trailing, pivots, plan):
        return finish(NARROW, *ready, whole_t, trailing, plan)

    def wide(ready, panel_t, whole_t, trailing, pivots, plan):
        return finish(NB, *exchange(NB, panel_t, trailing, pivots, plan), whole_t, trailing, plan)

    return lax.cond(most[0] <= NARROW, narrow, wide, ready, panel_t, whole_t, trailing, pivots, plan)


def solution(mesh):
    fine = Mesh(mesh.devices.reshape(X, Z, C, Y), ("x", "z", "c", "y"))
    split = P(("x", "z", "c"), "y")
    return jax.shard_map(shards, mesh=fine, in_specs=(split, split, P()), out_specs=split, check_vma=False)
```

```python
import functools

import jax
import jax.numpy as jnp
from jax import lax
from jax.experimental import pallas as pl
from jax.experimental.pallas import tpu as pltpu
from jax.sharding import Mesh, PartitionSpec as P

NB = 256
ORDER = 32768
LANES = 128
X, Z, C, Y = 4, 8, 2, 8
BLOCKS = X * C
ROWS = ORDER // (X * Z * C)
COLS = BLOCKS * LANES
DIAG = NB // Y
BATCH = 16
BITS = NB.bit_length() - 1
PLANE_BITS = (ROWS * C).bit_length() - 1
NARROW = 64
HIGHEST = lax.Precision.HIGHEST
VMEM = pl.BlockSpec(memory_space=pltpu.VMEM)
SMEM = pl.BlockSpec(memory_space=pltpu.SMEM)
PARAMS = pltpu.CompilerParams(vmem_limit_bytes=48 * 1024 * 1024)


def loop(count, body, unroll=1):
    def step(i, carry):
        body(i)
        return carry

    lax.fori_loop(0, count, step, 0, unroll=unroll)


def tile_of(row):
    return pl.ds(pl.multiple_of(row & -8, 8), 8)


def picked(row, width):
    return lax.broadcasted_iota(jnp.int32, (8, width), 0) == (row & 7)


def load_row(ref, row):
    tile = ref[tile_of(row), :]
    return jnp.sum(jnp.where(picked(row, tile.shape[1]), tile, 0.0), axis=0, keepdims=True)


def store_row(ref, row, values):
    at = tile_of(row)
    tile = ref[at, :]
    ref[at, :] = jnp.where(picked(row, tile.shape[1]), values, tile)


def plane_of(row):
    return (row >> PLANE_BITS) & (Z - 1)


def first_row():
    return ((lax.axis_index("x") * Z + lax.axis_index("z")) * C + lax.axis_index("c")) * ROWS


def plan_kernel(pivots, filler, place, slot_of, tops, count, most, content):
    def start(i):
        content[pivots[i]] = pivots[i]

    def start_top(i):
        content[i] = i

    loop(NB, start, 8)
    loop(NB, start_top, 8)

    def exchange(i, found):
        at = pivots[i]
        left, right = content[i], content[at]
        content[i] = right
        content[at] = left
        tops[found] = i * NB + right
        return found + (right != at).astype(jnp.int32)

    found = lax.fori_loop(0, NB, exchange, jnp.int32(0), unroll=4)
    for z in range(Z):
        count[z] = 0

    def rank(i):
        row = pivots[i]
        filler[i] = jnp.where(row < NB, 0, content[row])
        plane = plane_of(row)
        have = count[plane]
        place[i] = plane * NB + have
        slot_of[plane * NB + have] = i
        count[plane] = have + 1

    loop(NB, rank, 4)
    count[Z] = found
    peak = count[0]
    for z in range(1, Z):
        peak = jnp.maximum(peak, count[z])
    most[0] = peak + found


def make_plan(pivots):
    sizes = (NB, NB, Z * NB, NB + 8, Z + 1, 1)
    return pl.pallas_call(
        plan_kernel,
        out_shape=[jax.ShapeDtypeStruct((n,), jnp.int32) for n in sizes],
        in_specs=[SMEM],
        out_specs=[SMEM] * len(sizes),
        scratch_shapes=[pltpu.SMEM((ORDER,), jnp.int32)],
        cost_estimate=pl.CostEstimate(flops=0, bytes_accessed=16 * 1024 * 1024, transcendentals=0),
        name="plan",
    )(pivots)


def invert_diagonal(panel_t, at):
    y = lax.axis_index("y")
    lanes = pl.ds(pl.multiple_of((y * DIAG) & -LANES, LANES), LANES)
    shift = (y * DIAG) & (LANES - 1)
    window = pltpu.roll(panel_t[:, lanes], (LANES - shift) & (LANES - 1), axis=1)
    rows = lax.broadcasted_iota(jnp.int32, (DIAG, LANES), 0)
    cols = lax.broadcasted_iota(jnp.int32, (DIAG, LANES), 1)
    strict = (cols > rows) & (cols < DIAG)
    values = jnp.where(strict, window, 0.0)
    inverse = jnp.where(rows == cols, 1.0, 0.0)
    for k in range(DIAG - 1, 0, -1):
        inverse = inverse - values[:, k : k + 1] * inverse[k : k + 1, :]
    window = jnp.where(strict, inverse, window)
    at[:, :] = panel_t[:, :NB]
    at[:, lanes] = pltpu.roll(window, shift, axis=1)


def pack_kernel(cap, pivots, panel_t, trailing, out, triangle, rows, mine, sem):
    copy = pltpu.make_async_copy(trailing, rows, sem)
    copy.start()
    z = lax.axis_index("z")
    first = first_row()

    def find(i, carry):
        rank, found = carry
        row = pivots[i]
        local = row - first
        mine[found] = local * NB + jnp.minimum(rank, cap - 1)
        hit = (local >= 0) & (local < ROWS)
        return rank + (plane_of(row) == z).astype(jnp.int32), found + hit.astype(jnp.int32)

    _, found = lax.fori_loop(0, NB, find, (jnp.int32(0), jnp.int32(0)), unroll=16)
    invert_diagonal(panel_t, triangle)
    for b in range(BLOCKS):
        out[b, :cap, :] = jnp.zeros((cap, LANES), jnp.float32)
        q, h = b // C, b % C
        out[b, cap + NB :, :] = triangle[8 * q : 8 * q + 8, h * LANES : (h + 1) * LANES]
    copy.wait()
    for b in range(BLOCKS):
        out[b, cap : cap + NB, :] = rows[:NB, b * LANES : (b + 1) * LANES]

    def put(k):
        entry = mine[k]
        values = load_row(rows, entry >> BITS)
        at = pl.ds(entry & (NB - 1), 1)
        for b in range(BLOCKS):
            out[b, at, :] = values[:, b * LANES : (b + 1) * LANES]

    loop(found, put)


def spread_kernel(cap, room, filler, place, tops, count, got, out):
    for z in range(Z):
        out[z, cap + room :, :] = got[0, cap + NB :, :]
    rows = got[0, :cap, :]
    for s in range(1, BLOCKS):
        rows = rows + got[s, :cap, :]
    for z in range(Z):
        out[z, :cap, :] = rows

    @pl.when(lax.axis_index("z") == 0)
    def _():
        def put(k):
            moves = []
            for i in range(BATCH):
                where = place[k * BATCH + i]
                rank = jnp.minimum(where & (NB - 1), cap - 1)
                values = got[0, pl.ds(cap + filler[k * BATCH + i], 1), :]
                moves.append((where >> BITS, cap + rank, values))
            for plane, at, values in moves:
                out[plane, pl.ds(at, 1), :] = values

        loop(NB // BATCH, put)

        def top(k):
            values = got[0, pl.ds(cap + (tops[k] & (NB - 1)), 1), :]
            for z in range(Z):
                out[z, pl.ds(cap + jnp.minimum(count[z] + k, room - 1), 1), :] = values

        loop(count[Z], top)


def collect_kernel(cap, room, place, tops, count, got, pieces, out):
    z = lax.axis_index("z")

    def take(k):
        base = pl.multiple_of(k * BATCH, BATCH)
        rows = []
        for i in range(BATCH):
            where = place[base + i]
            rank = jnp.minimum(where & (NB - 1), cap - 1)
            rows.append(got[where >> BITS, pl.ds(rank, 1), :])
        for i in range(BATCH):
            out[0, pl.ds(base + i, 1), :] = rows[i]

    loop(NB // BATCH, take)

    def top(k):
        at = cap + jnp.minimum(count[z] + k, room - 1)
        out[0, pl.ds(tops[k] >> BITS, 1), :] = got[0, pl.ds(at, 1), :]

    loop(count[Z], top)
    out[0, NB : NB + cap, :] = got[0, cap : 2 * cap, :]
    for y in range(Y):
        out[0, NB + cap + 8 * y : NB + cap + 8 * y + 8, :] = pieces[y]
    for x in range(1, X):
        out[x] = out[0]


def dot(a, b):
    return jnp.dot(a, b, precision=HIGHEST, preferred_element_type=jnp.float32)


def invert(upper):
    half = NB // 2
    rows = lax.broadcasted_iota(jnp.int32, (half, half), 0)
    cols = lax.broadcasted_iota(jnp.int32, (half, half), 1)
    parts = []
    for k in range(2):
        values = upper[k * half : (k + 1) * half, k * half : (k + 1) * half]
        part = jnp.where((rows // DIAG == cols // DIAG) & (rows < cols), values, 0.0)
        part = part + jnp.where(rows == cols, 1.0, 0.0)
        parts.append((values, part))
    size = DIAG
    while size < half:
        mask = (rows // (2 * size) == cols // (2 * size)) & (rows // size < cols // size)
        parts = [(v, p - dot(dot(p, jnp.where(mask, v, 0.0)), p)) for v, p in parts]
        size *= 2
    (_, first), (_, second) = parts
    corner = -dot(dot(first, upper[:half, half:]), second)
    left = jnp.concatenate([first.T, corner.T], axis=0)
    right = jnp.concatenate([jnp.zeros((half, half), jnp.float32), second.T], axis=0)
    return jnp.concatenate([left, right], axis=1)


def turn_kernel(whole_t, out):
    c = lax.axis_index("c")
    for y in range(Y):
        out[:, DIAG * y : DIAG * (y + 1)] = whole_t[y, c].T


def finish_kernel(cap, pivots, slot_of, count, own, other, multipliers, trailing, out,
                  upper, inverse, block, current, in_sem, out_sem):
    copy = pltpu.make_async_copy(trailing, current, in_sem)
    copy.start()
    c = lax.axis_index("c")
    z = lax.axis_index("z")
    first = first_row()
    sides = ((pl.multiple_of(c * LANES, LANES), own), (pl.multiple_of((1 - c) * LANES, LANES), other))
    for x in range(X):
        for lane, ref in sides:
            for y in range(Y):
                at = DIAG * y + 8 * x
                upper[at : at + 8, pl.ds(lane, LANES)] = ref[x, NB + cap + 8 * y : NB + cap + 8 * y + 8, :]
    inverse[...] = invert(upper)
    copy.wait()

    def put(r):
        local = pivots[slot_of[z * NB + r]] - first

        @pl.when((local >= 0) & (local < ROWS))
        def _():
            at = tile_of(local)
            hit = picked(local, LANES)
            for x in range(X):
                for lane, ref in sides:
                    lanes = pl.ds(pl.multiple_of(x * C * LANES + lane, LANES), LANES)
                    current[at, lanes] = jnp.where(hit, ref[x, pl.ds(NB + r, 1), :], current[at, lanes])

    loop(jnp.minimum(count[z], cap), put)
    copies = []
    width = C * LANES
    for x in range(X):
        lanes = slice(x * width, (x + 1) * width)
        for lane, ref in sides:
            block[x, :, pl.ds(lane, LANES)] = ref[x, :NB, :]
        solved = dot(inverse[...], block[x])
        block[x] = solved
        current[:, lanes] = current[:, lanes] - dot(multipliers[...], solved)

        @pl.when(first == 0)
        def _():
            current[:NB, lanes] = block[x]

        copies.append(pltpu.make_async_copy(current.at[:, lanes], out.at[:, lanes], out_sem.at[x]))
        copies[-1].start()
    for copy in copies:
        copy.wait()


def call(kernel, shape, smem, vmem, scratch=(), name=None, last=VMEM, out=VMEM, busy=2):
    return pl.pallas_call(
        kernel,
        out_shape=jax.ShapeDtypeStruct(shape, jnp.float32),
        in_specs=[SMEM] * len(smem) + [VMEM] * (len(vmem) - 1) + [last],
        out_specs=out,
        scratch_shapes=list(scratch),
        compiler_params=PARAMS,
        cost_estimate=pl.CostEstimate(flops=0, bytes_accessed=busy * 2**20, transcendentals=0),
        name=name,
    )(*smem, *vmem)


def pack(cap, pivots, trailing, panel_t):
    scratch = [pltpu.VMEM((DIAG, NB), jnp.float32), pltpu.VMEM((ROWS, COLS), jnp.float32),
               pltpu.SMEM((NB + 8,), jnp.int32), pltpu.SemaphoreType.DMA]
    return call(functools.partial(pack_kernel, cap), (BLOCKS, cap + NB + 8, LANES),
                (pivots,), (panel_t, trailing), scratch, name="pack", last=pl.BlockSpec(memory_space=pl.ANY))


def spread(cap, room, plan, packed):
    filler, place, _, tops, count = plan
    return call(functools.partial(spread_kernel, cap, room), (Z, cap + room + 8, LANES),
                (filler, place, tops, count), (packed,), name="spread")


def collect(cap, room, plan, planes, pieces):
    _, place, _, tops, count = plan
    return call(functools.partial(collect_kernel, cap, room), (X, NB + cap + 8 * Y, LANES),
                (place, tops, count), (planes, pieces), name="collect")


def finish(cap, pivots, plan, own, other, multipliers, trailing):
    _, _, slot_of, _, count = plan
    scratch = [pltpu.VMEM(s, jnp.float32) for s in ((NB, NB), (NB, NB), (X, NB, C * LANES), (ROWS, COLS))]
    scratch += [pltpu.SemaphoreType.DMA, pltpu.SemaphoreType.DMA((X,))]
    return call(functools.partial(finish_kernel, cap), (ROWS, COLS), (pivots, slot_of, count),
                (own, other, multipliers, trailing), scratch, name="finish",
                last=pl.BlockSpec(memory_space=pl.ANY), out=pl.BlockSpec(memory_space=pltpu.HBM), busy=16)


def exchange(cap, room, panel_t, trailing, pivots, plan):
    swap = functools.partial(lax.all_to_all, split_axis=0, concat_axis=0, tiled=True)
    packed = swap(pack(cap, pivots, trailing, panel_t), ("x", "c"))
    planes = swap(spread(cap, room, plan, packed), "z")
    pieces = swap(jnp.broadcast_to(planes[:1, cap + room :], (Y, 8, LANES)), "y")
    own = swap(collect(cap, room, plan, planes, pieces), "x")
    return own, lax.ppermute(own, "c", [(0, 1), (1, 0)])


def shards(panel, trailing, pivots):
    panel_t = panel.T
    whole_t = lax.all_gather(panel_t, ("y", "c"), axis=0).reshape(Y, C, DIAG, ROWS)
    multipliers = call(turn_kernel, (ROWS, NB), (), (whole_t,), name="turn")
    *plan, most = make_plan(pivots)

    def with_room(cap, room):
        ready = exchange(cap, room, panel_t, trailing, pivots, plan)
        return finish(cap, pivots, plan, *ready, multipliers, trailing)

    def pending(carry):
        return carry[0]

    def again(carry):
        return jnp.zeros_like(carry[0]), with_room(NB, 2 * NB)

    return lax.while_loop(pending, again, (most[0] > NARROW, with_room(NARROW, NARROW)))[1]


def solution(mesh):
    fine = Mesh(mesh.devices.reshape(X, Z, C, Y), ("x", "z", "c", "y"))
    split = P(("x", "z", "c"), "y")
    return jax.shard_map(shards, mesh=fine, in_specs=(split, split, P()), out_specs=split, check_vma=False)
```

```python
import functools

import jax
import jax.numpy as jnp
from jax import lax
from jax.experimental import pallas as pl
from jax.experimental.pallas import tpu as pltpu
from jax.sharding import Mesh, PartitionSpec as P

NB = 256
ORDER = 32768
LANES = 128
X, Z, C, Y = 4, 8, 2, 8
BLOCKS = X * C
ROWS = ORDER // (X * Z * C)
COLS = BLOCKS * LANES
DIAG = NB // Y
BATCH = 16
BITS = NB.bit_length() - 1
PLANE_BITS = (ROWS * C).bit_length() - 1
NARROW = 64
HIGHEST = lax.Precision.HIGHEST
VMEM = pl.BlockSpec(memory_space=pltpu.VMEM)
SMEM = pl.BlockSpec(memory_space=pltpu.SMEM)
PARAMS = pltpu.CompilerParams(vmem_limit_bytes=48 * 1024 * 1024)


def loop(count, body, unroll=1):
    def step(i, carry):
        body(i)
        return carry

    lax.fori_loop(0, count, step, 0, unroll=unroll)


def tile_of(row):
    return pl.ds(pl.multiple_of(row & -8, 8), 8)


def picked(row, width):
    return lax.broadcasted_iota(jnp.int32, (8, width), 0) == (row & 7)


def load_row(ref, row):
    tile = ref[tile_of(row), :]
    return jnp.sum(jnp.where(picked(row, tile.shape[1]), tile, 0.0), axis=0, keepdims=True)


def store_row(ref, row, values):
    at = tile_of(row)
    tile = ref[at, :]
    ref[at, :] = jnp.where(picked(row, tile.shape[1]), values, tile)


def plane_of(row):
    return (row >> PLANE_BITS) & (Z - 1)


def first_row():
    return ((lax.axis_index("x") * Z + lax.axis_index("z")) * C + lax.axis_index("c")) * ROWS


def plan_kernel(pivots, filler, place, slot_of, tops, count, most, content):
    def start(i):
        content[pivots[i]] = pivots[i]

    def start_top(i):
        content[i] = i

    loop(NB, start, 8)
    loop(NB, start_top, 8)

    def exchange(i, found):
        at = pivots[i]
        left, right = content[i], content[at]
        content[i] = right
        content[at] = left
        tops[found] = i * NB + right
        return found + (right != at).astype(jnp.int32)

    found = lax.fori_loop(0, NB, exchange, jnp.int32(0), unroll=4)
    for z in range(Z):
        count[z] = 0

    def rank(i):
        row = pivots[i]
        filler[i] = jnp.where(row < NB, 0, content[row])
        plane = plane_of(row)
        have = count[plane]
        place[i] = plane * NB + have
        slot_of[plane * NB + have] = i
        count[plane] = have + 1

    loop(NB, rank, 4)
    count[Z] = found
    peak = count[0]
    for z in range(1, Z):
        peak = jnp.maximum(peak, count[z])
    most[0] = peak + found


def make_plan(pivots):
    sizes = (NB, NB, Z * NB, NB + 8, Z + 1, 1)
    return pl.pallas_call(
        plan_kernel,
        out_shape=[jax.ShapeDtypeStruct((n,), jnp.int32) for n in sizes],
        in_specs=[SMEM],
        out_specs=[SMEM] * len(sizes),
        scratch_shapes=[pltpu.SMEM((ORDER,), jnp.int32)],
        cost_estimate=pl.CostEstimate(flops=0, bytes_accessed=16 * 1024 * 1024, transcendentals=0),
        name="plan",
    )(pivots)


def invert_diagonal(panel_t, at):
    y = lax.axis_index("y")
    lanes = pl.ds(pl.multiple_of((y * DIAG) & -LANES, LANES), LANES)
    shift = (y * DIAG) & (LANES - 1)
    window = pltpu.roll(panel_t[:, lanes], (LANES - shift) & (LANES - 1), axis=1)
    rows = lax.broadcasted_iota(jnp.int32, (DIAG, LANES), 0)
    cols = lax.broadcasted_iota(jnp.int32, (DIAG, LANES), 1)
    strict = (cols > rows) & (cols < DIAG)
    values = jnp.where(strict, window, 0.0)
    inverse = jnp.where(rows == cols, 1.0, 0.0)
    for k in range(DIAG - 1, 0, -1):
        inverse = inverse - values[:, k : k + 1] * inverse[k : k + 1, :]
    window = jnp.where(strict, inverse, window)
    at[:, :] = panel_t[:, :NB]
    at[:, lanes] = pltpu.roll(window, shift, axis=1)


def pack_kernel(cap, pivots, panel_t, trailing, keep, send, triangle, rows, mine, sem):
    copy = pltpu.make_async_copy(trailing, rows, sem)
    copy.start()
    z = lax.axis_index("z")
    c = lax.axis_index("c")
    first = first_row()

    def find(i, carry):
        rank, found = carry
        row = pivots[i]
        local = row - first
        mine[found] = local * NB + jnp.minimum(rank, cap - 1)
        hit = (local >= 0) & (local < ROWS)
        return rank + (plane_of(row) == z).astype(jnp.int32), found + hit.astype(jnp.int32)

    _, found = lax.fori_loop(0, NB, find, (jnp.int32(0), jnp.int32(0)), unroll=16)
    invert_diagonal(panel_t, triangle)
    sides = ((keep, c), (send, 1 - c))
    for out, side in sides:
        for x in range(X):
            out[x, :cap, :] = jnp.zeros((cap, LANES), jnp.float32)
            lanes = pl.ds(pl.multiple_of(side * LANES, LANES), LANES)
            out[x, cap + NB :, :] = triangle[8 * x : 8 * x + 8, lanes]
    copy.wait()
    for out, side in sides:
        for x in range(X):
            lanes = pl.ds(pl.multiple_of((x * C + side) * LANES, LANES), LANES)
            out[x, cap : cap + NB, :] = rows[:NB, lanes]

    def put(k):
        entry = mine[k]
        row = entry >> BITS
        at = pl.ds(entry & (NB - 1), 1)
        hit = picked(row, LANES)
        for out, side in sides:
            for x in range(X):
                lanes = pl.ds(pl.multiple_of((x * C + side) * LANES, LANES), LANES)
                tile = jnp.where(hit, rows[tile_of(row), lanes], 0.0)
                out[x, at, :] = jnp.sum(tile, axis=0, keepdims=True)

    loop(found, put)


def join_kernel(cap, keep, got, *blocks):
    x = lax.axis_index("x")
    c = lax.axis_index("c")
    for s, out in enumerate(blocks):
        at = (x + s) & (X - 1)
        out[:cap, :] = keep[at, :cap, :] + got[at, :cap, :]
        out[cap:, :] = jnp.where(c == 0, keep[at, cap:, :], got[at, cap:, :])


def spread_kernel(cap, room, filler, place, tops, count, *refs):
    blocks, out, former = refs[:X], refs[-2], refs[-1]
    x = lax.axis_index("x")
    rest = blocks[0][cap:, :]
    for s in range(1, X):
        rest = jnp.where(x == s, blocks[s][cap:, :], rest)
    former[...] = rest
    rows = blocks[0][:cap, :]
    for s in range(1, X):
        rows = rows + blocks[s][:cap, :]
    for z in range(Z):
        out[z, :cap, :] = rows
        out[z, cap + room :, :] = former[NB:, :]

    @pl.when(lax.axis_index("z") == 0)
    def _():
        def put(k):
            moves = []
            for i in range(BATCH):
                where = place[k * BATCH + i]
                rank = jnp.minimum(where & (NB - 1), cap - 1)
                moves.append((where >> BITS, cap + rank, former[pl.ds(filler[k * BATCH + i], 1), :]))
            for plane, at, values in moves:
                out[plane, pl.ds(at, 1), :] = values

        loop(NB // BATCH, put)

        def top(k):
            values = former[pl.ds(tops[k] & (NB - 1), 1), :]
            for z in range(Z):
                out[z, pl.ds(cap + jnp.minimum(count[z] + k, room - 1), 1), :] = values

        loop(count[Z], top)


def collect_kernel(cap, room, place, tops, count, got, pieces, out):
    z = lax.axis_index("z")

    def take(k):
        base = pl.multiple_of(k * BATCH, BATCH)
        rows = []
        for i in range(BATCH):
            where = place[base + i]
            rank = jnp.minimum(where & (NB - 1), cap - 1)
            rows.append(got[where >> BITS, pl.ds(rank, 1), :])
        for i in range(BATCH):
            out[0, pl.ds(base + i, 1), :] = rows[i]

    loop(NB // BATCH, take)

    def top(k):
        at = cap + jnp.minimum(count[z] + k, room - 1)
        out[0, pl.ds(tops[k] >> BITS, 1), :] = got[0, pl.ds(at, 1), :]

    loop(count[Z], top)
    out[0, NB : NB + cap, :] = got[0, cap : 2 * cap, :]
    for y in range(Y):
        out[0, NB + cap + 8 * y : NB + cap + 8 * y + 8, :] = pieces[y]
    for x in range(1, X):
        out[x] = out[0]


def dot(a, b):
    return jnp.dot(a, b, precision=HIGHEST, preferred_element_type=jnp.float32)


def invert(upper):
    half = NB // 2
    rows = lax.broadcasted_iota(jnp.int32, (half, half), 0)
    cols = lax.broadcasted_iota(jnp.int32, (half, half), 1)
    parts = []
    for k in range(2):
        values = upper[k * half : (k + 1) * half, k * half : (k + 1) * half]
        part = jnp.where((rows // DIAG == cols // DIAG) & (rows < cols), values, 0.0)
        part = part + jnp.where(rows == cols, 1.0, 0.0)
        parts.append((values, part))
    size = DIAG
    while size < half:
        mask = (rows // (2 * size) == cols // (2 * size)) & (rows // size < cols // size)
        parts = [(v, p - dot(dot(p, jnp.where(mask, v, 0.0)), p)) for v, p in parts]
        size *= 2
    (_, first), (_, second) = parts
    corner = -dot(dot(first, upper[:half, half:]), second)
    left = jnp.concatenate([first.T, corner.T], axis=0)
    right = jnp.concatenate([jnp.zeros((half, half), jnp.float32), second.T], axis=0)
    return jnp.concatenate([left, right], axis=1)


def turn_kernel(whole_t, out):
    for y in range(Y):
        out[:, DIAG * y : DIAG * (y + 1)] = whole_t[y].T


def finish_kernel(cap, pivots, slot_of, count, own, other, multipliers, trailing, out,
                  upper, inverse, block, current, in_sem, out_sem):
    copy = pltpu.make_async_copy(trailing, current, in_sem)
    copy.start()
    c = lax.axis_index("c")
    z = lax.axis_index("z")
    first = first_row()
    sides = ((pl.multiple_of(c * LANES, LANES), own), (pl.multiple_of((1 - c) * LANES, LANES), other))
    for x in range(X):
        for lane, ref in sides:
            for y in range(Y):
                at = DIAG * y + 8 * x
                upper[at : at + 8, pl.ds(lane, LANES)] = ref[x, NB + cap + 8 * y : NB + cap + 8 * y + 8, :]
    inverse[...] = invert(upper)
    copy.wait()

    def put(r):
        local = pivots[slot_of[z * NB + r]] - first

        @pl.when((local >= 0) & (local < ROWS))
        def _():
            at = tile_of(local)
            hit = picked(local, LANES)
            for x in range(X):
                for lane, ref in sides:
                    lanes = pl.ds(pl.multiple_of(x * C * LANES + lane, LANES), LANES)
                    current[at, lanes] = jnp.where(hit, ref[x, pl.ds(NB + r, 1), :], current[at, lanes])

    loop(jnp.minimum(count[z], cap), put)
    copies = []
    width = C * LANES
    for x in range(X):
        lanes = slice(x * width, (x + 1) * width)
        for lane, ref in sides:
            block[x, :, pl.ds(lane, LANES)] = ref[x, :NB, :]
        solved = dot(inverse[...], block[x])
        block[x] = solved
        current[:, lanes] = current[:, lanes] - dot(multipliers[...], solved)

        @pl.when(first == 0)
        def _():
            current[:NB, lanes] = block[x]

        copies.append(pltpu.make_async_copy(current.at[:, lanes], out.at[:, lanes], out_sem.at[x]))
        copies[-1].start()
    for copy in copies:
        copy.wait()


def call(kernel, shape, smem, vmem, scratch=(), name=None, last=VMEM, out=VMEM, busy=2):
    many = isinstance(shape, list)
    shapes = shape if many else [shape]
    got = pl.pallas_call(
        kernel,
        out_shape=[jax.ShapeDtypeStruct(s, jnp.float32) for s in shapes],
        in_specs=[SMEM] * len(smem) + [VMEM] * (len(vmem) - 1) + [last],
        out_specs=[out] * len(shapes),
        scratch_shapes=list(scratch),
        compiler_params=PARAMS,
        cost_estimate=pl.CostEstimate(flops=0, bytes_accessed=busy * 2**20, transcendentals=0),
        name=name,
    )(*smem, *vmem)
    return list(got) if many else got[0]


ANY = pl.BlockSpec(memory_space=pl.ANY)


def pack(cap, pivots, trailing, panel_t):
    scratch = [pltpu.VMEM((DIAG, NB), jnp.float32), pltpu.VMEM((ROWS, COLS), jnp.float32),
               pltpu.SMEM((NB + 8,), jnp.int32), pltpu.SemaphoreType.DMA]
    return call(functools.partial(pack_kernel, cap), [(X, cap + NB + 8, LANES)] * 2,
                (pivots,), (panel_t, trailing), scratch, name="pack", last=ANY)


def join(cap, keep, got):
    return call(functools.partial(join_kernel, cap), [keep.shape[1:]] * X, (), (keep, got), name="join")


def spread(cap, room, plan, blocks, whole_t):
    filler, place, _, tops, count = plan
    return call(functools.partial(spread_kernel, cap, room), (Z, cap + room + 8, LANES),
                (filler, place, tops, count), (*blocks, whole_t),
                [pltpu.VMEM((NB + 8, LANES), jnp.float32)], name="spread", last=ANY)


def collect(cap, room, plan, planes, pieces):
    _, place, _, tops, count = plan
    return call(functools.partial(collect_kernel, cap, room), (X, NB + cap + 8 * Y, LANES),
                (place, tops, count), (planes, pieces), name="collect")


def finish(cap, pivots, plan, own, other, multipliers, trailing):
    _, _, slot_of, _, count = plan
    scratch = [pltpu.VMEM(s, jnp.float32) for s in ((NB, NB), (NB, NB), (X, NB, C * LANES), (ROWS, COLS))]
    scratch += [pltpu.SemaphoreType.DMA, pltpu.SemaphoreType.DMA((X,))]
    return call(functools.partial(finish_kernel, cap), (ROWS, COLS), (pivots, slot_of, count),
                (own, other, multipliers, trailing), scratch, name="finish",
                last=ANY, out=pl.BlockSpec(memory_space=pltpu.HBM), busy=16)


swap = functools.partial(lax.all_to_all, split_axis=0, concat_axis=0, tiled=True)


def other_core(values):
    return lax.ppermute(values, "c", [(0, 1), (1, 0)])


def exchange(cap, room, panel_t, trailing, pivots, plan, whole_t):
    keep, send = pack(cap, pivots, trailing, panel_t)
    blocks = join(cap, keep, other_core(send))
    for s in range(1, X):
        blocks[s] = lax.ppermute(blocks[s], "x", [(x, (x + s) % X) for x in range(X)])
    planes = swap(spread(cap, room, plan, blocks, whole_t), "z")
    pieces = swap(jnp.broadcast_to(planes[:1, cap + room :], (Y, 8, LANES)), "y")
    own = swap(collect(cap, room, plan, planes, pieces), "x")
    return own, other_core(own)


def shards(panel, trailing, pivots):
    panel_t = panel.T
    whole_t = swap(jnp.broadcast_to(panel_t[None], (Y, DIAG, ROWS)), "y")
    multipliers = call(turn_kernel, (ROWS, NB), (), (whole_t,), name="turn")
    *plan, most = make_plan(pivots)

    def with_room(cap, room):
        ready = exchange(cap, room, panel_t, trailing, pivots, plan, whole_t)
        return finish(cap, pivots, plan, *ready, multipliers, trailing)

    def pending(carry):
        return carry[0]

    def again(carry):
        return jnp.zeros_like(carry[0]), with_room(NB, 2 * NB)

    return lax.while_loop(pending, again, (most[0] > NARROW, with_room(NARROW, NARROW)))[1]


def solution(mesh):
    fine = Mesh(mesh.devices.reshape(X, Z, C, Y), ("x", "z", "c", "y"))
    split = P(("x", "z", "c"), "y")
    return jax.shard_map(shards, mesh=fine, in_specs=(split, split, P()), out_specs=split, check_vma=False)
```

```python
import functools

import jax
import jax.numpy as jnp
from jax import lax
from jax.experimental import pallas as pl
from jax.experimental.pallas import tpu as pltpu
from jax.sharding import Mesh, PartitionSpec as P

NB = 256
ORDER = 32768
LANES = 128
X, Z, C, Y = 4, 8, 2, 8
BLOCKS = X * C
ROWS = ORDER // (X * Z * C)
COLS = BLOCKS * LANES
DIAG = NB // Y
BATCH = 16
BITS = NB.bit_length() - 1
PLANE_BITS = (ROWS * C).bit_length() - 1
NARROW = 56
HIGHEST = lax.Precision.HIGHEST
VMEM = pl.BlockSpec(memory_space=pltpu.VMEM)
SMEM = pl.BlockSpec(memory_space=pltpu.SMEM)
ANY = pl.BlockSpec(memory_space=pl.ANY)
PARAMS = pltpu.CompilerParams(vmem_limit_bytes=48 * 1024 * 1024)


def loop(count, body, unroll=1):
    def step(i, carry):
        body(i)
        return carry

    lax.fori_loop(0, count, step, 0, unroll=unroll)


def tile_of(row):
    return pl.ds(pl.multiple_of(row & -8, 8), 8)


def picked(row, width):
    return lax.broadcasted_iota(jnp.int32, (8, width), 0) == (row & 7)


def load_row(ref, row):
    tile = ref[tile_of(row), :]
    return jnp.sum(jnp.where(picked(row, tile.shape[1]), tile, 0.0), axis=0, keepdims=True)


def store_row(ref, row, values):
    at = tile_of(row)
    tile = ref[at, :]
    ref[at, :] = jnp.where(picked(row, tile.shape[1]), values, tile)


def plane_of(row):
    return (row >> PLANE_BITS) & (Z - 1)


def first_row():
    return ((lax.axis_index("x") * Z + lax.axis_index("z")) * C + lax.axis_index("c")) * ROWS


def plan_kernel(pivots, filler, place, slot_of, tops, count, most, content):
    def start(i):
        content[pivots[i]] = pivots[i]

    def start_top(i):
        content[i] = i

    loop(NB, start, 8)
    loop(NB, start_top, 8)

    def exchange(i, found):
        at = pivots[i]
        left, right = content[i], content[at]
        content[i] = right
        content[at] = left
        tops[found] = i * NB + right
        return found + (right != at).astype(jnp.int32)

    found = lax.fori_loop(0, NB, exchange, jnp.int32(0), unroll=4)
    for z in range(Z):
        count[z] = 0

    def rank(i):
        row = pivots[i]
        filler[i] = jnp.where(row < NB, 0, content[row])
        plane = plane_of(row)
        have = count[plane]
        place[i] = plane * NB + have
        slot_of[plane * NB + have] = i
        count[plane] = have + 1

    loop(NB, rank, 4)
    count[Z] = found
    peak = count[0]
    for z in range(1, Z):
        peak = jnp.maximum(peak, count[z])
    most[0] = peak + found


def early_plan_kernel(*refs):
    @pl.when(lax.axis_index("z") == 0)
    def _():
        plan_kernel(*refs)


def late_plan_kernel(pivots, after, *refs):
    plan_kernel(pivots, *refs)


def make_plan(pivots, after=None):
    sizes = (NB, NB, Z * NB, NB + 8, Z + 1, 1)
    early = after is None
    return pl.pallas_call(
        early_plan_kernel if early else late_plan_kernel,
        out_shape=[jax.ShapeDtypeStruct((n,), jnp.int32) for n in sizes],
        in_specs=[SMEM] if early else [SMEM, VMEM],
        out_specs=[SMEM] * len(sizes),
        scratch_shapes=[pltpu.SMEM((ORDER,), jnp.int32)],
        compiler_params=PARAMS,
        cost_estimate=pl.CostEstimate(flops=0, bytes_accessed=16 * 1024 * 1024, transcendentals=0),
        name="plan",
    )(*([pivots] if early else [pivots, after]))


def invert_diagonal(panel_t, at):
    y = lax.axis_index("y")
    lanes = pl.ds(pl.multiple_of((y * DIAG) & -LANES, LANES), LANES)
    shift = (y * DIAG) & (LANES - 1)
    window = pltpu.roll(panel_t[:, lanes], (LANES - shift) & (LANES - 1), axis=1)
    rows = lax.broadcasted_iota(jnp.int32, (DIAG, LANES), 0)
    cols = lax.broadcasted_iota(jnp.int32, (DIAG, LANES), 1)
    strict = (cols > rows) & (cols < DIAG)
    values = jnp.where(strict, window, 0.0)
    inverse = jnp.where(rows == cols, 1.0, 0.0)
    for k in range(DIAG - 1, 0, -1):
        inverse = inverse - values[:, k : k + 1] * inverse[k : k + 1, :]
    window = jnp.where(strict, inverse, window)
    at[:, :] = panel_t[:, :NB]
    at[:, lanes] = pltpu.roll(window, shift, axis=1)


def pack_kernel(cap, pivots, panel_t, trailing, keep, send, mine, triangle, rows, sem):
    copy = pltpu.make_async_copy(trailing, rows, sem)
    copy.start()
    z = lax.axis_index("z")
    c = lax.axis_index("c")
    first = first_row()

    def find(i, carry):
        rank, found = carry
        row = pivots[i]
        local = row - first
        mine[found] = local * NB + jnp.minimum(rank, cap - 1)
        hit = (local >= 0) & (local < ROWS)
        return rank + (plane_of(row) == z).astype(jnp.int32), found + hit.astype(jnp.int32)

    _, found = lax.fori_loop(0, NB, find, (jnp.int32(0), jnp.int32(0)), unroll=16)
    invert_diagonal(panel_t, triangle)
    sides = ((keep, c), (send, 1 - c))
    for out, side in sides:
        for x in range(X):
            out[x, :cap, :] = jnp.zeros((cap, LANES), jnp.float32)
            lanes = pl.ds(pl.multiple_of(side * LANES, LANES), LANES)
            out[x, cap + NB :, :] = triangle[8 * x : 8 * x + 8, lanes]
    copy.wait()
    for out, side in sides:
        for x in range(X):
            lanes = pl.ds(pl.multiple_of((x * C + side) * LANES, LANES), LANES)
            out[x, cap : cap + NB, :] = rows[:NB, lanes]

    def put(k):
        entry = mine[k]
        row = entry >> BITS
        at = pl.ds(entry & (NB - 1), 1)
        hit = picked(row, LANES)
        for out, side in sides:
            for x in range(X):
                lanes = pl.ds(pl.multiple_of((x * C + side) * LANES, LANES), LANES)
                tile = jnp.where(hit, rows[tile_of(row), lanes], 0.0)
                out[x, at, :] = jnp.sum(tile, axis=0, keepdims=True)

    loop(found, put)
    mine[NB] = found


def join_kernel(cap, keep, got, *blocks):
    x = lax.axis_index("x")
    c = lax.axis_index("c")
    for s, out in enumerate(blocks):
        at = (x + s) & (X - 1)
        out[:cap, :] = keep[at, :cap, :] + got[at, :cap, :]
        out[cap:, :] = jnp.where(c == 0, keep[at, cap:, :], got[at, cap:, :])


def spread_kernel(cap, room, filler, place, tops, count, *refs):
    blocks, out, former = refs[:X], refs[-2], refs[-1]
    x = lax.axis_index("x")
    rest = blocks[0][cap:, :]
    for s in range(1, X):
        rest = jnp.where(x == s, blocks[s][cap:, :], rest)
    former[...] = rest
    rows = blocks[0][:cap, :]
    for s in range(1, X):
        rows = rows + blocks[s][:cap, :]
    for z in range(Z):
        out[z, :cap, :] = rows
        out[z, cap + room :, :] = former[NB:, :]

    @pl.when(lax.axis_index("z") == 0)
    def _():
        def put(k):
            moves = []
            for i in range(BATCH):
                where = place[k * BATCH + i]
                rank = jnp.minimum(where & (NB - 1), cap - 1)
                moves.append((where >> BITS, cap + rank, former[pl.ds(filler[k * BATCH + i], 1), :]))
            for plane, at, values in moves:
                out[plane, pl.ds(at, 1), :] = values

        loop(NB // BATCH, put)

        def top(k):
            values = former[pl.ds(tops[k] & (NB - 1), 1), :]
            for z in range(Z):
                out[z, pl.ds(cap + jnp.minimum(count[z] + k, room - 1), 1), :] = values

        loop(count[Z], top)


def pieces_kernel(count, got, out):
    for y in range(Y):
        out[y] = got[0, got.shape[1] - 8 :, :]


def collect_kernel(cap, room, place, tops, count, got, pieces, out):
    z = lax.axis_index("z")

    def take(k):
        base = pl.multiple_of(k * BATCH, BATCH)
        rows = []
        for i in range(BATCH):
            where = place[base + i]
            rank = jnp.minimum(where & (NB - 1), cap - 1)
            rows.append(got[where >> BITS, pl.ds(rank, 1), :])
        for i in range(BATCH):
            out[0, pl.ds(base + i, 1), :] = rows[i]

    loop(NB // BATCH, take)

    def top(k):
        at = cap + jnp.minimum(count[z] + k, room - 1)
        out[0, pl.ds(tops[k] >> BITS, 1), :] = got[0, pl.ds(at, 1), :]

    loop(count[Z], top)
    out[0, NB : NB + cap, :] = got[0, cap : 2 * cap, :]
    for y in range(Y):
        out[0, NB + cap + 8 * y : NB + cap + 8 * y + 8, :] = pieces[y]
    for x in range(1, X):
        out[x] = out[0]


def dot(a, b):
    return jnp.dot(a, b, precision=HIGHEST, preferred_element_type=jnp.float32)


def invert(upper):
    half = NB // 2
    rows = lax.broadcasted_iota(jnp.int32, (half, half), 0)
    cols = lax.broadcasted_iota(jnp.int32, (half, half), 1)
    parts = []
    for k in range(2):
        values = upper[k * half : (k + 1) * half, k * half : (k + 1) * half]
        part = jnp.where((rows // DIAG == cols // DIAG) & (rows < cols), values, 0.0)
        part = part + jnp.where(rows == cols, 1.0, 0.0)
        parts.append((values, part))
    size = DIAG
    while size < half:
        mask = (rows // (2 * size) == cols // (2 * size)) & (rows // size < cols // size)
        parts = [(v, p - dot(dot(p, jnp.where(mask, v, 0.0)), p)) for v, p in parts]
        size *= 2
    (_, first), (_, second) = parts
    corner = -dot(dot(first, upper[:half, half:]), second)
    left = jnp.concatenate([first.T, corner.T], axis=0)
    right = jnp.concatenate([jnp.zeros((half, half), jnp.float32), second.T], axis=0)
    return jnp.concatenate([left, right], axis=1)


def repeat_kernel(values, out):
    for y in range(Y):
        out[y] = values[...]


def turn_kernel(whole_t, out):
    for y in range(Y):
        out[:, DIAG * y : DIAG * (y + 1)] = whole_t[y].T


def finish_kernel(cap, mine, own, other, multipliers, trailing, out,
                  upper, inverse, block, current, in_sem, out_sem):
    copy = pltpu.make_async_copy(trailing, current, in_sem)
    copy.start()
    c = lax.axis_index("c")
    first = first_row()
    sides = ((pl.multiple_of(c * LANES, LANES), own), (pl.multiple_of((1 - c) * LANES, LANES), other))
    for x in range(X):
        for lane, ref in sides:
            for y in range(Y):
                at = DIAG * y + 8 * x
                upper[at : at + 8, pl.ds(lane, LANES)] = ref[x, NB + cap + 8 * y : NB + cap + 8 * y + 8, :]
    inverse[...] = invert(upper)
    copy.wait()

    def put(k):
        entry = mine[k]
        row = entry >> BITS
        rank = pl.ds(NB + (entry & (NB - 1)), 1)
        at = tile_of(row)
        hit = picked(row, LANES)
        for x in range(X):
            for lane, ref in sides:
                lanes = pl.ds(pl.multiple_of(x * C * LANES + lane, LANES), LANES)
                current[at, lanes] = jnp.where(hit, ref[x, rank, :], current[at, lanes])

    loop(mine[NB], put)
    copies = []
    width = C * LANES
    for x in range(X):
        lanes = slice(x * width, (x + 1) * width)
        for lane, ref in sides:
            block[x, :, pl.ds(lane, LANES)] = ref[x, :NB, :]
        solved = dot(inverse[...], block[x])
        block[x] = solved
        current[:, lanes] = current[:, lanes] - dot(multipliers[...], solved)

        @pl.when(first == 0)
        def _():
            current[:NB, lanes] = block[x]

        copies.append(pltpu.make_async_copy(current.at[:, lanes], out.at[:, lanes], out_sem.at[x]))
        copies[-1].start()
    for copy in copies:
        copy.wait()


def call(kernel, shape, smem, vmem, scratch=(), name=None, last=VMEM, out=VMEM, busy=2, table=None):
    many = isinstance(shape, list)
    shapes = [jax.ShapeDtypeStruct(s, jnp.float32) for s in (shape if many else [shape])]
    specs = [out] * len(shapes)
    if table is not None:
        shapes.append(jax.ShapeDtypeStruct((table,), jnp.int32))
        specs.append(SMEM)
    got = pl.pallas_call(
        kernel,
        out_shape=shapes,
        in_specs=[SMEM] * len(smem) + [VMEM] * (len(vmem) - 1) + [last],
        out_specs=specs,
        scratch_shapes=list(scratch),
        compiler_params=PARAMS,
        cost_estimate=pl.CostEstimate(flops=0, bytes_accessed=busy * 2**20, transcendentals=0),
        name=name,
    )(*smem, *vmem)
    return list(got) if many else got[0]


def pack(cap, pivots, trailing, panel_t):
    scratch = [pltpu.VMEM((DIAG, NB), jnp.float32), pltpu.VMEM((ROWS, COLS), jnp.float32), pltpu.SemaphoreType.DMA]
    return call(functools.partial(pack_kernel, cap), [(X, cap + NB + 8, LANES)] * 2,
                (pivots,), (panel_t, trailing), scratch, name="pack", last=ANY, table=NB + 8)


def join(cap, keep, got):
    return call(functools.partial(join_kernel, cap), [keep.shape[1:]] * X, (), (keep, got), name="join")


def spread(cap, room, plan, blocks, whole_t):
    filler, place, _, tops, count = plan
    return call(functools.partial(spread_kernel, cap, room), (Z, cap + room + 8, LANES),
                (filler, place, tops, count), (*blocks, whole_t),
                [pltpu.VMEM((NB + 8, LANES), jnp.float32)], name="spread")


def collect(cap, room, plan, planes, pieces):
    _, place, _, tops, count = plan
    return call(functools.partial(collect_kernel, cap, room), (X, NB + cap + 8 * Y, LANES),
                (place, tops, count), (planes, pieces), name="collect")


def finish(cap, mine, own, other, multipliers, trailing):
    scratch = [pltpu.VMEM(s, jnp.float32) for s in ((NB, NB), (NB, NB), (X, NB, C * LANES), (ROWS, COLS))]
    scratch += [pltpu.SemaphoreType.DMA, pltpu.SemaphoreType.DMA((X,))]
    return call(functools.partial(finish_kernel, cap), (ROWS, COLS), (mine,),
                (own, other, multipliers, trailing), scratch, name="finish",
                last=ANY, out=pl.BlockSpec(memory_space=pltpu.HBM), busy=16)


swap = functools.partial(lax.all_to_all, split_axis=0, concat_axis=0, tiled=True)


def other_core(values):
    return lax.ppermute(values, "c", [(0, 1), (1, 0)])


def first_phase(cap, room, panel_t, trailing, pivots, whole_t):
    keep, send, mine = pack(cap, pivots, trailing, panel_t)
    blocks = join(cap, keep, other_core(send))
    for s in range(1, X):
        blocks[s] = lax.ppermute(blocks[s], "x", [(x, (x + s) % X) for x in range(X)])
    plan = make_plan(pivots)
    return spread(cap, room, plan[:-1], blocks, whole_t), mine


def later_phases(cap, room, planes, plan):
    planes = swap(planes, "z")
    pieces = swap(call(pieces_kernel, (Y, 8, LANES), (plan[-1],), (planes,), name="pieces"), "y")
    own = swap(collect(cap, room, plan, planes, pieces), "x")
    return own, other_core(own)


def shards(panel, trailing, pivots):
    panel_t = panel.T
    whole_t = swap(call(repeat_kernel, (Y, DIAG, ROWS), (), (panel_t,), name="repeat"), "y")
    multipliers = call(turn_kernel, (ROWS, NB), (), (whole_t,), name="turn")
    planes, mine = first_phase(NARROW, NARROW, panel_t, trailing, pivots, whole_t)
    *plan, most = make_plan(pivots, planes)
    ready = later_phases(NARROW, NARROW, planes, plan)
    result = finish(NARROW, mine, *ready, multipliers, trailing)

    def pending(carry):
        return carry[0]

    def again(carry):
        planes, mine = first_phase(NB, 2 * NB, panel_t, trailing, pivots, whole_t)
        ready = later_phases(NB, 2 * NB, planes, plan)
        return jnp.zeros_like(carry[0]), finish(NB, mine, *ready, multipliers, trailing)

    return lax.while_loop(pending, again, (most[0] > NARROW, result))[1]


def solution(mesh):
    fine = Mesh(mesh.devices.reshape(X, Z, C, Y), ("x", "z", "c", "y"))
    split = P(("x", "z", "c"), "y")
    return jax.shard_map(shards, mesh=fine, in_specs=(split, split, P()), out_specs=split, check_vma=False)
```

```python
import functools

import jax
import jax.numpy as jnp
from jax import lax
from jax.experimental import pallas as pl
from jax.experimental.pallas import tpu as pltpu
from jax.sharding import Mesh, PartitionSpec as P

NB = 256
ORDER = 32768
LANES = 128
X, Z, C, Y = 4, 8, 2, 8
BLOCKS = X * C
ROWS = ORDER // (X * Z * C)
COLS = BLOCKS * LANES
DIAG = NB // Y
BATCH = 16
DISTANCES = (4, 2, 1)
BITS = NB.bit_length() - 1
PLANE_BITS = (ROWS * C).bit_length() - 1
NARROW = 56
HIGHEST = lax.Precision.HIGHEST
VMEM = pl.BlockSpec(memory_space=pltpu.VMEM)
SMEM = pl.BlockSpec(memory_space=pltpu.SMEM)
ANY = pl.BlockSpec(memory_space=pl.ANY)
PARAMS = pltpu.CompilerParams(vmem_limit_bytes=48 * 1024 * 1024)


def loop(count, body, unroll=1):
    def step(i, carry):
        body(i)
        return carry

    lax.fori_loop(0, count, step, 0, unroll=unroll)


def tile_of(row):
    return pl.ds(pl.multiple_of(row & -8, 8), 8)


def picked(row, width):
    return lax.broadcasted_iota(jnp.int32, (8, width), 0) == (row & 7)


def load_row(ref, row):
    tile = ref[tile_of(row), :]
    return jnp.sum(jnp.where(picked(row, tile.shape[1]), tile, 0.0), axis=0, keepdims=True)


def store_row(ref, row, values):
    at = tile_of(row)
    tile = ref[at, :]
    ref[at, :] = jnp.where(picked(row, tile.shape[1]), values, tile)


def plane_of(row):
    return (row >> PLANE_BITS) & (Z - 1)


def first_row():
    return ((lax.axis_index("x") * Z + lax.axis_index("z")) * C + lax.axis_index("c")) * ROWS


def plan_kernel(pivots, filler, place, slot_of, tops, count, most, content):
    def start(i):
        content[pivots[i]] = pivots[i]

    def start_top(i):
        content[i] = i

    loop(NB, start, 8)
    loop(NB, start_top, 8)

    def exchange(i, found):
        at = pivots[i]
        left, right = content[i], content[at]
        content[i] = right
        content[at] = left
        tops[found] = i * NB + right
        return found + (right != at).astype(jnp.int32)

    found = lax.fori_loop(0, NB, exchange, jnp.int32(0), unroll=4)
    for z in range(Z):
        count[z] = 0

    def rank(i):
        row = pivots[i]
        filler[i] = jnp.where(row < NB, 0, content[row])
        plane = plane_of(row)
        have = count[plane]
        place[i] = plane * NB + have
        slot_of[plane * NB + have] = i
        count[plane] = have + 1

    loop(NB, rank, 4)
    count[Z] = found
    peak = count[0]
    for z in range(1, Z):
        peak = jnp.maximum(peak, count[z])
    most[0] = peak + found


def early_plan_kernel(*refs):
    @pl.when(lax.axis_index("z") == 0)
    def _():
        plan_kernel(*refs)


def late_plan_kernel(pivots, after, *refs):
    plan_kernel(pivots, *refs)


def make_plan(pivots, after=None):
    sizes = (NB, NB, Z * NB, NB + 8, Z + 1, 1)
    early = after is None
    return pl.pallas_call(
        early_plan_kernel if early else late_plan_kernel,
        out_shape=[jax.ShapeDtypeStruct((n,), jnp.int32) for n in sizes],
        in_specs=[SMEM] if early else [SMEM, VMEM],
        out_specs=[SMEM] * len(sizes),
        scratch_shapes=[pltpu.SMEM((ORDER,), jnp.int32)],
        compiler_params=PARAMS,
        cost_estimate=pl.CostEstimate(flops=0, bytes_accessed=16 * 1024 * 1024, transcendentals=0),
        name="plan",
    )(*([pivots] if early else [pivots, after]))


def invert_diagonal(panel_t, at):
    y = lax.axis_index("y")
    lanes = pl.ds(pl.multiple_of((y * DIAG) & -LANES, LANES), LANES)
    shift = (y * DIAG) & (LANES - 1)
    window = pltpu.roll(panel_t[:, lanes], (LANES - shift) & (LANES - 1), axis=1)
    rows = lax.broadcasted_iota(jnp.int32, (DIAG, LANES), 0)
    cols = lax.broadcasted_iota(jnp.int32, (DIAG, LANES), 1)
    strict = (cols > rows) & (cols < DIAG)
    values = jnp.where(strict, window, 0.0)
    inverse = jnp.where(rows == cols, 1.0, 0.0)
    for k in range(DIAG - 1, 0, -1):
        inverse = inverse - values[:, k : k + 1] * inverse[k : k + 1, :]
    window = jnp.where(strict, inverse, window)
    at[:, :] = panel_t[:, :NB]
    at[:, lanes] = pltpu.roll(window, shift, axis=1)


def pack_kernel(cap, pivots, panel_t, trailing, keep, send, mine, triangle, rows, sem):
    copy = pltpu.make_async_copy(trailing, rows, sem)
    copy.start()
    z = lax.axis_index("z")
    c = lax.axis_index("c")
    first = first_row()

    def find(i, carry):
        rank, found = carry
        row = pivots[i]
        local = row - first
        mine[found] = local * NB + jnp.minimum(rank, cap - 1)
        hit = (local >= 0) & (local < ROWS)
        return rank + (plane_of(row) == z).astype(jnp.int32), found + hit.astype(jnp.int32)

    _, found = lax.fori_loop(0, NB, find, (jnp.int32(0), jnp.int32(0)), unroll=16)
    invert_diagonal(panel_t, triangle)
    sides = ((keep, c), (send, 1 - c))
    for out, side in sides:
        for x in range(X):
            out[x, :cap, :] = jnp.zeros((cap, LANES), jnp.float32)
            lanes = pl.ds(pl.multiple_of(side * LANES, LANES), LANES)
            out[x, cap + NB :, :] = triangle[8 * x : 8 * x + 8, lanes]
    copy.wait()
    for out, side in sides:
        for x in range(X):
            lanes = pl.ds(pl.multiple_of((x * C + side) * LANES, LANES), LANES)
            out[x, cap : cap + NB, :] = rows[:NB, lanes]

    def put(k):
        entry = mine[k]
        row = entry >> BITS
        at = pl.ds(entry & (NB - 1), 1)
        hit = picked(row, LANES)
        for out, side in sides:
            for x in range(X):
                lanes = pl.ds(pl.multiple_of((x * C + side) * LANES, LANES), LANES)
                tile = jnp.where(hit, rows[tile_of(row), lanes], 0.0)
                out[x, at, :] = jnp.sum(tile, axis=0, keepdims=True)

    loop(found, put)
    mine[NB] = found


def join_kernel(cap, keep, got, *blocks):
    x = lax.axis_index("x")
    c = lax.axis_index("c")
    for s, out in enumerate(blocks):
        at = (x + s) & (X - 1)
        out[:cap, :] = keep[at, :cap, :] + got[at, :cap, :]
        out[cap:, :] = jnp.where(c == 0, keep[at, cap:, :], got[at, cap:, :])


def spread_kernel(cap, room, filler, place, tops, count, *refs):
    blocks, out, former = refs[:X], refs[-2], refs[-1]
    x = lax.axis_index("x")
    rest = blocks[0][cap:, :]
    for s in range(1, X):
        rest = jnp.where(x == s, blocks[s][cap:, :], rest)
    former[...] = rest
    rows = blocks[0][:cap, :]
    for s in range(1, X):
        rows = rows + blocks[s][:cap, :]
    for z in range(Z):
        out[z, :cap, :] = rows
        out[z, cap + room :, :] = former[NB:, :]

    @pl.when(lax.axis_index("z") == 0)
    def _():
        def put(k):
            moves = []
            for i in range(BATCH):
                where = place[k * BATCH + i]
                rank = jnp.minimum(where & (NB - 1), cap - 1)
                moves.append((where >> BITS, cap + rank, former[pl.ds(filler[k * BATCH + i], 1), :]))
            for plane, at, values in moves:
                out[plane, pl.ds(at, 1), :] = values

        loop(NB // BATCH, put)

        def top(k):
            values = former[pl.ds(tops[k] & (NB - 1), 1), :]
            for z in range(Z):
                out[z, pl.ds(cap + jnp.minimum(count[z] + k, room - 1), 1), :] = values

        loop(count[Z], top)


def pieces_kernel(count, slices, got, out):
    for y in range(Y):
        out[y] = got[0, got.shape[1] - 8 :, :]


def collect_kernel(cap, room, place, tops, count, slices, got, pieces, out):
    z = lax.axis_index("z")

    def take(k):
        base = pl.multiple_of(k * BATCH, BATCH)
        rows = []
        for i in range(BATCH):
            where = place[base + i]
            rank = jnp.minimum(where & (NB - 1), cap - 1)
            rows.append(got[where >> BITS, pl.ds(rank, 1), :])
        for i in range(BATCH):
            out[0, pl.ds(base + i, 1), :] = rows[i]

    loop(NB // BATCH, take)

    def top(k):
        at = cap + jnp.minimum(count[z] + k, room - 1)
        out[0, pl.ds(tops[k] >> BITS, 1), :] = got[0, pl.ds(at, 1), :]

    loop(count[Z], top)
    out[0, NB : NB + cap, :] = got[0, cap : 2 * cap, :]
    for y in range(Y):
        out[0, NB + cap + 8 * y : NB + cap + 8 * y + 8, :] = pieces[y]
    for x in range(1, X):
        out[x] = out[0]


def dot(a, b):
    return jnp.dot(a, b, precision=HIGHEST, preferred_element_type=jnp.float32)


def invert(upper):
    half = NB // 2
    rows = lax.broadcasted_iota(jnp.int32, (half, half), 0)
    cols = lax.broadcasted_iota(jnp.int32, (half, half), 1)
    parts = []
    for k in range(2):
        values = upper[k * half : (k + 1) * half, k * half : (k + 1) * half]
        part = jnp.where((rows // DIAG == cols // DIAG) & (rows < cols), values, 0.0)
        part = part + jnp.where(rows == cols, 1.0, 0.0)
        parts.append((values, part))
    size = DIAG
    while size < half:
        mask = (rows // (2 * size) == cols // (2 * size)) & (rows // size < cols // size)
        parts = [(v, p - dot(dot(p, jnp.where(mask, v, 0.0)), p)) for v, p in parts]
        size *= 2
    (_, first), (_, second) = parts
    corner = -dot(dot(first, upper[:half, half:]), second)
    left = jnp.concatenate([first.T, corner.T], axis=0)
    right = jnp.concatenate([jnp.zeros((half, half), jnp.float32), second.T], axis=0)
    return jnp.concatenate([left, right], axis=1)


def later_kernel(values, after, out):
    out[...] = values[...]


def double_kernel(first, second, out):
    half = first.shape[0]
    out[:half] = first[...]
    out[half:] = second[...]


def turn_kernel(slices, out, ordered):
    y = lax.axis_index("y")
    columns = [y]
    for distance in DISTANCES:
        columns += [column ^ distance for column in columns]
    for k, column in enumerate(columns):
        at = pl.ds(pl.multiple_of(column * DIAG, DIAG), DIAG)
        ordered[at, :] = slices[k * DIAG : (k + 1) * DIAG, :]
    out[...] = ordered[...].T


def finish_kernel(cap, mine, own, other, multipliers, trailing, out,
                  upper, inverse, block, current, in_sem, out_sem):
    copy = pltpu.make_async_copy(trailing, current, in_sem)
    copy.start()
    c = lax.axis_index("c")
    first = first_row()
    sides = ((pl.multiple_of(c * LANES, LANES), own), (pl.multiple_of((1 - c) * LANES, LANES), other))
    for x in range(X):
        for lane, ref in sides:
            for y in range(Y):
                at = DIAG * y + 8 * x
                upper[at : at + 8, pl.ds(lane, LANES)] = ref[x, NB + cap + 8 * y : NB + cap + 8 * y + 8, :]
    inverse[...] = invert(upper)
    copy.wait()

    def put(k):
        entry = mine[k]
        row = entry >> BITS
        rank = pl.ds(NB + (entry & (NB - 1)), 1)
        at = tile_of(row)
        hit = picked(row, LANES)
        for x in range(X):
            for lane, ref in sides:
                lanes = pl.ds(pl.multiple_of(x * C * LANES + lane, LANES), LANES)
                current[at, lanes] = jnp.where(hit, ref[x, rank, :], current[at, lanes])

    loop(mine[NB], put)
    copies = []
    width = C * LANES
    for x in range(X):
        lanes = slice(x * width, (x + 1) * width)
        for lane, ref in sides:
            block[x, :, pl.ds(lane, LANES)] = ref[x, :NB, :]
        solved = dot(inverse[...], block[x])
        block[x] = solved
        current[:, lanes] = current[:, lanes] - dot(multipliers[...], solved)

        @pl.when(first == 0)
        def _():
            current[:NB, lanes] = block[x]

        copies.append(pltpu.make_async_copy(current.at[:, lanes], out.at[:, lanes], out_sem.at[x]))
        copies[-1].start()
    for copy in copies:
        copy.wait()


def call(kernel, shape, smem, vmem, scratch=(), name=None, last=VMEM, out=VMEM, busy=2, table=None):
    many = isinstance(shape, list)
    shapes = [jax.ShapeDtypeStruct(s, jnp.float32) for s in (shape if many else [shape])]
    specs = [out] * len(shapes)
    if table is not None:
        shapes.append(jax.ShapeDtypeStruct((table,), jnp.int32))
        specs.append(SMEM)
    got = pl.pallas_call(
        kernel,
        out_shape=shapes,
        in_specs=[SMEM] * len(smem) + [VMEM] * (len(vmem) - 1) + [last],
        out_specs=specs,
        scratch_shapes=list(scratch),
        compiler_params=PARAMS,
        cost_estimate=pl.CostEstimate(flops=0, bytes_accessed=busy * 2**20, transcendentals=0),
        name=name,
    )(*smem, *vmem)
    return list(got) if many else got[0]


def pack(cap, pivots, trailing, panel_t):
    scratch = [pltpu.VMEM((DIAG, NB), jnp.float32), pltpu.VMEM((ROWS, COLS), jnp.float32), pltpu.SemaphoreType.DMA]
    return call(functools.partial(pack_kernel, cap), [(X, cap + NB + 8, LANES)] * 2,
                (pivots,), (panel_t, trailing), scratch, name="pack", last=ANY, table=NB + 8)


def join(cap, keep, got):
    return call(functools.partial(join_kernel, cap), [keep.shape[1:]] * X, (), (keep, got), name="join")


def spread(cap, room, plan, blocks):
    filler, place, _, tops, count = plan
    return call(functools.partial(spread_kernel, cap, room), (Z, cap + room + 8, LANES),
                (filler, place, tops, count), blocks,
                [pltpu.VMEM((NB + 8, LANES), jnp.float32)], name="spread")


def collect(cap, room, plan, planes, pieces, slices):
    _, place, _, tops, count = plan
    return call(functools.partial(collect_kernel, cap, room), (X, NB + cap + 8 * Y, LANES),
                (place, tops, count), (slices, planes, pieces), name="collect")


def finish(cap, mine, own, other, multipliers, trailing):
    scratch = [pltpu.VMEM(s, jnp.float32) for s in ((NB, NB), (NB, NB), (X, NB, C * LANES), (ROWS, COLS))]
    scratch += [pltpu.SemaphoreType.DMA, pltpu.SemaphoreType.DMA((X,))]
    return call(functools.partial(finish_kernel, cap), (ROWS, COLS), (mine,),
                (own, other, multipliers, trailing), scratch, name="finish",
                last=ANY, out=pl.BlockSpec(memory_space=pltpu.HBM), busy=16)


swap = functools.partial(lax.all_to_all, split_axis=0, concat_axis=0, tiled=True)


def other_core(values):
    return lax.ppermute(values, "c", [(0, 1), (1, 0)])


def first_phase(cap, room, panel_t, trailing, pivots):
    keep, send, mine = pack(cap, pivots, trailing, panel_t)
    blocks = join(cap, keep, other_core(send))
    for s in range(1, X):
        blocks[s] = lax.ppermute(blocks[s], "x", [(x, (x + s) % X) for x in range(X)])
    plan = make_plan(pivots)
    return spread(cap, room, plan[:-1], blocks), mine


def from_column(values, distance):
    return lax.ppermute(values, "y", [(y, y ^ distance) for y in range(Y)])


def doubled(slices, distance):
    shape = (2 * slices.shape[0], ROWS)
    return call(double_kernel, shape, (), (slices, from_column(slices, distance)), name="double")


def later_phases(cap, room, planes, plan, panel_t):
    slices = call(later_kernel, panel_t.shape, (), (panel_t, planes), name="later")
    slices = doubled(slices, DISTANCES[0])
    planes = swap(planes, "z")
    pieces = call(pieces_kernel, (Y, 8, LANES), (plan[-1],), (slices, planes), name="pieces")
    slices = doubled(slices, DISTANCES[1])
    blocks = collect(cap, room, plan, planes, swap(pieces, "y"), slices)
    slices = doubled(slices, DISTANCES[2])
    multipliers = call(turn_kernel, (ROWS, NB), (), (slices,), [pltpu.VMEM((NB, ROWS), jnp.float32)], name="turn")
    own, multipliers = lax.optimization_barrier((swap(blocks, "x"), multipliers))
    return own, other_core(own), multipliers


def shards(panel, trailing, pivots):
    panel_t = panel.T
    planes, mine = first_phase(NARROW, NARROW, panel_t, trailing, pivots)
    *plan, most = make_plan(pivots, planes)
    ready = later_phases(NARROW, NARROW, planes, plan, panel_t)
    result = finish(NARROW, mine, *ready, trailing)

    def pending(carry):
        return carry[0]

    def again(carry):
        planes, mine = first_phase(NB, 2 * NB, panel_t, trailing, pivots)
        ready = later_phases(NB, 2 * NB, planes, plan, panel_t)
        return jnp.zeros_like(carry[0]), finish(NB, mine, *ready, trailing)

    return lax.while_loop(pending, again, (most[0] > NARROW, result))[1]


def solution(mesh):
    fine = Mesh(mesh.devices.reshape(X, Z, C, Y), ("x", "z", "c", "y"))
    split = P(("x", "z", "c"), "y")
    return jax.shard_map(shards, mesh=fine, in_specs=(split, split, P()), out_specs=split, check_vma=False)
```

```python
import functools

import jax
import jax.numpy as jnp
from jax import lax
from jax.experimental import pallas as pl
from jax.experimental.pallas import tpu as pltpu
from jax.sharding import Mesh, PartitionSpec as P

NB = 256
ORDER = 32768
LANES = 128
X, Z, C, Y = 4, 8, 2, 8
BLOCKS = X * C
ROWS = ORDER // (X * Z * C)
COLS = BLOCKS * LANES
DIAG = NB // Y
BATCH = 16
DISTANCES = (4, 2, 1)
FILLER, PLACE, TOPS = 0, NB, 2 * NB
COUNT = TOPS + NB + 8
MOST = COUNT + Z + 1
TABLE = 1024
BITS = NB.bit_length() - 1
PLANE_BITS = (ROWS * C).bit_length() - 1
NARROW = 56
HIGHEST = lax.Precision.HIGHEST
VMEM = pl.BlockSpec(memory_space=pltpu.VMEM)
SMEM = pl.BlockSpec(memory_space=pltpu.SMEM)
ANY = pl.BlockSpec(memory_space=pl.ANY)
PARAMS = pltpu.CompilerParams(vmem_limit_bytes=48 * 1024 * 1024)


def loop(count, body, unroll=1):
    def step(i, carry):
        body(i)
        return carry

    lax.fori_loop(0, count, step, 0, unroll=unroll)


def tile_of(row):
    return pl.ds(pl.multiple_of(row & -8, 8), 8)


def picked(row, width):
    return lax.broadcasted_iota(jnp.int32, (8, width), 0) == (row & 7)


def load_row(ref, row):
    tile = ref[tile_of(row), :]
    return jnp.sum(jnp.where(picked(row, tile.shape[1]), tile, 0.0), axis=0, keepdims=True)


def store_row(ref, row, values):
    at = tile_of(row)
    tile = ref[at, :]
    ref[at, :] = jnp.where(picked(row, tile.shape[1]), values, tile)


def plane_of(row):
    return (row >> PLANE_BITS) & (Z - 1)


def first_row():
    return ((lax.axis_index("x") * Z + lax.axis_index("z")) * C + lax.axis_index("c")) * ROWS


def plan_kernel(pivots, table, content):
    def start(i):
        content[i] = i
        content[pivots[i]] = pivots[i]

    loop(NB, start, 8)
    for z in range(Z):
        table[COUNT + z] = 0

    def exchange(i, found):
        at = pivots[i]
        left, right = content[i], content[at]
        content[i] = right
        content[at] = left
        table[TOPS + found] = i * NB + right
        plane = plane_of(at)
        have = table[COUNT + plane]
        table[PLACE + i] = plane * NB + have
        table[COUNT + plane] = have + 1
        return found + (right != at).astype(jnp.int32)

    found = lax.fori_loop(0, NB, exchange, jnp.int32(0), unroll=4)

    def fill(i):
        row = pivots[i]
        table[FILLER + i] = jnp.where(row < NB, 0, content[row])

    loop(NB, fill, 8)
    table[COUNT + Z] = found
    peak = table[COUNT]
    for z in range(1, Z):
        peak = jnp.maximum(peak, table[COUNT + z])
    table[MOST] = peak + found


def early_plan_kernel(*refs):
    @pl.when(lax.axis_index("z") == 0)
    def _():
        plan_kernel(*refs)


def late_plan_kernel(pivots, after, table, content):
    plan_kernel(pivots, table, content)


def make_plan(pivots, after=None):
    early = after is None
    return pl.pallas_call(
        early_plan_kernel if early else late_plan_kernel,
        out_shape=jax.ShapeDtypeStruct((TABLE,), jnp.int32),
        in_specs=[SMEM] if early else [SMEM, VMEM],
        out_specs=SMEM,
        scratch_shapes=[pltpu.SMEM((ORDER,), jnp.int32)],
        compiler_params=PARAMS,
        cost_estimate=pl.CostEstimate(flops=0, bytes_accessed=16 * 1024 * 1024, transcendentals=0),
        name="plan",
    )(*([pivots] if early else [pivots, after]))


def invert_diagonal(panel_t, at):
    y = lax.axis_index("y")
    lanes = pl.ds(pl.multiple_of((y * DIAG) & -LANES, LANES), LANES)
    shift = (y * DIAG) & (LANES - 1)
    window = pltpu.roll(panel_t[:, lanes], (LANES - shift) & (LANES - 1), axis=1)
    rows = lax.broadcasted_iota(jnp.int32, (DIAG, LANES), 0)
    cols = lax.broadcasted_iota(jnp.int32, (DIAG, LANES), 1)
    strict = (cols > rows) & (cols < DIAG)
    values = jnp.where(strict, window, 0.0)
    inverse = jnp.where(rows == cols, 1.0, 0.0)
    for k in range(DIAG - 1, 0, -1):
        inverse = inverse - values[:, k : k + 1] * inverse[k : k + 1, :]
    window = jnp.where(strict, inverse, window)
    at[:, :] = panel_t[:, :NB]
    at[:, lanes] = pltpu.roll(window, shift, axis=1)


def pack_kernel(cap, pivots, panel_t, trailing, keep, send, mine, triangle, rows, sem):
    copy = pltpu.make_async_copy(trailing, rows, sem)
    copy.start()
    z = lax.axis_index("z")
    c = lax.axis_index("c")
    first = first_row()

    def find(i, carry):
        rank, found = carry
        row = pivots[i]
        local = row - first
        mine[found] = local * NB + jnp.minimum(rank, cap - 1)
        hit = (local >= 0) & (local < ROWS)
        return rank + (plane_of(row) == z).astype(jnp.int32), found + hit.astype(jnp.int32)

    _, found = lax.fori_loop(0, NB, find, (jnp.int32(0), jnp.int32(0)), unroll=16)
    invert_diagonal(panel_t, triangle)
    sides = ((keep, c), (send, 1 - c))
    for out, side in sides:
        for x in range(X):
            out[x, :cap, :] = jnp.zeros((cap, LANES), jnp.float32)
            lanes = pl.ds(pl.multiple_of(side * LANES, LANES), LANES)
            out[x, cap + NB :, :] = triangle[8 * x : 8 * x + 8, lanes]
    copy.wait()
    for out, side in sides:
        for x in range(X):
            lanes = pl.ds(pl.multiple_of((x * C + side) * LANES, LANES), LANES)
            out[x, cap : cap + NB, :] = rows[:NB, lanes]

    def put(k):
        entry = mine[k]
        row = entry >> BITS
        at = pl.ds(entry & (NB - 1), 1)
        hit = picked(row, LANES)
        for out, side in sides:
            for x in range(X):
                lanes = pl.ds(pl.multiple_of((x * C + side) * LANES, LANES), LANES)
                tile = jnp.where(hit, rows[tile_of(row), lanes], 0.0)
                out[x, at, :] = jnp.sum(tile, axis=0, keepdims=True)

    loop(found, put)
    mine[NB] = found


def join_kernel(cap, keep, got, *blocks):
    x = lax.axis_index("x")
    c = lax.axis_index("c")
    for s, out in enumerate(blocks):
        at = (x + s) & (X - 1)
        out[:cap, :] = keep[at, :cap, :] + got[at, :cap, :]
        out[cap:, :] = jnp.where(c == 0, keep[at, cap:, :], got[at, cap:, :])


def spread_kernel(cap, room, table, *refs):
    blocks, panel_t, out, panel_out, former = refs[:X], *refs[X:]
    x = lax.axis_index("x")
    rest = blocks[0][cap:, :]
    for s in range(1, X):
        rest = jnp.where(x == s, blocks[s][cap:, :], rest)
    former[...] = rest
    rows = blocks[0][:cap, :]
    for s in range(1, X):
        rows = rows + blocks[s][:cap, :]
    for z in range(Z):
        out[z, :cap, :] = rows
        out[z, cap + room :, :] = former[NB:, :]
    panel_out[...] = panel_t[...]

    @pl.when(lax.axis_index("z") == 0)
    def _():
        def put(k):
            moves = []
            for i in range(BATCH):
                where = table[PLACE + k * BATCH + i]
                rank = jnp.minimum(where & (NB - 1), cap - 1)
                filler = table[FILLER + k * BATCH + i]
                moves.append((where >> BITS, cap + rank, former[pl.ds(filler, 1), :]))
            for plane, at, values in moves:
                out[plane, pl.ds(at, 1), :] = values

        loop(NB // BATCH, put)

        def top(k):
            values = former[pl.ds(table[TOPS + k] & (NB - 1), 1), :]
            for z in range(Z):
                at = cap + jnp.minimum(table[COUNT + z] + k, room - 1)
                out[z, pl.ds(at, 1), :] = values

        loop(table[COUNT + Z], top)


def pieces_kernel(token, got, out):
    for y in range(Y):
        out[y] = got[0, got.shape[1] - 8 :, :]


def collect_kernel(cap, room, table, token, got, pieces, out):
    z = lax.axis_index("z")

    def take(k):
        base = pl.multiple_of(k * BATCH, BATCH)
        rows = []
        for i in range(BATCH):
            where = table[PLACE + base + i]
            rank = jnp.minimum(where & (NB - 1), cap - 1)
            rows.append(got[where >> BITS, pl.ds(rank, 1), :])
        for i in range(BATCH):
            out[0, pl.ds(base + i, 1), :] = rows[i]

    loop(NB // BATCH, take)

    def top(k):
        at = cap + jnp.minimum(table[COUNT + z] + k, room - 1)
        out[0, pl.ds(table[TOPS + k] >> BITS, 1), :] = got[0, pl.ds(at, 1), :]

    loop(table[COUNT + Z], top)
    out[0, NB : NB + cap, :] = got[0, cap : 2 * cap, :]
    for y in range(Y):
        out[0, NB + cap + 8 * y : NB + cap + 8 * y + 8, :] = pieces[y]
    for x in range(1, X):
        out[x] = out[0]


def dot(a, b):
    return jnp.dot(a, b, precision=HIGHEST, preferred_element_type=jnp.float32)


def invert(upper):
    half = NB // 2
    rows = lax.broadcasted_iota(jnp.int32, (half, half), 0)
    cols = lax.broadcasted_iota(jnp.int32, (half, half), 1)
    parts = []
    for k in range(2):
        values = upper[k * half : (k + 1) * half, k * half : (k + 1) * half]
        part = jnp.where((rows // DIAG == cols // DIAG) & (rows < cols), values, 0.0)
        part = part + jnp.where(rows == cols, 1.0, 0.0)
        parts.append((values, part))
    size = DIAG
    while size < half:
        mask = (rows // (2 * size) == cols // (2 * size)) & (rows // size < cols // size)
        parts = [(v, p - dot(dot(p, jnp.where(mask, v, 0.0)), p)) for v, p in parts]
        size *= 2
    (_, first), (_, second) = parts
    corner = -dot(dot(first, upper[:half, half:]), second)
    left = jnp.concatenate([first.T, corner.T], axis=0)
    right = jnp.concatenate([jnp.zeros((half, half), jnp.float32), second.T], axis=0)
    return jnp.concatenate([left, right], axis=1)


def double_kernel(first, second, out, token):
    half = first.shape[0]
    out[:half] = first[...]
    out[half:] = second[...]
    token[...] = second[:8, :LANES]


def turn_kernel(slices, out, ordered):
    y = lax.axis_index("y")
    columns = [y]
    for distance in DISTANCES:
        columns += [column ^ distance for column in columns]
    for k, column in enumerate(columns):
        at = pl.ds(pl.multiple_of(column * DIAG, DIAG), DIAG)
        ordered[at, :] = slices[k * DIAG : (k + 1) * DIAG, :]
    out[...] = ordered[...].T


def finish_kernel(cap, mine, own, other, multipliers, trailing, out,
                  upper, inverse, block, current, in_sem, out_sem):
    copy = pltpu.make_async_copy(trailing, current, in_sem)
    copy.start()
    c = lax.axis_index("c")
    first = first_row()
    sides = ((pl.multiple_of(c * LANES, LANES), own), (pl.multiple_of((1 - c) * LANES, LANES), other))
    for x in range(X):
        for lane, ref in sides:
            for y in range(Y):
                at = DIAG * y + 8 * x
                upper[at : at + 8, pl.ds(lane, LANES)] = ref[x, NB + cap + 8 * y : NB + cap + 8 * y + 8, :]
    inverse[...] = invert(upper)
    copy.wait()

    def put(k):
        entry = mine[k]
        row = entry >> BITS
        rank = pl.ds(NB + (entry & (NB - 1)), 1)
        at = tile_of(row)
        hit = picked(row, LANES)
        for x in range(X):
            for lane, ref in sides:
                lanes = pl.ds(pl.multiple_of(x * C * LANES + lane, LANES), LANES)
                current[at, lanes] = jnp.where(hit, ref[x, rank, :], current[at, lanes])

    loop(mine[NB], put)
    copies = []
    width = C * LANES
    for x in range(X):
        lanes = slice(x * width, (x + 1) * width)
        for lane, ref in sides:
            block[x, :, pl.ds(lane, LANES)] = ref[x, :NB, :]
        solved = dot(inverse[...], block[x])
        block[x] = solved
        current[:, lanes] = current[:, lanes] - dot(multipliers[...], solved)

        @pl.when(first == 0)
        def _():
            current[:NB, lanes] = block[x]

        copies.append(pltpu.make_async_copy(current.at[:, lanes], out.at[:, lanes], out_sem.at[x]))
        copies[-1].start()
    for copy in copies:
        copy.wait()


def call(kernel, shape, smem, vmem, scratch=(), name=None, last=VMEM, out=VMEM, busy=2, table=None):
    many = isinstance(shape, list)
    shapes = [jax.ShapeDtypeStruct(s, jnp.float32) for s in (shape if many else [shape])]
    specs = [out] * len(shapes)
    if table is not None:
        shapes.append(jax.ShapeDtypeStruct((table,), jnp.int32))
        specs.append(SMEM)
    got = pl.pallas_call(
        kernel,
        out_shape=shapes,
        in_specs=[SMEM] * len(smem) + [VMEM] * (len(vmem) - 1) + [last],
        out_specs=specs,
        scratch_shapes=list(scratch),
        compiler_params=PARAMS,
        cost_estimate=pl.CostEstimate(flops=0, bytes_accessed=busy * 2**20, transcendentals=0),
        name=name,
    )(*smem, *vmem)
    return list(got) if many else got[0]


def pack(cap, pivots, trailing, panel_t):
    scratch = [pltpu.VMEM((DIAG, NB), jnp.float32), pltpu.VMEM((ROWS, COLS), jnp.float32), pltpu.SemaphoreType.DMA]
    return call(functools.partial(pack_kernel, cap), [(X, cap + NB + 8, LANES)] * 2,
                (pivots,), (panel_t, trailing), scratch, name="pack", last=ANY, table=NB + 8)


def join(cap, keep, got):
    return call(functools.partial(join_kernel, cap), [keep.shape[1:]] * X, (), (keep, got), name="join")


def spread(cap, room, plan, blocks, panel_t):
    return call(functools.partial(spread_kernel, cap, room), [(Z, cap + room + 8, LANES), panel_t.shape],
                (plan,), (*blocks, panel_t), [pltpu.VMEM((NB + 8, LANES), jnp.float32)], name="spread")


def collect(cap, room, plan, token, planes, pieces):
    return call(functools.partial(collect_kernel, cap, room), (X, NB + cap + 8 * Y, LANES),
                (plan,), (token, planes, pieces), name="collect")


def finish(cap, mine, own, other, multipliers, trailing):
    scratch = [pltpu.VMEM(s, jnp.float32) for s in ((NB, NB), (NB, NB), (X, NB, C * LANES), (ROWS, COLS))]
    scratch += [pltpu.SemaphoreType.DMA, pltpu.SemaphoreType.DMA((X,))]
    return call(functools.partial(finish_kernel, cap), (ROWS, COLS), (mine,),
                (own, other, multipliers, trailing), scratch, name="finish",
                last=ANY, out=pl.BlockSpec(memory_space=pltpu.HBM), busy=16)


swap = functools.partial(lax.all_to_all, split_axis=0, concat_axis=0, tiled=True)


def other_core(values):
    return lax.ppermute(values, "c", [(0, 1), (1, 0)])


def first_phase(cap, room, panel_t, trailing, pivots):
    keep, send, mine = pack(cap, pivots, trailing, panel_t)
    blocks = join(cap, keep, other_core(send))
    for s in range(1, X):
        blocks[s] = lax.ppermute(blocks[s], "x", [(x, (x + s) % X) for x in range(X)])
    return *spread(cap, room, make_plan(pivots), blocks, panel_t), mine


def from_column(values, distance):
    return lax.ppermute(values, "y", [(y, y ^ distance) for y in range(Y)])


def doubled(slices, distance):
    shape = (2 * slices.shape[0], ROWS)
    return call(double_kernel, [shape, (8, LANES)], (), (slices, from_column(slices, distance)), name="double")


def later_phases(cap, room, planes, slices, pivots):
    slices, token = doubled(slices, DISTANCES[0])
    planes = swap(planes, "z")
    pieces = call(pieces_kernel, (Y, 8, LANES), (), (token, planes), name="pieces")
    plan = make_plan(pivots, pieces)
    slices, token = doubled(slices, DISTANCES[1])
    blocks = collect(cap, room, plan, token, planes, swap(pieces, "y"))
    slices, _ = doubled(slices, DISTANCES[2])
    multipliers = call(turn_kernel, (ROWS, NB), (), (slices,), [pltpu.VMEM((NB, ROWS), jnp.float32)], name="turn")
    own, multipliers = lax.optimization_barrier((swap(blocks, "x"), multipliers))
    return plan[MOST], own, other_core(own), multipliers


def shards(panel, trailing, pivots):
    panel_t = panel.T

    def with_room(cap, room):
        planes, slices, mine = first_phase(cap, room, panel_t, trailing, pivots)
        most, *ready = later_phases(cap, room, planes, slices, pivots)
        return most, finish(cap, mine, *ready, trailing)

    def pending(carry):
        return carry[0]

    def again(carry):
        return jnp.zeros_like(carry[0]), with_room(NB, 2 * NB)[1]

    most, result = with_room(NARROW, NARROW)
    return lax.while_loop(pending, again, (most > NARROW, result))[1]


def solution(mesh):
    fine = Mesh(mesh.devices.reshape(X, Z, C, Y), ("x", "z", "c", "y"))
    split = P(("x", "z", "c"), "y")
    return jax.shard_map(shards, mesh=fine, in_specs=(split, split, P()), out_specs=split, check_vma=False)
```

```python
import functools

import jax
import jax.numpy as jnp
from jax import lax
from jax.experimental import pallas as pl
from jax.experimental.pallas import tpu as pltpu
from jax.sharding import Mesh, PartitionSpec as P

NB = 256
ORDER = 32768
LANES = 128
X, Z, C, Y = 4, 8, 2, 8
BLOCKS = X * C
ROWS = ORDER // (X * Z * C)
COLS = BLOCKS * LANES
DIAG = NB // Y
BATCH = 16
DISTANCES = (4, 2, 1)
FILLER, PLACE, TOPS = 0, NB, 2 * NB
COUNT = TOPS + NB + 8
MOST = COUNT + Z + 1
TABLE = 1024
BITS = NB.bit_length() - 1
ROW_BITS = ROWS.bit_length() - 1
PLANE_BITS = (ROWS * C).bit_length() - 1
NARROW = 56
HIGHEST = lax.Precision.HIGHEST
VMEM = pl.BlockSpec(memory_space=pltpu.VMEM)
SMEM = pl.BlockSpec(memory_space=pltpu.SMEM)
ANY = pl.BlockSpec(memory_space=pl.ANY)
PARAMS = pltpu.CompilerParams(vmem_limit_bytes=48 * 1024 * 1024)


def loop(count, body, unroll=1):
    def step(i, carry):
        body(i)
        return carry

    lax.fori_loop(0, count, step, 0, unroll=unroll)


def tile_of(row):
    return pl.ds(pl.multiple_of(row & -8, 8), 8)


def picked(row, width):
    return lax.broadcasted_iota(jnp.int32, (8, width), 0) == (row & 7)


def load_row(ref, row):
    tile = ref[tile_of(row), :]
    return jnp.sum(jnp.where(picked(row, tile.shape[1]), tile, 0.0), axis=0, keepdims=True)


def store_row(ref, row, values):
    at = tile_of(row)
    tile = ref[at, :]
    ref[at, :] = jnp.where(picked(row, tile.shape[1]), values, tile)


def plane_of(row):
    return (row >> PLANE_BITS) & (Z - 1)


def first_row():
    return ((lax.axis_index("x") * Z + lax.axis_index("z")) * C + lax.axis_index("c")) * ROWS


def plan_kernel(pivots, table, content):
    def start(i):
        content[i] = i
        content[pivots[i]] = pivots[i]

    loop(NB, start, 8)
    for z in range(Z):
        table[COUNT + z] = 0

    def exchange(i, found):
        at = pivots[i]
        left, right = content[i], content[at]
        content[i] = right
        content[at] = left
        table[TOPS + found] = i * NB + right
        plane = plane_of(at)
        have = table[COUNT + plane]
        table[PLACE + i] = plane * NB + have
        table[COUNT + plane] = have + 1
        return found + (right != at).astype(jnp.int32)

    found = lax.fori_loop(0, NB, exchange, jnp.int32(0), unroll=4)

    def fill(i):
        row = pivots[i]
        table[FILLER + i] = jnp.where(row < NB, 0, content[row])

    loop(NB, fill, 8)
    table[COUNT + Z] = found
    peak = table[COUNT]
    for z in range(1, Z):
        peak = jnp.maximum(peak, table[COUNT + z])
    table[MOST] = peak + found


def early_plan_kernel(*refs):
    @pl.when(lax.axis_index("z") == 0)
    def _():
        plan_kernel(*refs)


def late_plan_kernel(pivots, after, table, content):
    plan_kernel(pivots, table, content)


def make_plan(pivots, after=None):
    early = after is None
    return pl.pallas_call(
        early_plan_kernel if early else late_plan_kernel,
        out_shape=jax.ShapeDtypeStruct((TABLE,), jnp.int32),
        in_specs=[SMEM] if early else [SMEM, VMEM],
        out_specs=SMEM,
        scratch_shapes=[pltpu.SMEM((ORDER,), jnp.int32)],
        compiler_params=PARAMS,
        cost_estimate=pl.CostEstimate(flops=0, bytes_accessed=16 * 1024 * 1024, transcendentals=0),
        name="plan",
    )(*([pivots] if early else [pivots, after]))


def invert_diagonal(panel_t, at):
    y = lax.axis_index("y")
    lanes = pl.ds(pl.multiple_of((y * DIAG) & -LANES, LANES), LANES)
    shift = (y * DIAG) & (LANES - 1)
    window = pltpu.roll(panel_t[:, lanes], (LANES - shift) & (LANES - 1), axis=1)
    rows = lax.broadcasted_iota(jnp.int32, (DIAG, LANES), 0)
    cols = lax.broadcasted_iota(jnp.int32, (DIAG, LANES), 1)
    strict = (cols > rows) & (cols < DIAG)
    values = jnp.where(strict, window, 0.0)
    inverse = jnp.where(rows == cols, 1.0, 0.0)
    for k in range(DIAG - 1, 0, -1):
        inverse = inverse - values[:, k : k + 1] * inverse[k : k + 1, :]
    window = jnp.where(strict, inverse, window)
    at[:, :] = panel_t[:, :NB]
    at[:, lanes] = pltpu.roll(window, shift, axis=1)


def local_entry(cap, entry):
    return (entry >> BITS) & (ROWS - 1), jnp.minimum(entry & (NB - 1), cap - 1)


def pack_kernel(cap, pivots, panel_t, trailing, keep, send, mine, triangle, rows, sem):
    copy = pltpu.make_async_copy(trailing, rows, sem)
    copy.start()
    z = lax.axis_index("z")
    c = lax.axis_index("c")
    first = first_row()

    device = first >> ROW_BITS

    def find(i, carry):
        rank, found = carry
        row = pivots[i]
        mine[found] = (row << BITS) + rank
        rank = jnp.where(plane_of(row) == z, rank + 1, rank)
        return rank, jnp.where(row >> ROW_BITS == device, found + 1, found)

    _, found = lax.fori_loop(0, NB, find, (jnp.int32(0), jnp.int32(0)), unroll=16)
    invert_diagonal(panel_t, triangle)
    sides = ((keep, c), (send, 1 - c))
    for out, side in sides:
        for x in range(X):
            out[x, :cap, :] = jnp.zeros((cap, LANES), jnp.float32)
            lanes = pl.ds(pl.multiple_of(side * LANES, LANES), LANES)
            out[x, cap + NB :, :] = triangle[8 * x : 8 * x + 8, lanes]
    copy.wait()
    for out, side in sides:
        for x in range(X):
            lanes = pl.ds(pl.multiple_of((x * C + side) * LANES, LANES), LANES)
            out[x, cap : cap + NB, :] = rows[:NB, lanes]

    def put(k):
        row, rank = local_entry(cap, mine[k])
        at = pl.ds(rank, 1)
        hit = picked(row, LANES)
        for out, side in sides:
            for x in range(X):
                lanes = pl.ds(pl.multiple_of((x * C + side) * LANES, LANES), LANES)
                tile = jnp.where(hit, rows[tile_of(row), lanes], 0.0)
                out[x, at, :] = jnp.sum(tile, axis=0, keepdims=True)

    loop(found, put)
    mine[NB] = found


def join_kernel(cap, keep, got, *blocks):
    x = lax.axis_index("x")
    c = lax.axis_index("c")
    for s, out in enumerate(blocks):
        at = (x + s) & (X - 1)
        out[:cap, :] = keep[at, :cap, :] + got[at, :cap, :]
        out[cap:, :] = jnp.where(c == 0, keep[at, cap:, :], got[at, cap:, :])


def spread_kernel(cap, room, table, *refs):
    blocks, panel_t, out, panel_out, former = refs[:X], *refs[X:]
    x = lax.axis_index("x")
    rest = blocks[0][cap:, :]
    for s in range(1, X):
        rest = jnp.where(x == s, blocks[s][cap:, :], rest)
    former[...] = rest
    rows = blocks[0][:cap, :]
    for s in range(1, X):
        rows = rows + blocks[s][:cap, :]
    for z in range(Z):
        out[z, :cap, :] = rows
        out[z, cap + room :, :] = former[NB:, :]
    panel_out[...] = panel_t[...]

    @pl.when(lax.axis_index("z") == 0)
    def _():
        def put(k):
            moves = []
            for i in range(BATCH):
                where = table[PLACE + k * BATCH + i]
                rank = jnp.minimum(where & (NB - 1), cap - 1)
                filler = table[FILLER + k * BATCH + i]
                moves.append((where >> BITS, cap + rank, former[pl.ds(filler, 1), :]))
            for plane, at, values in moves:
                out[plane, pl.ds(at, 1), :] = values

        loop(NB // BATCH, put)

        def top(k):
            values = former[pl.ds(table[TOPS + k] & (NB - 1), 1), :]
            for z in range(Z):
                at = cap + jnp.minimum(table[COUNT + z] + k, room - 1)
                out[z, pl.ds(at, 1), :] = values

        loop(table[COUNT + Z], top)


def pieces_kernel(token, got, out):
    for y in range(Y):
        out[y] = got[0, got.shape[1] - 8 :, :]


def collect_kernel(cap, room, table, token, got, pieces, out):
    z = lax.axis_index("z")

    def take(k):
        base = pl.multiple_of(k * BATCH, BATCH)
        rows = []
        for i in range(BATCH):
            where = table[PLACE + base + i]
            rank = jnp.minimum(where & (NB - 1), cap - 1)
            rows.append(got[where >> BITS, pl.ds(rank, 1), :])
        for i in range(BATCH):
            out[0, pl.ds(base + i, 1), :] = rows[i]

    loop(NB // BATCH, take)

    def top(k):
        at = cap + jnp.minimum(table[COUNT + z] + k, room - 1)
        out[0, pl.ds(table[TOPS + k] >> BITS, 1), :] = got[0, pl.ds(at, 1), :]

    loop(table[COUNT + Z], top)
    out[0, NB : NB + cap, :] = got[0, cap : 2 * cap, :]
    for y in range(Y):
        out[0, NB + cap + 8 * y : NB + cap + 8 * y + 8, :] = pieces[y]
    for x in range(1, X):
        out[x] = out[0]


def dot(a, b):
    return jnp.dot(a, b, precision=HIGHEST, preferred_element_type=jnp.float32)


def invert(upper):
    half = NB // 2
    rows = lax.broadcasted_iota(jnp.int32, (half, half), 0)
    cols = lax.broadcasted_iota(jnp.int32, (half, half), 1)
    parts = []
    for k in range(2):
        values = upper[k * half : (k + 1) * half, k * half : (k + 1) * half]
        part = jnp.where((rows // DIAG == cols // DIAG) & (rows < cols), values, 0.0)
        part = part + jnp.where(rows == cols, 1.0, 0.0)
        parts.append((values, part))
    size = DIAG
    while size < half:
        mask = (rows // (2 * size) == cols // (2 * size)) & (rows // size < cols // size)
        parts = [(v, p - dot(dot(p, jnp.where(mask, v, 0.0)), p)) for v, p in parts]
        size *= 2
    (_, first), (_, second) = parts
    corner = -dot(dot(first, upper[:half, half:]), second)
    left = jnp.concatenate([first.T, corner.T], axis=0)
    right = jnp.concatenate([jnp.zeros((half, half), jnp.float32), second.T], axis=0)
    return jnp.concatenate([left, right], axis=1)


def double_kernel(first, second, out, token):
    half = first.shape[0]
    out[:half] = first[...]
    out[half:] = second[...]
    token[...] = second[:8, :LANES]


def turn_kernel(slices, out, ordered):
    y = lax.axis_index("y")
    columns = [y]
    for distance in DISTANCES:
        columns += [column ^ distance for column in columns]
    for k, column in enumerate(columns):
        at = pl.ds(pl.multiple_of(column * DIAG, DIAG), DIAG)
        ordered[at, :] = slices[k * DIAG : (k + 1) * DIAG, :]
    out[...] = ordered[...].T


def finish_kernel(cap, mine, own, other, multipliers, trailing, out,
                  upper, inverse, block, current, in_sem, out_sem):
    copy = pltpu.make_async_copy(trailing, current, in_sem)
    copy.start()
    c = lax.axis_index("c")
    first = first_row()
    sides = ((pl.multiple_of(c * LANES, LANES), own), (pl.multiple_of((1 - c) * LANES, LANES), other))
    for x in range(X):
        for lane, ref in sides:
            for y in range(Y):
                at = DIAG * y + 8 * x
                upper[at : at + 8, pl.ds(lane, LANES)] = ref[x, NB + cap + 8 * y : NB + cap + 8 * y + 8, :]
    inverse[...] = invert(upper)
    copy.wait()

    def put(k):
        row, rank = local_entry(cap, mine[k])
        rank = pl.ds(NB + rank, 1)
        at = tile_of(row)
        hit = picked(row, LANES)
        for x in range(X):
            for lane, ref in sides:
                lanes = pl.ds(pl.multiple_of(x * C * LANES + lane, LANES), LANES)
                current[at, lanes] = jnp.where(hit, ref[x, rank, :], current[at, lanes])

    loop(mine[NB], put)
    width = C * LANES

    def write(x):
        lanes = pl.ds(pl.multiple_of(x * width, width), width)
        return pltpu.make_async_copy(current.at[:, lanes], out.at[:, lanes], out_sem.at[x])

    def solve(x):
        slot = x & 1
        for lane, ref in sides:
            block[slot, :, pl.ds(lane, LANES)] = ref[x, :NB, :]
        block[slot] = dot(inverse[...], block[slot])

    def update(x):
        lanes = pl.ds(pl.multiple_of(x * width, width), width)
        slot = x & 1
        current[:, lanes] = current[:, lanes] - dot(multipliers[...], block[slot])

        @pl.when(first == 0)
        def _():
            current[:NB, lanes] = block[slot]

        write(x).start()

    def both(x):
        lanes = pl.ds(pl.multiple_of(x * width, width), width)
        slot = x & 1
        for lane, ref in sides:
            block[1 - slot, :, pl.ds(lane, LANES)] = ref[x + 1, :NB, :]
        solved = dot(inverse[...], block[1 - slot])
        product = dot(multipliers[...], block[slot])
        block[1 - slot] = solved
        current[:, lanes] = current[:, lanes] - product

        @pl.when(first == 0)
        def _():
            current[:NB, lanes] = block[slot]

        write(x).start()

    solve(0)
    loop(X - 1, both)
    update(X - 1)
    for x in range(X):
        write(x).wait()


def call(kernel, shape, smem, vmem, scratch=(), name=None, last=VMEM, out=VMEM, busy=2, table=None):
    many = isinstance(shape, list)
    shapes = [jax.ShapeDtypeStruct(s, jnp.float32) for s in (shape if many else [shape])]
    specs = [out] * len(shapes)
    if table is not None:
        shapes.append(jax.ShapeDtypeStruct((table,), jnp.int32))
        specs.append(SMEM)
    got = pl.pallas_call(
        kernel,
        out_shape=shapes,
        in_specs=[SMEM] * len(smem) + [VMEM] * (len(vmem) - 1) + [last],
        out_specs=specs,
        scratch_shapes=list(scratch),
        compiler_params=PARAMS,
        cost_estimate=pl.CostEstimate(flops=0, bytes_accessed=busy * 2**20, transcendentals=0),
        name=name,
    )(*smem, *vmem)
    return list(got) if many else got[0]


def pack(cap, pivots, trailing, panel_t):
    scratch = [pltpu.VMEM((DIAG, NB), jnp.float32), pltpu.VMEM((ROWS, COLS), jnp.float32), pltpu.SemaphoreType.DMA]
    return call(functools.partial(pack_kernel, cap), [(X, cap + NB + 8, LANES)] * 2,
                (pivots,), (panel_t, trailing), scratch, name="pack", last=ANY, table=NB + 8)


def join(cap, keep, got):
    return call(functools.partial(join_kernel, cap), [keep.shape[1:]] * X, (), (keep, got), name="join")


def spread(cap, room, plan, blocks, panel_t):
    return call(functools.partial(spread_kernel, cap, room), [(Z, cap + room + 8, LANES), panel_t.shape],
                (plan,), (*blocks, panel_t), [pltpu.VMEM((NB + 8, LANES), jnp.float32)], name="spread")


def collect(cap, room, plan, token, planes, pieces):
    return call(functools.partial(collect_kernel, cap, room), (X, NB + cap + 8 * Y, LANES),
                (plan,), (token, planes, pieces), name="collect")


def finish(cap, mine, own, other, multipliers, trailing):
    scratch = [pltpu.VMEM(s, jnp.float32) for s in ((NB, NB), (NB, NB), (2, NB, C * LANES), (ROWS, COLS))]
    scratch += [pltpu.SemaphoreType.DMA, pltpu.SemaphoreType.DMA((X,))]
    return call(functools.partial(finish_kernel, cap), (ROWS, COLS), (mine,),
                (own, other, multipliers, trailing), scratch, name="finish",
                last=ANY, out=pl.BlockSpec(memory_space=pltpu.HBM), busy=16)


swap = functools.partial(lax.all_to_all, split_axis=0, concat_axis=0, tiled=True)


def other_core(values):
    return lax.ppermute(values, "c", [(0, 1), (1, 0)])


def first_phase(cap, room, panel_t, trailing, pivots):
    keep, send, mine = pack(cap, pivots, trailing, panel_t)
    blocks = join(cap, keep, other_core(send))
    for s in range(1, X):
        blocks[s] = lax.ppermute(blocks[s], "x", [(x, (x + s) % X) for x in range(X)])
    return *spread(cap, room, make_plan(pivots), blocks, panel_t), mine


def from_column(values, distance):
    return lax.ppermute(values, "y", [(y, y ^ distance) for y in range(Y)])


def doubled(slices, distance):
    shape = (2 * slices.shape[0], ROWS)
    return call(double_kernel, [shape, (8, LANES)], (), (slices, from_column(slices, distance)), name="double")


def later_phases(cap, room, planes, slices, pivots):
    slices, token = doubled(slices, DISTANCES[0])
    planes = swap(planes, "z")
    pieces = call(pieces_kernel, (Y, 8, LANES), (), (token, planes), name="pieces")
    plan = make_plan(pivots, pieces)
    slices, token = doubled(slices, DISTANCES[1])
    blocks = collect(cap, room, plan, token, planes, swap(pieces, "y"))
    slices, _ = doubled(slices, DISTANCES[2])
    multipliers = call(turn_kernel, (ROWS, NB), (), (slices,), [pltpu.VMEM((NB, ROWS), jnp.float32)], name="turn")
    own, multipliers = lax.optimization_barrier((swap(blocks, "x"), multipliers))
    return plan[MOST], own, other_core(own), multipliers


def shards(panel, trailing, pivots):
    panel_t = panel.T

    def with_room(cap, room):
        planes, slices, mine = first_phase(cap, room, panel_t, trailing, pivots)
        most, *ready = later_phases(cap, room, planes, slices, pivots)
        return most, finish(cap, mine, *ready, trailing)

    def pending(carry):
        return carry[0]

    def again(carry):
        return jnp.zeros_like(carry[0]), with_room(NB, 2 * NB)[1]

    most, result = with_room(NARROW, NARROW)
    return lax.while_loop(pending, again, (most > NARROW, result))[1]


def solution(mesh):
    fine = Mesh(mesh.devices.reshape(X, Z, C, Y), ("x", "z", "c", "y"))
    split = P(("x", "z", "c"), "y")
    return jax.shard_map(shards, mesh=fine, in_specs=(split, split, P()), out_specs=split, check_vma=False)
```

```python
import functools

import jax
import jax.numpy as jnp
from jax import lax
from jax.experimental import pallas as pl
from jax.experimental.pallas import tpu as pltpu
from jax.sharding import Mesh, PartitionSpec as P

NB = 256
ORDER = 32768
LANES = 128
X, Z, C, Y = 4, 8, 2, 8
BLOCKS = X * C
ROWS = ORDER // (X * Z * C)
COLS = BLOCKS * LANES
DIAG = NB // Y
BATCH = 16
PIECE = DIAG // X * NB // LANES
DISTANCES = (4, 2, 1)
FILLER, PLACE, TOPS = 0, NB, 2 * NB
COUNT = TOPS + NB + 8
MOST = COUNT + Z + 1
TABLE = 1024
BITS = NB.bit_length() - 1
ROW_BITS = ROWS.bit_length() - 1
PLANE_BITS = (ROWS * C).bit_length() - 1
NARROW = 56
HIGHEST = lax.Precision.HIGHEST
VMEM = pl.BlockSpec(memory_space=pltpu.VMEM)
SMEM = pl.BlockSpec(memory_space=pltpu.SMEM)
ANY = pl.BlockSpec(memory_space=pl.ANY)
PARAMS = pltpu.CompilerParams(vmem_limit_bytes=48 * 1024 * 1024)


def loop(count, body, unroll=1):
    def step(i, carry):
        body(i)
        return carry

    lax.fori_loop(0, count, step, 0, unroll=unroll)


def tile_of(row):
    return pl.ds(pl.multiple_of(row & -8, 8), 8)


def picked(row, width):
    return lax.broadcasted_iota(jnp.int32, (8, width), 0) == (row & 7)


def load_row(ref, row):
    tile = ref[tile_of(row), :]
    return jnp.sum(jnp.where(picked(row, tile.shape[1]), tile, 0.0), axis=0, keepdims=True)


def store_row(ref, row, values):
    at = tile_of(row)
    tile = ref[at, :]
    ref[at, :] = jnp.where(picked(row, tile.shape[1]), values, tile)


def plane_of(row):
    return (row >> PLANE_BITS) & (Z - 1)


def first_row():
    return ((lax.axis_index("x") * Z + lax.axis_index("z")) * C + lax.axis_index("c")) * ROWS


def plan_kernel(pivots, table, content):
    def start(i):
        content[i] = i
        content[pivots[i]] = pivots[i]

    loop(NB, start, 8)
    for z in range(Z):
        table[COUNT + z] = 0

    def exchange(i, found):
        at = pivots[i]
        left, right = content[i], content[at]
        content[i] = right
        content[at] = left
        table[TOPS + found] = i * NB + right
        plane = plane_of(at)
        have = table[COUNT + plane]
        table[PLACE + i] = plane * NB + have
        table[COUNT + plane] = have + 1
        return found + (right != at).astype(jnp.int32)

    found = lax.fori_loop(0, NB, exchange, jnp.int32(0), unroll=4)

    def fill(i):
        row = pivots[i]
        table[FILLER + i] = jnp.where(row < NB, 0, content[row])

    loop(NB, fill, 8)
    table[COUNT + Z] = found
    peak = table[COUNT]
    for z in range(1, Z):
        peak = jnp.maximum(peak, table[COUNT + z])
    table[MOST] = peak + found


def make_plan(pivots):
    return pl.pallas_call(
        plan_kernel,
        out_shape=jax.ShapeDtypeStruct((TABLE,), jnp.int32),
        in_specs=[SMEM],
        out_specs=SMEM,
        scratch_shapes=[pltpu.SMEM((ORDER,), jnp.int32)],
        compiler_params=PARAMS,
        cost_estimate=pl.CostEstimate(flops=0, bytes_accessed=16 * 1024 * 1024, transcendentals=0),
        name="plan",
    )(pivots)


def invert_diagonal(panel_t, at):
    y = lax.axis_index("y")
    lanes = pl.ds(pl.multiple_of((y * DIAG) & -LANES, LANES), LANES)
    shift = (y * DIAG) & (LANES - 1)
    window = pltpu.roll(panel_t[:, lanes], (LANES - shift) & (LANES - 1), axis=1)
    rows = lax.broadcasted_iota(jnp.int32, (DIAG, LANES), 0)
    cols = lax.broadcasted_iota(jnp.int32, (DIAG, LANES), 1)
    strict = (cols > rows) & (cols < DIAG)
    values = jnp.where(strict, window, 0.0)
    inverse = jnp.where(rows == cols, 1.0, 0.0)
    for k in range(DIAG - 1, 0, -1):
        inverse = inverse - values[:, k : k + 1] * inverse[k : k + 1, :]
    window = jnp.where(strict, inverse, window)
    at[:, :] = panel_t[:, :NB]
    at[:, lanes] = pltpu.roll(window, shift, axis=1)


def local_entry(cap, entry):
    return (entry >> BITS) & (ROWS - 1), jnp.minimum(entry & (NB - 1), cap - 1)


def pack_kernel(cap, pivots, panel_t, trailing, keep, send, mine, triangle, rows, sem):
    copy = pltpu.make_async_copy(trailing, rows, sem)
    copy.start()
    z = lax.axis_index("z")
    c = lax.axis_index("c")
    first = first_row()

    device = first >> ROW_BITS

    def find(i, carry):
        rank, found = carry
        row = pivots[i]
        mine[found] = (row << BITS) + rank
        rank = jnp.where(plane_of(row) == z, rank + 1, rank)
        return rank, jnp.where(row >> ROW_BITS == device, found + 1, found)

    _, found = lax.fori_loop(0, NB, find, (jnp.int32(0), jnp.int32(0)), unroll=16)
    invert_diagonal(panel_t, triangle)
    sides = ((keep, c), (send, 1 - c))
    for out, side in sides:
        for x in range(X):
            out[x, :cap, :] = jnp.zeros((cap, LANES), jnp.float32)
            for h in range(2):
                at = cap + NB + 8 * h
                out[x, at : at + 8, :] = triangle[8 * x : 8 * x + 8, h * LANES : (h + 1) * LANES]
    copy.wait()
    for out, side in sides:
        for x in range(X):
            lanes = pl.ds(pl.multiple_of((x * C + side) * LANES, LANES), LANES)
            out[x, cap : cap + NB, :] = rows[:NB, lanes]

    def put(k):
        row, rank = local_entry(cap, mine[k])
        at = pl.ds(rank, 1)
        hit = picked(row, LANES)
        for out, side in sides:
            for x in range(X):
                lanes = pl.ds(pl.multiple_of((x * C + side) * LANES, LANES), LANES)
                tile = jnp.where(hit, rows[tile_of(row), lanes], 0.0)
                out[x, at, :] = jnp.sum(tile, axis=0, keepdims=True)

    loop(found, put)
    mine[NB] = found


def join_kernel(cap, keep, got, *blocks):
    x = lax.axis_index("x")
    c = lax.axis_index("c")
    for s, out in enumerate(blocks):
        at = (x + s) & (X - 1)
        out[:cap, :] = keep[at, :cap, :] + got[at, :cap, :]
        out[cap:, :] = jnp.where(c == 0, keep[at, cap:, :], got[at, cap:, :])


def spread_kernel(cap, room, table, *refs):
    blocks, panel_t, out, panel_out, former = refs[:X], *refs[X:]
    x = lax.axis_index("x")
    rest = blocks[0][cap:, :]
    for s in range(1, X):
        rest = jnp.where(x == s, blocks[s][cap:, :], rest)
    former[...] = rest
    rows = blocks[0][:cap, :]
    for s in range(1, X):
        rows = rows + blocks[s][:cap, :]
    for z in range(Z):
        out[z, :cap, :] = rows
        out[z, cap + room :, :] = former[NB:, :]
    panel_out[...] = panel_t[...]

    @pl.when(lax.axis_index("z") == 0)
    def _():
        def put(k):
            moves = []
            for i in range(BATCH):
                where = table[PLACE + k * BATCH + i]
                rank = jnp.minimum(where & (NB - 1), cap - 1)
                filler = table[FILLER + k * BATCH + i]
                moves.append((where >> BITS, cap + rank, former[pl.ds(filler, 1), :]))
            for plane, at, values in moves:
                out[plane, pl.ds(at, 1), :] = values

        loop(NB // BATCH, put)

        def top(k):
            values = former[pl.ds(table[TOPS + k] & (NB - 1), 1), :]
            for z in range(Z):
                at = cap + jnp.minimum(table[COUNT + z] + k, room - 1)
                out[z, pl.ds(at, 1), :] = values

        loop(table[COUNT + Z], top)


def slice_kernel(token, own, out):
    for x in range(X):
        for y in range(Y):
            out[y, x * PIECE : (x + 1) * PIECE, :] = own[x, own.shape[1] - PIECE :, :]


def collect_kernel(cap, room, table, token, got, out):
    z = lax.axis_index("z")

    def take(k):
        base = pl.multiple_of(k * BATCH, BATCH)
        rows = []
        for i in range(BATCH):
            where = table[PLACE + base + i]
            rank = jnp.minimum(where & (NB - 1), cap - 1)
            rows.append(got[where >> BITS, pl.ds(rank, 1), :])
        for i in range(BATCH):
            out[0, pl.ds(base + i, 1), :] = rows[i]

    loop(NB // BATCH, take)

    def top(k):
        at = cap + jnp.minimum(table[COUNT + z] + k, room - 1)
        out[0, pl.ds(table[TOPS + k] >> BITS, 1), :] = got[0, pl.ds(at, 1), :]

    loop(table[COUNT + Z], top)
    out[0, NB : NB + cap, :] = got[0, cap : 2 * cap, :]
    out[0, NB + cap :, :] = got[0, cap + room :, :]
    for x in range(1, X):
        out[x] = out[0]


def dot(a, b):
    return jnp.dot(a, b, precision=HIGHEST, preferred_element_type=jnp.float32)


def invert(upper):
    half = NB // 2
    rows = lax.broadcasted_iota(jnp.int32, (half, half), 0)
    cols = lax.broadcasted_iota(jnp.int32, (half, half), 1)
    parts = []
    for k in range(2):
        values = upper[k * half : (k + 1) * half, k * half : (k + 1) * half]
        part = jnp.where((rows // DIAG == cols // DIAG) & (rows < cols), values, 0.0)
        part = part + jnp.where(rows == cols, 1.0, 0.0)
        parts.append((values, part))
    size = DIAG
    while size < half:
        mask = (rows // (2 * size) == cols // (2 * size)) & (rows // size < cols // size)
        parts = [(v, p - dot(dot(p, jnp.where(mask, v, 0.0)), p)) for v, p in parts]
        size *= 2
    (_, first), (_, second) = parts
    corner = -dot(dot(first, upper[:half, half:]), second)
    left = jnp.concatenate([first.T, corner.T], axis=0)
    right = jnp.concatenate([jnp.zeros((half, half), jnp.float32), second.T], axis=0)
    return jnp.concatenate([left, right], axis=1)


def double_kernel(first, second, out, token):
    half = first.shape[0]
    out[:half] = first[...]
    out[half:] = second[...]
    token[...] = second[:8, :LANES]


def turn_kernel(slices, out, ordered):
    y = lax.axis_index("y")
    columns = [y]
    for distance in DISTANCES:
        columns += [column ^ distance for column in columns]
    for k, column in enumerate(columns):
        at = pl.ds(pl.multiple_of(column * DIAG, DIAG), DIAG)
        ordered[at, :] = slices[k * DIAG : (k + 1) * DIAG, :]
    out[...] = ordered[...].T


def finish_kernel(cap, mine, whole, own, other, multipliers, trailing, out,
                  upper, inverse, block, current, in_sem, out_sem):
    copy = pltpu.make_async_copy(trailing, current, in_sem)
    copy.start()
    c = lax.axis_index("c")
    first = first_row()
    sides = ((pl.multiple_of(c * LANES, LANES), own), (pl.multiple_of((1 - c) * LANES, LANES), other))
    for y in range(Y):
        for x in range(X):
            for h in range(2):
                at, start = DIAG * y + 8 * x, PIECE * x + 8 * h
                upper[at : at + 8, h * LANES : (h + 1) * LANES] = whole[y, start : start + 8, :]
    inverse[...] = invert(upper)
    copy.wait()

    def put(k):
        row, rank = local_entry(cap, mine[k])
        rank = pl.ds(NB + rank, 1)
        at = tile_of(row)
        hit = picked(row, LANES)
        for x in range(X):
            for lane, ref in sides:
                lanes = pl.ds(pl.multiple_of(x * C * LANES + lane, LANES), LANES)
                current[at, lanes] = jnp.where(hit, ref[x, rank, :], current[at, lanes])

    loop(mine[NB], put)
    width = C * LANES

    def write(x):
        lanes = pl.ds(pl.multiple_of(x * width, width), width)
        return pltpu.make_async_copy(current.at[:, lanes], out.at[:, lanes], out_sem.at[x])

    def solve(x):
        slot = x & 1
        for lane, ref in sides:
            block[slot, :, pl.ds(lane, LANES)] = ref[x, :NB, :]
        block[slot] = dot(inverse[...], block[slot])

    def update(x):
        lanes = pl.ds(pl.multiple_of(x * width, width), width)
        slot = x & 1
        current[:, lanes] = current[:, lanes] - dot(multipliers[...], block[slot])

        @pl.when(first == 0)
        def _():
            current[:NB, lanes] = block[slot]

        write(x).start()

    def both(x):
        lanes = pl.ds(pl.multiple_of(x * width, width), width)
        slot = x & 1
        for lane, ref in sides:
            block[1 - slot, :, pl.ds(lane, LANES)] = ref[x + 1, :NB, :]
        solved = dot(inverse[...], block[1 - slot])
        product = dot(multipliers[...], block[slot])
        block[1 - slot] = solved
        current[:, lanes] = current[:, lanes] - product

        @pl.when(first == 0)
        def _():
            current[:NB, lanes] = block[slot]

        write(x).start()

    solve(0)
    loop(X - 1, both)
    update(X - 1)
    for x in range(X):
        write(x).wait()


def call(kernel, shape, smem, vmem, scratch=(), name=None, last=VMEM, out=VMEM, busy=2, table=None):
    many = isinstance(shape, list)
    shapes = [jax.ShapeDtypeStruct(s, jnp.float32) for s in (shape if many else [shape])]
    specs = [out] * len(shapes)
    if table is not None:
        shapes.append(jax.ShapeDtypeStruct((table,), jnp.int32))
        specs.append(SMEM)
    got = pl.pallas_call(
        kernel,
        out_shape=shapes,
        in_specs=[SMEM] * len(smem) + [VMEM] * (len(vmem) - 1) + [last],
        out_specs=specs,
        scratch_shapes=list(scratch),
        compiler_params=PARAMS,
        cost_estimate=pl.CostEstimate(flops=0, bytes_accessed=busy * 2**20, transcendentals=0),
        name=name,
    )(*smem, *vmem)
    return list(got) if many else got[0]


def pack(cap, pivots, trailing, panel_t):
    scratch = [pltpu.VMEM((DIAG, NB), jnp.float32), pltpu.VMEM((ROWS, COLS), jnp.float32), pltpu.SemaphoreType.DMA]
    return call(functools.partial(pack_kernel, cap), [(X, cap + NB + PIECE, LANES)] * 2,
                (pivots,), (panel_t, trailing), scratch, name="pack", last=ANY, table=NB + 8)


def join(cap, keep, got):
    return call(functools.partial(join_kernel, cap), [keep.shape[1:]] * X, (), (keep, got), name="join")


def spread(cap, room, plan, blocks, panel_t):
    return call(functools.partial(spread_kernel, cap, room), [(Z, cap + room + PIECE, LANES), panel_t.shape],
                (plan,), (*blocks, panel_t), [pltpu.VMEM((NB + PIECE, LANES), jnp.float32)], name="spread")


def collect(cap, room, plan, token, planes):
    return call(functools.partial(collect_kernel, cap, room), (X, NB + cap + PIECE, LANES),
                (plan,), (token, planes), name="collect")


def finish(cap, mine, whole, own, other, multipliers, trailing):
    scratch = [pltpu.VMEM(s, jnp.float32) for s in ((NB, NB), (NB, NB), (2, NB, C * LANES), (ROWS, COLS))]
    scratch += [pltpu.SemaphoreType.DMA, pltpu.SemaphoreType.DMA((X,))]
    return call(functools.partial(finish_kernel, cap), (ROWS, COLS), (mine,),
                (whole, own, other, multipliers, trailing), scratch, name="finish",
                last=ANY, out=pl.BlockSpec(memory_space=pltpu.HBM), busy=16)


swap = functools.partial(lax.all_to_all, split_axis=0, concat_axis=0, tiled=True)


def other_core(values):
    return lax.ppermute(values, "c", [(0, 1), (1, 0)])


def first_phase(cap, room, panel_t, trailing, pivots):
    keep, send, mine = pack(cap, pivots, trailing, panel_t)
    blocks = join(cap, keep, other_core(send))
    for s in range(1, X):
        blocks[s] = lax.ppermute(blocks[s], "x", [(x, (x + s) % X) for x in range(X)])
    plan = make_plan(pivots)
    return *spread(cap, room, plan, blocks, panel_t), plan, mine


def from_column(values, distance):
    return lax.ppermute(values, "y", [(y, y ^ distance) for y in range(Y)])


def doubled(slices, distance):
    shape = (2 * slices.shape[0], ROWS)
    return call(double_kernel, [shape, (8, LANES)], (), (slices, from_column(slices, distance)), name="double")


def later_phases(cap, room, planes, slices, plan):
    slices, token = doubled(slices, DISTANCES[0])
    blocks = collect(cap, room, plan, token, swap(planes, "z"))
    slices, token = doubled(slices, DISTANCES[1])
    own = swap(blocks, "x")
    whole = swap(call(slice_kernel, (Y, X * PIECE, LANES), (), (token, own), name="slice"), "y")
    other = other_core(own)
    slices, _ = doubled(slices, DISTANCES[2])
    multipliers = call(turn_kernel, (ROWS, NB), (), (slices,), [pltpu.VMEM((NB, ROWS), jnp.float32)], name="turn")
    return whole, own, other, multipliers


def shards(panel, trailing, pivots):
    panel_t = panel.T

    def with_room(cap, room):
        planes, slices, plan, mine = first_phase(cap, room, panel_t, trailing, pivots)
        ready = later_phases(cap, room, planes, slices, plan)
        return plan[MOST], finish(cap, mine, *ready, trailing)

    def pending(carry):
        return carry[0]

    def again(carry):
        return jnp.zeros_like(carry[0]), with_room(NB, 2 * NB)[1]

    most, result = with_room(NARROW, NARROW)
    return lax.while_loop(pending, again, (most > NARROW, result))[1]


def solution(mesh):
    fine = Mesh(mesh.devices.reshape(X, Z, C, Y), ("x", "z", "c", "y"))
    split = P(("x", "z", "c"), "y")
    return jax.shard_map(shards, mesh=fine, in_specs=(split, split, P()), out_specs=split, check_vma=False)
```

```python
import functools

import jax
import jax.numpy as jnp
from jax import lax
from jax.experimental import pallas as pl
from jax.experimental.pallas import tpu as pltpu
from jax.sharding import Mesh, PartitionSpec as P

NB = 256
ORDER = 32768
LANES = 128
X, Z, C, Y = 4, 8, 2, 8
BLOCKS = X * C
ROWS = ORDER // (X * Z * C)
COLS = BLOCKS * LANES
DIAG = NB // Y
BATCH = 16
DISTANCES = (4, 2, 1)
FILLER, PLACE, TOPS = 0, NB, 2 * NB
COUNT = TOPS + NB + 8
MOST = COUNT + Z + 1
TABLE = 1024
BITS = NB.bit_length() - 1
ROW_BITS = ROWS.bit_length() - 1
PLANE_BITS = (ROWS * C).bit_length() - 1
NARROW = 56
HIGHEST = lax.Precision.HIGHEST
VMEM = pl.BlockSpec(memory_space=pltpu.VMEM)
SMEM = pl.BlockSpec(memory_space=pltpu.SMEM)
ANY = pl.BlockSpec(memory_space=pl.ANY)
HBM = pl.BlockSpec(memory_space=pltpu.HBM)
PARAMS = pltpu.CompilerParams(vmem_limit_bytes=48 * 1024 * 1024)


def loop(count, body, unroll=1):
    def step(i, carry):
        body(i)
        return carry

    lax.fori_loop(0, count, step, 0, unroll=unroll)


def tile_of(row):
    return pl.ds(pl.multiple_of(row & -8, 8), 8)


def picked(row, width):
    return lax.broadcasted_iota(jnp.int32, (8, width), 0) == (row & 7)


def load_row(ref, row):
    tile = ref[tile_of(row), :]
    return jnp.sum(jnp.where(picked(row, tile.shape[1]), tile, 0.0), axis=0, keepdims=True)


def store_row(ref, row, values):
    at = tile_of(row)
    tile = ref[at, :]
    ref[at, :] = jnp.where(picked(row, tile.shape[1]), values, tile)


def plane_of(row):
    return (row >> PLANE_BITS) & (Z - 1)


def first_row():
    return ((lax.axis_index("x") * Z + lax.axis_index("z")) * C + lax.axis_index("c")) * ROWS


def plan_kernel(pivots, table, content):
    def start(i):
        content[i] = i
        content[pivots[i]] = pivots[i]

    loop(NB, start, 8)
    for z in range(Z):
        table[COUNT + z] = 0

    def exchange(i, found):
        at = pivots[i]
        left, right = content[i], content[at]
        content[i] = right
        content[at] = left
        table[TOPS + found] = i * NB + right
        plane = plane_of(at)
        have = table[COUNT + plane]
        table[PLACE + i] = plane * NB + have
        table[COUNT + plane] = have + 1
        return found + (right != at).astype(jnp.int32)

    found = lax.fori_loop(0, NB, exchange, jnp.int32(0), unroll=4)

    def fill(i):
        row = pivots[i]
        table[FILLER + i] = jnp.where(row < NB, 0, content[row])

    loop(NB, fill, 8)
    table[COUNT + Z] = found
    peak = table[COUNT]
    for z in range(1, Z):
        peak = jnp.maximum(peak, table[COUNT + z])
    table[MOST] = peak + found


def early_plan_kernel(*refs):
    @pl.when(lax.axis_index("z") == 0)
    def _():
        plan_kernel(*refs)


def late_plan_kernel(pivots, after, table, content):
    plan_kernel(pivots, table, content)


def make_plan(pivots, after=None):
    early = after is None
    return pl.pallas_call(
        early_plan_kernel if early else late_plan_kernel,
        out_shape=jax.ShapeDtypeStruct((TABLE,), jnp.int32),
        in_specs=[SMEM] if early else [SMEM, VMEM],
        out_specs=SMEM,
        scratch_shapes=[pltpu.SMEM((ORDER,), jnp.int32)],
        compiler_params=PARAMS,
        cost_estimate=pl.CostEstimate(flops=0, bytes_accessed=16 * 1024 * 1024, transcendentals=0),
        name="plan",
    )(*([pivots] if early else [pivots, after]))


def invert_diagonal(panel_t, at):
    y = lax.axis_index("y")
    lanes = pl.ds(pl.multiple_of((y * DIAG) & -LANES, LANES), LANES)
    shift = (y * DIAG) & (LANES - 1)
    window = pltpu.roll(panel_t[:, lanes], (LANES - shift) & (LANES - 1), axis=1)
    rows = lax.broadcasted_iota(jnp.int32, (DIAG, LANES), 0)
    cols = lax.broadcasted_iota(jnp.int32, (DIAG, LANES), 1)
    strict = (cols > rows) & (cols < DIAG)
    values = jnp.where(strict, window, 0.0)
    inverse = jnp.where(rows == cols, 1.0, 0.0)
    for k in range(DIAG - 1, 0, -1):
        inverse = inverse - values[:, k : k + 1] * inverse[k : k + 1, :]
    window = jnp.where(strict, inverse, window)
    at[:, :] = panel_t[:, :NB]
    at[:, lanes] = pltpu.roll(window, shift, axis=1)


def local_entry(cap, entry):
    return (entry >> BITS) & (ROWS - 1), jnp.minimum(entry & (NB - 1), cap - 1)


def pack_kernel(cap, pivots, panel_t, trailing, keep, send, mine, triangle, rows, sem):
    copy = pltpu.make_async_copy(trailing, rows, sem)
    copy.start()
    z = lax.axis_index("z")
    c = lax.axis_index("c")
    first = first_row()

    device = first >> ROW_BITS

    def find(i, carry):
        rank, found = carry
        row = pivots[i]
        mine[found] = (row << BITS) + rank
        rank = jnp.where(plane_of(row) == z, rank + 1, rank)
        return rank, jnp.where(row >> ROW_BITS == device, found + 1, found)

    _, found = lax.fori_loop(0, NB, find, (jnp.int32(0), jnp.int32(0)), unroll=16)
    invert_diagonal(panel_t, triangle)
    sides = ((keep, c), (send, 1 - c))
    for out, side in sides:
        for x in range(X):
            out[x, :cap, :] = jnp.zeros((cap, LANES), jnp.float32)
            lanes = pl.ds(pl.multiple_of(side * LANES, LANES), LANES)
            out[x, cap + NB :, :] = triangle[8 * x : 8 * x + 8, lanes]
    copy.wait()
    for out, side in sides:
        for x in range(X):
            lanes = pl.ds(pl.multiple_of((x * C + side) * LANES, LANES), LANES)
            out[x, cap : cap + NB, :] = rows[:NB, lanes]

    def put(k):
        row, rank = local_entry(cap, mine[k])
        at = pl.ds(rank, 1)
        hit = picked(row, LANES)
        for out, side in sides:
            for x in range(X):
                lanes = pl.ds(pl.multiple_of((x * C + side) * LANES, LANES), LANES)
                tile = jnp.where(hit, rows[tile_of(row), lanes], 0.0)
                out[x, at, :] = jnp.sum(tile, axis=0, keepdims=True)

    loop(found, put)
    mine[NB] = found


def join_kernel(cap, keep, got, *blocks):
    x = lax.axis_index("x")
    c = lax.axis_index("c")
    for s, out in enumerate(blocks):
        at = (x + s) & (X - 1)
        out[:cap, :] = keep[at, :cap, :] + got[at, :cap, :]
        out[cap:, :] = jnp.where(c == 0, keep[at, cap:, :], got[at, cap:, :])


def spread_kernel(cap, room, table, *refs):
    blocks, panel_t, out, panel_out, former = refs[:X], *refs[X:]
    x = lax.axis_index("x")
    rows = blocks[0][:cap, :]
    for s in range(1, X):
        rows = rows + blocks[s][:cap, :]
    for z in range(Z):
        out[z, :cap, :] = rows
    panel_out[...] = panel_t[...]

    @pl.when(lax.axis_index("z") == 0)
    def _():
        rest = blocks[0][cap:, :]
        for s in range(1, X):
            rest = jnp.where(x == s, blocks[s][cap:, :], rest)
        former[...] = rest
        for z in range(Z):
            out[z, cap + room :, :] = former[NB:, :]

        def put(k):
            moves = []
            for i in range(BATCH):
                where = table[PLACE + k * BATCH + i]
                rank = jnp.minimum(where & (NB - 1), cap - 1)
                filler = table[FILLER + k * BATCH + i]
                moves.append((where >> BITS, cap + rank, former[pl.ds(filler, 1), :]))
            for plane, at, values in moves:
                out[plane, pl.ds(at, 1), :] = values

        loop(NB // BATCH, put)

        def top(k):
            values = former[pl.ds(table[TOPS + k] & (NB - 1), 1), :]
            for z in range(Z):
                at = cap + jnp.minimum(table[COUNT + z] + k, room - 1)
                out[z, pl.ds(at, 1), :] = values

        loop(table[COUNT + Z], top)


def pieces_kernel(token, got, out):
    for y in range(Y):
        out[y] = got[0, got.shape[1] - 8 :, :]


def collect_kernel(cap, room, table, token, got, out, block, sem):
    z = lax.axis_index("z")

    def take(k):
        base = pl.multiple_of(k * BATCH, BATCH)
        rows = []
        for i in range(BATCH):
            where = table[PLACE + base + i]
            rank = jnp.minimum(where & (NB - 1), cap - 1)
            rows.append(got[where >> BITS, pl.ds(rank, 1), :])
        for i in range(BATCH):
            block[pl.ds(base + i, 1), :] = rows[i]

    loop(NB // BATCH, take)

    def top(k):
        at = cap + jnp.minimum(table[COUNT + z] + k, room - 1)
        block[pl.ds(table[TOPS + k] >> BITS, 1), :] = got[0, pl.ds(at, 1), :]

    loop(table[COUNT + Z], top)
    block[NB:, :] = got[0, cap : 2 * cap, :]
    copies = [pltpu.make_async_copy(block, out.at[x, pl.ds(0, NB + cap), :], sem.at[x]) for x in range(X)]
    for copy in copies:
        copy.start()
    for copy in copies:
        copy.wait()


def append_kernel(cap, pieces, blocks, out, rows, sem):
    for y in range(Y):
        rows[8 * y : 8 * y + 8, :] = pieces[y]
    copies = [pltpu.make_async_copy(rows, out.at[x, pl.ds(NB + cap, 8 * Y), :], sem.at[x]) for x in range(X)]
    for copy in copies:
        copy.start()
    for copy in copies:
        copy.wait()


def dot(a, b):
    return jnp.dot(a, b, precision=HIGHEST, preferred_element_type=jnp.float32)


def invert(upper):
    half = NB // 2
    rows = lax.broadcasted_iota(jnp.int32, (half, half), 0)
    cols = lax.broadcasted_iota(jnp.int32, (half, half), 1)
    parts = []
    for k in range(2):
        values = upper[k * half : (k + 1) * half, k * half : (k + 1) * half]
        part = jnp.where((rows // DIAG == cols // DIAG) & (rows < cols), values, 0.0)
        part = part + jnp.where(rows == cols, 1.0, 0.0)
        parts.append((values, part))
    size = DIAG
    while size < half:
        mask = (rows // (2 * size) == cols // (2 * size)) & (rows // size < cols // size)
        parts = [(v, p - dot(dot(p, jnp.where(mask, v, 0.0)), p)) for v, p in parts]
        size *= 2
    (_, first), (_, second) = parts
    corner = -dot(dot(first, upper[:half, half:]), second)
    left = jnp.concatenate([first.T, corner.T], axis=0)
    right = jnp.concatenate([jnp.zeros((half, half), jnp.float32), second.T], axis=0)
    return jnp.concatenate([left, right], axis=1)


def double_kernel(first, second, out, token):
    half = first.shape[0]
    out[:half] = first[...]
    out[half:] = second[...]
    token[...] = second[:8, :LANES]


def turn_kernel(slices, out, ordered):
    y = lax.axis_index("y")
    columns = [y]
    for distance in DISTANCES:
        columns += [column ^ distance for column in columns]
    for k, column in enumerate(columns):
        at = pl.ds(pl.multiple_of(column * DIAG, DIAG), DIAG)
        ordered[at, :] = slices[k * DIAG : (k + 1) * DIAG, :]
    out[...] = ordered[...].T


def finish_kernel(cap, mine, own, other, multipliers, trailing, out,
                  upper, inverse, block, current, in_sem, out_sem):
    copy = pltpu.make_async_copy(trailing, current, in_sem)
    copy.start()
    c = lax.axis_index("c")
    first = first_row()
    sides = ((pl.multiple_of(c * LANES, LANES), own), (pl.multiple_of((1 - c) * LANES, LANES), other))
    for x in range(X):
        for lane, ref in sides:
            for y in range(Y):
                at = DIAG * y + 8 * x
                upper[at : at + 8, pl.ds(lane, LANES)] = ref[x, NB + cap + 8 * y : NB + cap + 8 * y + 8, :]
    inverse[...] = invert(upper)
    copy.wait()

    def put(k):
        row, rank = local_entry(cap, mine[k])
        rank = pl.ds(NB + rank, 1)
        at = tile_of(row)
        hit = picked(row, LANES)
        for x in range(X):
            for lane, ref in sides:
                lanes = pl.ds(pl.multiple_of(x * C * LANES + lane, LANES), LANES)
                current[at, lanes] = jnp.where(hit, ref[x, rank, :], current[at, lanes])

    loop(mine[NB], put)
    width = C * LANES

    def write(x):
        lanes = pl.ds(pl.multiple_of(x * width, width), width)
        return pltpu.make_async_copy(current.at[:, lanes], out.at[:, lanes], out_sem.at[x])

    def solve(x):
        slot = x & 1
        for lane, ref in sides:
            block[slot, :, pl.ds(lane, LANES)] = ref[x, :NB, :]
        block[slot] = dot(inverse[...], block[slot])

    def update(x):
        lanes = pl.ds(pl.multiple_of(x * width, width), width)
        slot = x & 1
        current[:, lanes] = current[:, lanes] - dot(multipliers[...], block[slot])

        @pl.when(first == 0)
        def _():
            current[:NB, lanes] = block[slot]

        write(x).start()

    def both(x):
        lanes = pl.ds(pl.multiple_of(x * width, width), width)
        slot = x & 1
        for lane, ref in sides:
            block[1 - slot, :, pl.ds(lane, LANES)] = ref[x + 1, :NB, :]
        solved = dot(inverse[...], block[1 - slot])
        product = dot(multipliers[...], block[slot])
        block[1 - slot] = solved
        current[:, lanes] = current[:, lanes] - product

        @pl.when(first == 0)
        def _():
            current[:NB, lanes] = block[slot]

        write(x).start()

    solve(0)
    loop(X - 1, both)
    update(X - 1)
    for x in range(X):
        write(x).wait()


def call(kernel, shape, smem, vmem, scratch=(), name=None, last=VMEM, out=VMEM, busy=2, table=None, aliases={}):
    many = isinstance(shape, list)
    shapes = [jax.ShapeDtypeStruct(s, jnp.float32) for s in (shape if many else [shape])]
    specs = [out] * len(shapes)
    if table is not None:
        shapes.append(jax.ShapeDtypeStruct((table,), jnp.int32))
        specs.append(SMEM)
    got = pl.pallas_call(
        kernel,
        out_shape=shapes,
        in_specs=[SMEM] * len(smem) + [VMEM] * (len(vmem) - 1) + [last],
        out_specs=specs,
        scratch_shapes=list(scratch),
        compiler_params=PARAMS,
        input_output_aliases=aliases,
        cost_estimate=pl.CostEstimate(flops=0, bytes_accessed=busy * 2**20, transcendentals=0),
        name=name,
    )(*smem, *vmem)
    return list(got) if many else got[0]


def pack(cap, pivots, trailing, panel_t):
    scratch = [pltpu.VMEM((DIAG, NB), jnp.float32), pltpu.VMEM((ROWS, COLS), jnp.float32), pltpu.SemaphoreType.DMA]
    return call(functools.partial(pack_kernel, cap), [(X, cap + NB + 8, LANES)] * 2,
                (pivots,), (panel_t, trailing), scratch, name="pack", last=ANY, table=NB + 8)


def join(cap, keep, got):
    return call(functools.partial(join_kernel, cap), [keep.shape[1:]] * X, (), (keep, got), name="join")


def spread(cap, room, plan, blocks, panel_t):
    return call(functools.partial(spread_kernel, cap, room), [(Z, cap + room + 8, LANES), panel_t.shape],
                (plan,), (*blocks, panel_t), [pltpu.VMEM((NB + 8, LANES), jnp.float32)], name="spread")


def collect(cap, room, plan, token, planes):
    scratch = [pltpu.VMEM((NB + cap, LANES), jnp.float32), pltpu.SemaphoreType.DMA((X,))]
    return call(functools.partial(collect_kernel, cap, room), (X, NB + cap + 8 * Y, LANES),
                (plan,), (token, planes), scratch, name="collect", out=HBM)


def append(cap, pieces, blocks):
    scratch = [pltpu.VMEM((8 * Y, LANES), jnp.float32), pltpu.SemaphoreType.DMA((X,))]
    return call(functools.partial(append_kernel, cap), blocks.shape, (), (pieces, blocks), scratch,
                name="append", last=HBM, out=HBM, aliases={1: 0})


def finish(cap, mine, own, other, multipliers, trailing):
    scratch = [pltpu.VMEM(s, jnp.float32) for s in ((NB, NB), (NB, NB), (2, NB, C * LANES), (ROWS, COLS))]
    scratch += [pltpu.SemaphoreType.DMA, pltpu.SemaphoreType.DMA((X,))]
    return call(functools.partial(finish_kernel, cap), (ROWS, COLS), (mine,),
                (own, other, multipliers, trailing), scratch, name="finish",
                last=ANY, out=HBM, busy=16)


swap = functools.partial(lax.all_to_all, split_axis=0, concat_axis=0, tiled=True)


def other_core(values):
    return lax.ppermute(values, "c", [(0, 1), (1, 0)])


def first_phase(cap, room, panel_t, trailing, pivots):
    keep, send, mine = pack(cap, pivots, trailing, panel_t)
    blocks = join(cap, keep, other_core(send))
    for s in range(1, X):
        blocks[s] = lax.ppermute(blocks[s], "x", [(x, (x + s) % X) for x in range(X)])
    return *spread(cap, room, make_plan(pivots), blocks, panel_t), mine


def from_column(values, distance):
    return lax.ppermute(values, "y", [(y, y ^ distance) for y in range(Y)])


def doubled(slices, distance):
    shape = (2 * slices.shape[0], ROWS)
    return call(double_kernel, [shape, (8, LANES)], (), (slices, from_column(slices, distance)), name="double")


def later_phases(cap, room, planes, slices, pivots):
    slices, token = doubled(slices, DISTANCES[0])
    planes = swap(planes, "z")
    pieces = call(pieces_kernel, (Y, 8, LANES), (), (token, planes), name="pieces")
    plan = make_plan(pivots, pieces)
    slices, token = doubled(slices, DISTANCES[1])
    blocks = append(cap, swap(pieces, "y"), collect(cap, room, plan, token, planes))
    slices, _ = doubled(slices, DISTANCES[2])
    multipliers = call(turn_kernel, (ROWS, NB), (), (slices,), [pltpu.VMEM((NB, ROWS), jnp.float32)], name="turn")
    own, multipliers = lax.optimization_barrier((swap(blocks, "x"), multipliers))
    return plan[MOST], own, other_core(own), multipliers


def shards(panel, trailing, pivots):
    panel_t = panel.T

    def with_room(cap, room):
        planes, slices, mine = first_phase(cap, room, panel_t, trailing, pivots)
        most, *ready = later_phases(cap, room, planes, slices, pivots)
        return most, finish(cap, mine, *ready, trailing)

    def pending(carry):
        return carry[0]

    def again(carry):
        return jnp.zeros_like(carry[0]), with_room(NB, 2 * NB)[1]

    most, result = with_room(NARROW, NARROW)
    return lax.while_loop(pending, again, (most > NARROW, result))[1]


def solution(mesh):
    fine = Mesh(mesh.devices.reshape(X, Z, C, Y), ("x", "z", "c", "y"))
    split = P(("x", "z", "c"), "y")
    return jax.shard_map(shards, mesh=fine, in_specs=(split, split, P()), out_specs=split, check_vma=False)
```

```python
import functools

import jax
import jax.numpy as jnp
from jax import lax
from jax.experimental import pallas as pl
from jax.experimental.pallas import tpu as pltpu
from jax.sharding import Mesh, PartitionSpec as P

NB = 256
ORDER = 32768
LANES = 128
X, Z, C, Y = 4, 8, 2, 8
BLOCKS = X * C
ROWS = ORDER // (X * Z * C)
COLS = BLOCKS * LANES
DIAG = NB // Y
BATCH = 16
DISTANCES = (4, 2, 1)
FILLER, PLACE, TOPS = 0, NB, 2 * NB
COUNT = TOPS + NB + 8
MOST = COUNT + Z + 1
TABLE = 1024
BITS = NB.bit_length() - 1
ROW_BITS = ROWS.bit_length() - 1
PLANE_BITS = (ROWS * C).bit_length() - 1
NARROW = 56
HIGHEST = lax.Precision.HIGHEST
VMEM = pl.BlockSpec(memory_space=pltpu.VMEM)
SMEM = pl.BlockSpec(memory_space=pltpu.SMEM)
ANY = pl.BlockSpec(memory_space=pl.ANY)
HBM = pl.BlockSpec(memory_space=pltpu.HBM)
PARAMS = pltpu.CompilerParams(vmem_limit_bytes=48 * 1024 * 1024)


def loop(count, body, unroll=1):
    def step(i, carry):
        body(i)
        return carry

    lax.fori_loop(0, count, step, 0, unroll=unroll)


def tile_of(row):
    return pl.ds(pl.multiple_of(row & -8, 8), 8)


def picked(row, width):
    return lax.broadcasted_iota(jnp.int32, (8, width), 0) == (row & 7)


def load_row(ref, row):
    tile = ref[tile_of(row), :]
    return jnp.sum(jnp.where(picked(row, tile.shape[1]), tile, 0.0), axis=0, keepdims=True)


def store_row(ref, row, values):
    at = tile_of(row)
    tile = ref[at, :]
    ref[at, :] = jnp.where(picked(row, tile.shape[1]), values, tile)


def plane_of(row):
    return (row >> PLANE_BITS) & (Z - 1)


def first_row():
    return ((lax.axis_index("x") * Z + lax.axis_index("z")) * C + lax.axis_index("c")) * ROWS


def plan_kernel(pivots, table, content):
    def start(i):
        content[i] = i
        content[pivots[i]] = pivots[i]

    loop(NB, start, 8)
    for z in range(Z):
        table[COUNT + z] = 0

    def exchange(i, found):
        at = pivots[i]
        left, right = content[i], content[at]
        content[i] = right
        content[at] = left
        table[TOPS + found] = i * NB + right
        plane = plane_of(at)
        have = table[COUNT + plane]
        table[PLACE + i] = plane * NB + have
        table[COUNT + plane] = have + 1
        return found + (right != at).astype(jnp.int32)

    found = lax.fori_loop(0, NB, exchange, jnp.int32(0), unroll=4)

    def fill(i):
        row = pivots[i]
        table[FILLER + i] = jnp.where(row < NB, 0, content[row])

    loop(NB, fill, 8)
    table[COUNT + Z] = found
    peak = table[COUNT]
    for z in range(1, Z):
        peak = jnp.maximum(peak, table[COUNT + z])
    table[MOST] = peak + found


def make_plan(pivots):
    return pl.pallas_call(
        plan_kernel,
        out_shape=jax.ShapeDtypeStruct((TABLE,), jnp.int32),
        in_specs=[SMEM],
        out_specs=SMEM,
        scratch_shapes=[pltpu.SMEM((ORDER,), jnp.int32)],
        compiler_params=PARAMS,
        cost_estimate=pl.CostEstimate(flops=0, bytes_accessed=16 * 1024 * 1024, transcendentals=0),
        name="plan",
    )(pivots)


def invert_diagonal(panel_t, at):
    y = lax.axis_index("y")
    lanes = pl.ds(pl.multiple_of((y * DIAG) & -LANES, LANES), LANES)
    shift = (y * DIAG) & (LANES - 1)
    window = pltpu.roll(panel_t[:, lanes], (LANES - shift) & (LANES - 1), axis=1)
    rows = lax.broadcasted_iota(jnp.int32, (DIAG, LANES), 0)
    cols = lax.broadcasted_iota(jnp.int32, (DIAG, LANES), 1)
    strict = (cols > rows) & (cols < DIAG)
    values = jnp.where(strict, window, 0.0)
    inverse = jnp.where(rows == cols, 1.0, 0.0)
    for k in range(DIAG - 1, 0, -1):
        inverse = inverse - values[:, k : k + 1] * inverse[k : k + 1, :]
    window = jnp.where(strict, inverse, window)
    at[:, :] = panel_t[:, :NB]
    at[:, lanes] = pltpu.roll(window, shift, axis=1)


def local_entry(cap, entry):
    return (entry >> BITS) & (ROWS - 1), jnp.minimum(entry & (NB - 1), cap - 1)


def pack_kernel(cap, pivots, panel_t, trailing, keep, send, mine, triangle, rows, sem):
    copy = pltpu.make_async_copy(trailing, rows, sem)
    copy.start()
    z = lax.axis_index("z")
    c = lax.axis_index("c")
    first = first_row()

    device = first >> ROW_BITS

    def find(i, carry):
        rank, found = carry
        row = pivots[i]
        mine[found] = (row << BITS) + rank
        rank = jnp.where(plane_of(row) == z, rank + 1, rank)
        return rank, jnp.where(row >> ROW_BITS == device, found + 1, found)

    _, found = lax.fori_loop(0, NB, find, (jnp.int32(0), jnp.int32(0)), unroll=16)
    sides = ((keep, c), (send, 1 - c))
    for out, side in sides:
        for x in range(X):
            out[x, :cap, :] = jnp.zeros((cap, LANES), jnp.float32)

    @pl.when(first == 0)
    def _():
        invert_diagonal(panel_t, triangle)

    copy.wait()

    @pl.when(first == 0)
    def _():
        for out, side in sides:
            for x in range(X):
                lanes = pl.ds(pl.multiple_of(side * LANES, LANES), LANES)
                out[x, cap + NB :, :] = triangle[8 * x : 8 * x + 8, lanes]
                lanes = pl.ds(pl.multiple_of((x * C + side) * LANES, LANES), LANES)
                out[x, cap : cap + NB, :] = rows[:NB, lanes]

    def put(k):
        row, rank = local_entry(cap, mine[k])
        at = pl.ds(rank, 1)
        hit = picked(row, LANES)
        for out, side in sides:
            for x in range(X):
                lanes = pl.ds(pl.multiple_of((x * C + side) * LANES, LANES), LANES)
                tile = jnp.where(hit, rows[tile_of(row), lanes], 0.0)
                out[x, at, :] = jnp.sum(tile, axis=0, keepdims=True)

    loop(found, put)
    mine[NB] = found


def join_kernel(cap, keep, got, *blocks):
    x = lax.axis_index("x")
    c = lax.axis_index("c")
    for s, out in enumerate(blocks):
        at = (x + s) & (X - 1)
        out[:cap, :] = keep[at, :cap, :] + got[at, :cap, :]
        out[cap:, :] = jnp.where(c == 0, keep[at, cap:, :], got[at, cap:, :])


def spread_kernel(cap, room, table, *refs):
    blocks, panel_t, out, panel_out, former = refs[:X], *refs[X:]
    x = lax.axis_index("x")
    rows = blocks[0][:cap, :]
    for s in range(1, X):
        rows = rows + blocks[s][:cap, :]
    for z in range(Z):
        out[z, :cap, :] = rows
    panel_out[...] = panel_t[...]

    @pl.when(lax.axis_index("z") == 0)
    def _():
        rest = blocks[0][cap:, :]
        for s in range(1, X):
            rest = jnp.where(x == s, blocks[s][cap:, :], rest)
        former[...] = rest
        for z in range(Z):
            out[z, cap + room :, :] = former[NB:, :]

        def put(k):
            moves = []
            for i in range(BATCH):
                where = table[PLACE + k * BATCH + i]
                rank = jnp.minimum(where & (NB - 1), cap - 1)
                filler = table[FILLER + k * BATCH + i]
                moves.append((where >> BITS, cap + rank, former[pl.ds(filler, 1), :]))
            for plane, at, values in moves:
                out[plane, pl.ds(at, 1), :] = values

        loop(NB // BATCH, put)

        def top(k):
            values = former[pl.ds(table[TOPS + k] & (NB - 1), 1), :]
            for z in range(Z):
                at = cap + jnp.minimum(table[COUNT + z] + k, room - 1)
                out[z, pl.ds(at, 1), :] = values

        loop(table[COUNT + Z], top)


def pieces_kernel(token, got, out):
    for y in range(Y):
        out[y] = got[0, got.shape[1] - 8 :, :]


def collect_kernel(cap, room, table, token, got, out, block, sem):
    z = lax.axis_index("z")

    def take(k):
        base = pl.multiple_of(k * BATCH, BATCH)
        rows = []
        for i in range(BATCH):
            where = table[PLACE + base + i]
            rank = jnp.minimum(where & (NB - 1), cap - 1)
            rows.append(got[where >> BITS, pl.ds(rank, 1), :])
        for i in range(BATCH):
            block[pl.ds(base + i, 1), :] = rows[i]

    loop(NB // BATCH, take)

    def top(k):
        at = cap + jnp.minimum(table[COUNT + z] + k, room - 1)
        block[pl.ds(table[TOPS + k] >> BITS, 1), :] = got[0, pl.ds(at, 1), :]

    loop(table[COUNT + Z], top)
    block[NB:, :] = got[0, cap : 2 * cap, :]
    copies = [pltpu.make_async_copy(block, out.at[x, pl.ds(0, NB + cap), :], sem.at[x]) for x in range(X)]
    for copy in copies:
        copy.start()
    for copy in copies:
        copy.wait()


def append_kernel(cap, pieces, blocks, out, rows, sem):
    for y in range(Y):
        rows[8 * y : 8 * y + 8, :] = pieces[y]
    copies = [pltpu.make_async_copy(rows, out.at[x, pl.ds(NB + cap, 8 * Y), :], sem.at[x]) for x in range(X)]
    for copy in copies:
        copy.start()
    for copy in copies:
        copy.wait()


def dot(a, b):
    return jnp.dot(a, b, precision=HIGHEST, preferred_element_type=jnp.float32)


def invert(upper):
    half = NB // 2
    rows = lax.broadcasted_iota(jnp.int32, (half, half), 0)
    cols = lax.broadcasted_iota(jnp.int32, (half, half), 1)
    parts = []
    for k in range(2):
        values = upper[k * half : (k + 1) * half, k * half : (k + 1) * half]
        part = jnp.where((rows // DIAG == cols // DIAG) & (rows < cols), values, 0.0)
        part = part + jnp.where(rows == cols, 1.0, 0.0)
        parts.append((values, part))
    size = DIAG
    while size < half:
        mask = (rows // (2 * size) == cols // (2 * size)) & (rows // size < cols // size)
        parts = [(v, p - dot(dot(p, jnp.where(mask, v, 0.0)), p)) for v, p in parts]
        size *= 2
    (_, first), (_, second) = parts
    corner = -dot(dot(first, upper[:half, half:]), second)
    left = jnp.concatenate([first.T, corner.T], axis=0)
    right = jnp.concatenate([jnp.zeros((half, half), jnp.float32), second.T], axis=0)
    return jnp.concatenate([left, right], axis=1)


def double_kernel(first, second, out, token):
    half = first.shape[0]
    out[:half] = first[...]
    out[half:] = second[...]
    token[...] = second[:8, :LANES]


def turn_kernel(slices, out, ordered):
    y = lax.axis_index("y")
    columns = [y]
    for distance in DISTANCES:
        columns += [column ^ distance for column in columns]
    for k, column in enumerate(columns):
        at = pl.ds(pl.multiple_of(column * DIAG, DIAG), DIAG)
        ordered[at, :] = slices[k * DIAG : (k + 1) * DIAG, :]
    out[...] = ordered[...].T


def finish_kernel(cap, mine, own, other, multipliers, trailing, out,
                  upper, inverse, block, current, in_sem, out_sem):
    copy = pltpu.make_async_copy(trailing, current, in_sem)
    copy.start()
    c = lax.axis_index("c")
    first = first_row()
    sides = ((pl.multiple_of(c * LANES, LANES), own), (pl.multiple_of((1 - c) * LANES, LANES), other))
    for x in range(X):
        for lane, ref in sides:
            for y in range(Y):
                at = DIAG * y + 8 * x
                upper[at : at + 8, pl.ds(lane, LANES)] = ref[x, NB + cap + 8 * y : NB + cap + 8 * y + 8, :]
    inverse[...] = invert(upper)
    copy.wait()

    def put(k):
        row, rank = local_entry(cap, mine[k])
        rank = pl.ds(NB + rank, 1)
        at = tile_of(row)
        hit = picked(row, LANES)
        for x in range(X):
            for lane, ref in sides:
                lanes = pl.ds(pl.multiple_of(x * C * LANES + lane, LANES), LANES)
                current[at, lanes] = jnp.where(hit, ref[x, rank, :], current[at, lanes])

    loop(mine[NB], put)
    width = C * LANES

    def write(x):
        lanes = pl.ds(pl.multiple_of(x * width, width), width)
        return pltpu.make_async_copy(current.at[:, lanes], out.at[:, lanes], out_sem.at[x])

    def solve(x):
        slot = x & 1
        for lane, ref in sides:
            block[slot, :, pl.ds(lane, LANES)] = ref[x, :NB, :]
        block[slot] = dot(inverse[...], block[slot])

    def update(x):
        lanes = pl.ds(pl.multiple_of(x * width, width), width)
        slot = x & 1
        current[:, lanes] = current[:, lanes] - dot(multipliers[...], block[slot])

        @pl.when(first == 0)
        def _():
            current[:NB, lanes] = block[slot]

        write(x).start()

    def both(x):
        lanes = pl.ds(pl.multiple_of(x * width, width), width)
        slot = x & 1
        for lane, ref in sides:
            block[1 - slot, :, pl.ds(lane, LANES)] = ref[x + 1, :NB, :]
        solved = dot(inverse[...], block[1 - slot])
        product = dot(multipliers[...], block[slot])
        block[1 - slot] = solved
        current[:, lanes] = current[:, lanes] - product

        @pl.when(first == 0)
        def _():
            current[:NB, lanes] = block[slot]

        write(x).start()

    solve(0)
    loop(X - 1, both)
    update(X - 1)
    for x in range(X):
        write(x).wait()


def call(kernel, shape, smem, vmem, scratch=(), name=None, last=VMEM, out=VMEM, busy=2, table=None, aliases={}):
    many = isinstance(shape, list)
    shapes = [jax.ShapeDtypeStruct(s, jnp.float32) for s in (shape if many else [shape])]
    specs = [out] * len(shapes)
    if table is not None:
        shapes.append(jax.ShapeDtypeStruct((table,), jnp.int32))
        specs.append(SMEM)
    got = pl.pallas_call(
        kernel,
        out_shape=shapes,
        in_specs=[SMEM] * len(smem) + [VMEM] * (len(vmem) - 1) + [last],
        out_specs=specs,
        scratch_shapes=list(scratch),
        compiler_params=PARAMS,
        input_output_aliases=aliases,
        cost_estimate=pl.CostEstimate(flops=0, bytes_accessed=busy * 2**20, transcendentals=0),
        name=name,
    )(*smem, *vmem)
    return list(got) if many else got[0]


def pack(cap, pivots, trailing, panel_t):
    scratch = [pltpu.VMEM((DIAG, NB), jnp.float32), pltpu.VMEM((ROWS, COLS), jnp.float32), pltpu.SemaphoreType.DMA]
    return call(functools.partial(pack_kernel, cap), [(X, cap + NB + 8, LANES)] * 2,
                (pivots,), (panel_t, trailing), scratch, name="pack", last=ANY, table=NB + 8)


def join(cap, keep, got):
    return call(functools.partial(join_kernel, cap), [keep.shape[1:]] * X, (), (keep, got), name="join")


def spread(cap, room, plan, blocks, panel_t):
    return call(functools.partial(spread_kernel, cap, room), [(Z, cap + room + 8, LANES), panel_t.shape],
                (plan,), (*blocks, panel_t), [pltpu.VMEM((NB + 8, LANES), jnp.float32)], name="spread")


def collect(cap, room, plan, token, planes):
    scratch = [pltpu.VMEM((NB + cap, LANES), jnp.float32), pltpu.SemaphoreType.DMA((X,))]
    return call(functools.partial(collect_kernel, cap, room), (X, NB + cap + 8 * Y, LANES),
                (plan,), (token, planes), scratch, name="collect", out=HBM)


def append(cap, pieces, blocks):
    scratch = [pltpu.VMEM((8 * Y, LANES), jnp.float32), pltpu.SemaphoreType.DMA((X,))]
    return call(functools.partial(append_kernel, cap), blocks.shape, (), (pieces, blocks), scratch,
                name="append", last=HBM, out=HBM, aliases={1: 0})


def finish(cap, mine, own, other, multipliers, trailing):
    scratch = [pltpu.VMEM(s, jnp.float32) for s in ((NB, NB), (NB, NB), (2, NB, C * LANES), (ROWS, COLS))]
    scratch += [pltpu.SemaphoreType.DMA, pltpu.SemaphoreType.DMA((X,))]
    return call(functools.partial(finish_kernel, cap), (ROWS, COLS), (mine,),
                (own, other, multipliers, trailing), scratch, name="finish",
                last=ANY, out=HBM, busy=16)


swap = functools.partial(lax.all_to_all, split_axis=0, concat_axis=0, tiled=True)


def other_core(values):
    return lax.ppermute(values, "c", [(0, 1), (1, 0)])


def first_phase(cap, room, panel_t, trailing, pivots):
    keep, send, mine = pack(cap, pivots, trailing, panel_t)
    blocks = join(cap, keep, other_core(send))
    for s in range(1, X):
        blocks[s] = lax.ppermute(blocks[s], "x", [(x, (x + s) % X) for x in range(X)])
    plan = make_plan(pivots)
    return *spread(cap, room, plan, blocks, panel_t), plan, mine


def from_column(values, distance):
    return lax.ppermute(values, "y", [(y, y ^ distance) for y in range(Y)])


def doubled(slices, distance):
    shape = (2 * slices.shape[0], ROWS)
    return call(double_kernel, [shape, (8, LANES)], (), (slices, from_column(slices, distance)), name="double")


def later_phases(cap, room, planes, slices, plan):
    slices, token = doubled(slices, DISTANCES[0])
    planes = swap(planes, "z")
    pieces = call(pieces_kernel, (Y, 8, LANES), (), (token, planes), name="pieces")
    slices, token = doubled(slices, DISTANCES[1])
    blocks = append(cap, swap(pieces, "y"), collect(cap, room, plan, token, planes))
    slices, _ = doubled(slices, DISTANCES[2])
    multipliers = call(turn_kernel, (ROWS, NB), (), (slices,), [pltpu.VMEM((NB, ROWS), jnp.float32)], name="turn")
    own, multipliers = lax.optimization_barrier((swap(blocks, "x"), multipliers))
    return own, other_core(own), multipliers


def shards(panel, trailing, pivots):
    panel_t = panel.T

    def with_room(cap, room):
        planes, slices, plan, mine = first_phase(cap, room, panel_t, trailing, pivots)
        ready = later_phases(cap, room, planes, slices, plan)
        return plan[MOST], finish(cap, mine, *ready, trailing)

    def pending(carry):
        return carry[0]

    def again(carry):
        return jnp.zeros_like(carry[0]), with_room(NB, 2 * NB)[1]

    most, result = with_room(NARROW, NARROW)
    return lax.while_loop(pending, again, (most > NARROW, result))[1]


def solution(mesh):
    fine = Mesh(mesh.devices.reshape(X, Z, C, Y), ("x", "z", "c", "y"))
    split = P(("x", "z", "c"), "y")
    return jax.shard_map(shards, mesh=fine, in_specs=(split, split, P()), out_specs=split, check_vma=False)
```

```python
import functools

import jax
import jax.numpy as jnp
from jax import lax
from jax.experimental import pallas as pl
from jax.experimental.pallas import tpu as pltpu
from jax.sharding import Mesh, PartitionSpec as P

NB = 256
ORDER = 32768
LANES = 128
X, Z, C, Y = 4, 8, 2, 8
BLOCKS = X * C
ROWS = ORDER // (X * Z * C)
COLS = BLOCKS * LANES
DIAG = NB // Y
BATCH = 16
DISTANCES = (4, 2, 1)
FILLER, PLACE, TOPS = 0, NB, 2 * NB
COUNT = TOPS + NB + 8
MOST = COUNT + Z + 1
TABLE = 1024
BITS = NB.bit_length() - 1
ROW_BITS = ROWS.bit_length() - 1
PLANE_BITS = (ROWS * C).bit_length() - 1
NARROW = 56
HIGHEST = lax.Precision.HIGHEST
VMEM = pl.BlockSpec(memory_space=pltpu.VMEM)
SMEM = pl.BlockSpec(memory_space=pltpu.SMEM)
ANY = pl.BlockSpec(memory_space=pl.ANY)
HBM = pl.BlockSpec(memory_space=pltpu.HBM)
PARAMS = pltpu.CompilerParams(vmem_limit_bytes=48 * 1024 * 1024)


def loop(count, body, unroll=1):
    def step(i, carry):
        body(i)
        return carry

    lax.fori_loop(0, count, step, 0, unroll=unroll)


def tile_of(row):
    return pl.ds(pl.multiple_of(row & -8, 8), 8)


def picked(row, width):
    return lax.broadcasted_iota(jnp.int32, (8, width), 0) == (row & 7)


def load_row(ref, row):
    tile = ref[tile_of(row), :]
    return jnp.sum(jnp.where(picked(row, tile.shape[1]), tile, 0.0), axis=0, keepdims=True)


def store_row(ref, row, values):
    at = tile_of(row)
    tile = ref[at, :]
    ref[at, :] = jnp.where(picked(row, tile.shape[1]), values, tile)


def plane_of(row):
    return (row >> PLANE_BITS) & (Z - 1)


def first_row():
    return ((lax.axis_index("x") * Z + lax.axis_index("z")) * C + lax.axis_index("c")) * ROWS


def plan_kernel(pivots, table, content):
    def start(i):
        content[i] = i
        content[pivots[i]] = pivots[i]

    loop(NB, start, 8)
    for z in range(Z):
        table[COUNT + z] = 0

    def exchange(i, found):
        at = pivots[i]
        left, right = content[i], content[at]
        content[i] = right
        content[at] = left
        table[TOPS + found] = i * NB + right
        plane = plane_of(at)
        have = table[COUNT + plane]
        table[PLACE + i] = plane * NB + have
        table[COUNT + plane] = have + 1
        return found + (right != at).astype(jnp.int32)

    found = lax.fori_loop(0, NB, exchange, jnp.int32(0), unroll=4)

    def fill(i):
        row = pivots[i]
        table[FILLER + i] = jnp.where(row < NB, 0, content[row])

    loop(NB, fill, 8)
    table[COUNT + Z] = found
    peak = table[COUNT]
    for z in range(1, Z):
        peak = jnp.maximum(peak, table[COUNT + z])
    table[MOST] = peak + found


def early_plan_kernel(pivots, table, content):
    @pl.when(lax.axis_index("z") == 0)
    def _():
        plan_kernel(pivots, table, content)


def late_plan_kernel(pivots, early, after, table, content):
    z = lax.axis_index("z")

    @pl.when(z == 0)
    def _():
        table[MOST] = early[MOST]

    @pl.when(z != 0)
    def _():
        plan_kernel(pivots, table, content)


def make_plan(kernel, *args):
    return pl.pallas_call(
        kernel,
        out_shape=jax.ShapeDtypeStruct((TABLE,), jnp.int32),
        in_specs=[SMEM, SMEM, VMEM][: len(args)],
        out_specs=SMEM,
        scratch_shapes=[pltpu.SMEM((ORDER,), jnp.int32)],
        compiler_params=PARAMS,
        cost_estimate=pl.CostEstimate(flops=0, bytes_accessed=16 * 1024 * 1024, transcendentals=0),
        name="plan",
    )(*args)


def invert_diagonal(panel_t, at):
    y = lax.axis_index("y")
    lanes = pl.ds(pl.multiple_of((y * DIAG) & -LANES, LANES), LANES)
    shift = (y * DIAG) & (LANES - 1)
    window = pltpu.roll(panel_t[:, lanes], (LANES - shift) & (LANES - 1), axis=1)
    rows = lax.broadcasted_iota(jnp.int32, (DIAG, LANES), 0)
    cols = lax.broadcasted_iota(jnp.int32, (DIAG, LANES), 1)
    strict = (cols > rows) & (cols < DIAG)
    values = jnp.where(strict, window, 0.0)
    inverse = jnp.where(rows == cols, 1.0, 0.0)
    for k in range(DIAG - 1, 0, -1):
        inverse = inverse - values[:, k : k + 1] * inverse[k : k + 1, :]
    window = jnp.where(strict, inverse, window)
    at[:, :] = panel_t[:, :NB]
    at[:, lanes] = pltpu.roll(window, shift, axis=1)


def local_entry(cap, entry):
    return (entry >> BITS) & (ROWS - 1), jnp.minimum(entry & (NB - 1), cap - 1)


def pack_kernel(cap, pivots, panel_t, trailing, keep, send, mine, triangle, rows, sem):
    copy = pltpu.make_async_copy(trailing, rows, sem)
    copy.start()
    z = lax.axis_index("z")
    c = lax.axis_index("c")
    first = first_row()

    device = first >> ROW_BITS

    def find(i, carry):
        rank, found = carry
        row = pivots[i]
        mine[found] = (row << BITS) + rank
        rank = jnp.where(plane_of(row) == z, rank + 1, rank)
        return rank, jnp.where(row >> ROW_BITS == device, found + 1, found)

    _, found = lax.fori_loop(0, NB, find, (jnp.int32(0), jnp.int32(0)), unroll=16)
    sides = ((keep, c), (send, 1 - c))
    for out, side in sides:
        for x in range(X):
            out[x, :cap, :] = jnp.zeros((cap, LANES), jnp.float32)

    @pl.when(first == 0)
    def _():
        invert_diagonal(panel_t, triangle)

    copy.wait()

    @pl.when(first == 0)
    def _():
        for out, side in sides:
            for x in range(X):
                lanes = pl.ds(pl.multiple_of(side * LANES, LANES), LANES)
                out[x, cap + NB :, :] = triangle[8 * x : 8 * x + 8, lanes]
                lanes = pl.ds(pl.multiple_of((x * C + side) * LANES, LANES), LANES)
                out[x, cap : cap + NB, :] = rows[:NB, lanes]

    def put(k):
        row, rank = local_entry(cap, mine[k])
        at = pl.ds(rank, 1)
        hit = picked(row, LANES)
        for out, side in sides:
            for x in range(X):
                lanes = pl.ds(pl.multiple_of((x * C + side) * LANES, LANES), LANES)
                tile = jnp.where(hit, rows[tile_of(row), lanes], 0.0)
                out[x, at, :] = jnp.sum(tile, axis=0, keepdims=True)

    loop(found, put)
    mine[NB] = found


def join_kernel(cap, keep, got, *blocks):
    x = lax.axis_index("x")
    c = lax.axis_index("c")
    for s, out in enumerate(blocks):
        at = (x + s) & (X - 1)
        out[:cap, :] = keep[at, :cap, :] + got[at, :cap, :]
        out[cap:, :] = jnp.where(c == 0, keep[at, cap:, :], got[at, cap:, :])


def spread_kernel(cap, room, table, *refs):
    blocks, panel_t, out, panel_out, former = refs[:X], *refs[X:]
    x = lax.axis_index("x")
    rows = blocks[0][:cap, :]
    for s in range(1, X):
        rows = rows + blocks[s][:cap, :]
    for z in range(Z):
        out[z, :cap, :] = rows
    panel_out[...] = panel_t[...]

    @pl.when(lax.axis_index("z") == 0)
    def _():
        rest = blocks[0][cap:, :]
        for s in range(1, X):
            rest = jnp.where(x == s, blocks[s][cap:, :], rest)
        former[...] = rest
        for z in range(Z):
            out[z, cap + room :, :] = former[NB:, :]

        def put(k):
            moves = []
            for i in range(BATCH):
                where = table[PLACE + k * BATCH + i]
                rank = jnp.minimum(where & (NB - 1), cap - 1)
                filler = table[FILLER + k * BATCH + i]
                moves.append((where >> BITS, cap + rank, former[pl.ds(filler, 1), :]))
            for plane, at, values in moves:
                out[plane, pl.ds(at, 1), :] = values

        loop(NB // BATCH, put)

        def top(k):
            values = former[pl.ds(table[TOPS + k] & (NB - 1), 1), :]
            for z in range(Z):
                at = cap + jnp.minimum(table[COUNT + z] + k, room - 1)
                out[z, pl.ds(at, 1), :] = values

        loop(table[COUNT + Z], top)


def pieces_kernel(token, got, out):
    for y in range(Y):
        out[y] = got[0, got.shape[1] - 8 :, :]


def collect_kernel(cap, room, early, late, token, got, out, block, sem):
    z = lax.axis_index("z")

    def assemble(table):
        def take(k):
            base = pl.multiple_of(k * BATCH, BATCH)
            rows = []
            for i in range(BATCH):
                where = table[PLACE + base + i]
                rank = jnp.minimum(where & (NB - 1), cap - 1)
                rows.append(got[where >> BITS, pl.ds(rank, 1), :])
            for i in range(BATCH):
                block[pl.ds(base + i, 1), :] = rows[i]

        loop(NB // BATCH, take)

        def top(k):
            at = cap + jnp.minimum(table[COUNT + z] + k, room - 1)
            block[pl.ds(table[TOPS + k] >> BITS, 1), :] = got[0, pl.ds(at, 1), :]

        loop(table[COUNT + Z], top)

    pl.when(z == 0)(lambda: assemble(early))
    pl.when(z != 0)(lambda: assemble(late))
    block[NB:, :] = got[0, cap : 2 * cap, :]
    copies = [pltpu.make_async_copy(block, out.at[x, pl.ds(0, NB + cap), :], sem.at[x]) for x in range(X)]
    for copy in copies:
        copy.start()
    for copy in copies:
        copy.wait()


def append_kernel(cap, pieces, blocks, out, rows, sem):
    for y in range(Y):
        rows[8 * y : 8 * y + 8, :] = pieces[y]
    copies = [pltpu.make_async_copy(rows, out.at[x, pl.ds(NB + cap, 8 * Y), :], sem.at[x]) for x in range(X)]
    for copy in copies:
        copy.start()
    for copy in copies:
        copy.wait()


def dot(a, b):
    return jnp.dot(a, b, precision=HIGHEST, preferred_element_type=jnp.float32)


def invert(upper):
    half = NB // 2
    rows = lax.broadcasted_iota(jnp.int32, (half, half), 0)
    cols = lax.broadcasted_iota(jnp.int32, (half, half), 1)
    parts = []
    for k in range(2):
        values = upper[k * half : (k + 1) * half, k * half : (k + 1) * half]
        part = jnp.where((rows // DIAG == cols // DIAG) & (rows < cols), values, 0.0)
        part = part + jnp.where(rows == cols, 1.0, 0.0)
        parts.append((values, part))
    size = DIAG
    while size < half:
        mask = (rows // (2 * size) == cols // (2 * size)) & (rows // size < cols // size)
        parts = [(v, p - dot(dot(p, jnp.where(mask, v, 0.0)), p)) for v, p in parts]
        size *= 2
    (_, first), (_, second) = parts
    corner = -dot(dot(first, upper[:half, half:]), second)
    left = jnp.concatenate([first.T, corner.T], axis=0)
    right = jnp.concatenate([jnp.zeros((half, half), jnp.float32), second.T], axis=0)
    return jnp.concatenate([left, right], axis=1)


def double_kernel(first, second, out, token):
    half = first.shape[0]
    out[:half] = first[...]
    out[half:] = second[...]
    token[...] = second[:8, :LANES]


def turn_kernel(slices, out, ordered):
    y = lax.axis_index("y")
    columns = [y]
    for distance in DISTANCES:
        columns += [column ^ distance for column in columns]
    for k, column in enumerate(columns):
        at = pl.ds(pl.multiple_of(column * DIAG, DIAG), DIAG)
        ordered[at, :] = slices[k * DIAG : (k + 1) * DIAG, :]
    out[...] = ordered[...].T


def finish_kernel(cap, mine, own, other, multipliers, trailing, out,
                  upper, inverse, block, current, in_sem, out_sem):
    copy = pltpu.make_async_copy(trailing, current, in_sem)
    copy.start()
    c = lax.axis_index("c")
    first = first_row()
    sides = ((pl.multiple_of(c * LANES, LANES), own), (pl.multiple_of((1 - c) * LANES, LANES), other))
    for x in range(X):
        for lane, ref in sides:
            for y in range(Y):
                at = DIAG * y + 8 * x
                upper[at : at + 8, pl.ds(lane, LANES)] = ref[x, NB + cap + 8 * y : NB + cap + 8 * y + 8, :]
    inverse[...] = invert(upper)
    copy.wait()

    def put(k):
        row, rank = local_entry(cap, mine[k])
        rank = pl.ds(NB + rank, 1)
        at = tile_of(row)
        hit = picked(row, LANES)
        for x in range(X):
            for lane, ref in sides:
                lanes = pl.ds(pl.multiple_of(x * C * LANES + lane, LANES), LANES)
                current[at, lanes] = jnp.where(hit, ref[x, rank, :], current[at, lanes])

    loop(mine[NB], put)
    width = C * LANES

    def write(x):
        lanes = pl.ds(pl.multiple_of(x * width, width), width)
        return pltpu.make_async_copy(current.at[:, lanes], out.at[:, lanes], out_sem.at[x])

    def solve(x):
        slot = x & 1
        for lane, ref in sides:
            block[slot, :, pl.ds(lane, LANES)] = ref[x, :NB, :]
        block[slot] = dot(inverse[...], block[slot])

    def update(x):
        lanes = pl.ds(pl.multiple_of(x * width, width), width)
        slot = x & 1
        current[:, lanes] = current[:, lanes] - dot(multipliers[...], block[slot])

        @pl.when(first == 0)
        def _():
            current[:NB, lanes] = block[slot]

        write(x).start()

    def both(x):
        lanes = pl.ds(pl.multiple_of(x * width, width), width)
        slot = x & 1
        for lane, ref in sides:
            block[1 - slot, :, pl.ds(lane, LANES)] = ref[x + 1, :NB, :]
        solved = dot(inverse[...], block[1 - slot])
        product = dot(multipliers[...], block[slot])
        block[1 - slot] = solved
        current[:, lanes] = current[:, lanes] - product

        @pl.when(first == 0)
        def _():
            current[:NB, lanes] = block[slot]

        write(x).start()

    solve(0)
    loop(X - 1, both)
    update(X - 1)
    for x in range(X):
        write(x).wait()


def call(kernel, shape, smem, vmem, scratch=(), name=None, last=VMEM, out=VMEM, busy=2, table=None, aliases={}):
    many = isinstance(shape, list)
    shapes = [jax.ShapeDtypeStruct(s, jnp.float32) for s in (shape if many else [shape])]
    specs = [out] * len(shapes)
    if table is not None:
        shapes.append(jax.ShapeDtypeStruct((table,), jnp.int32))
        specs.append(SMEM)
    got = pl.pallas_call(
        kernel,
        out_shape=shapes,
        in_specs=[SMEM] * len(smem) + [VMEM] * (len(vmem) - 1) + [last],
        out_specs=specs,
        scratch_shapes=list(scratch),
        compiler_params=PARAMS,
        input_output_aliases=aliases,
        cost_estimate=pl.CostEstimate(flops=0, bytes_accessed=busy * 2**20, transcendentals=0),
        name=name,
    )(*smem, *vmem)
    return list(got) if many else got[0]


def pack(cap, pivots, trailing, panel_t):
    scratch = [pltpu.VMEM((DIAG, NB), jnp.float32), pltpu.VMEM((ROWS, COLS), jnp.float32), pltpu.SemaphoreType.DMA]
    return call(functools.partial(pack_kernel, cap), [(X, cap + NB + 8, LANES)] * 2,
                (pivots,), (panel_t, trailing), scratch, name="pack", last=ANY, table=NB + 8)


def join(cap, keep, got):
    return call(functools.partial(join_kernel, cap), [keep.shape[1:]] * X, (), (keep, got), name="join")


def spread(cap, room, plan, blocks, panel_t):
    return call(functools.partial(spread_kernel, cap, room), [(Z, cap + room + 8, LANES), panel_t.shape],
                (plan,), (*blocks, panel_t), [pltpu.VMEM((NB + 8, LANES), jnp.float32)], name="spread")


def collect(cap, room, plans, token, planes):
    scratch = [pltpu.VMEM((NB + cap, LANES), jnp.float32), pltpu.SemaphoreType.DMA((X,))]
    return call(functools.partial(collect_kernel, cap, room), (X, NB + cap + 8 * Y, LANES),
                plans, (token, planes), scratch, name="collect", out=HBM)


def append(cap, pieces, blocks):
    scratch = [pltpu.VMEM((8 * Y, LANES), jnp.float32), pltpu.SemaphoreType.DMA((X,))]
    return call(functools.partial(append_kernel, cap), blocks.shape, (), (pieces, blocks), scratch,
                name="append", last=HBM, out=HBM, aliases={1: 0})


def finish(cap, mine, own, other, multipliers, trailing):
    scratch = [pltpu.VMEM(s, jnp.float32) for s in ((NB, NB), (NB, NB), (2, NB, C * LANES), (ROWS, COLS))]
    scratch += [pltpu.SemaphoreType.DMA, pltpu.SemaphoreType.DMA((X,))]
    return call(functools.partial(finish_kernel, cap), (ROWS, COLS), (mine,),
                (own, other, multipliers, trailing), scratch, name="finish",
                last=ANY, out=HBM, busy=16)


swap = functools.partial(lax.all_to_all, split_axis=0, concat_axis=0, tiled=True)


def other_core(values):
    return lax.ppermute(values, "c", [(0, 1), (1, 0)])


def first_phase(cap, room, panel_t, trailing, pivots):
    keep, send, mine = pack(cap, pivots, trailing, panel_t)
    blocks = join(cap, keep, other_core(send))
    for s in range(1, X):
        blocks[s] = lax.ppermute(blocks[s], "x", [(x, (x + s) % X) for x in range(X)])
    plan = make_plan(early_plan_kernel, pivots)
    return *spread(cap, room, plan, blocks, panel_t), plan, mine


def from_column(values, distance):
    return lax.ppermute(values, "y", [(y, y ^ distance) for y in range(Y)])


def doubled(slices, distance):
    shape = (2 * slices.shape[0], ROWS)
    return call(double_kernel, [shape, (8, LANES)], (), (slices, from_column(slices, distance)), name="double")


def later_phases(cap, room, planes, slices, pivots, early):
    slices, token = doubled(slices, DISTANCES[0])
    planes = swap(planes, "z")
    pieces = call(pieces_kernel, (Y, 8, LANES), (), (token, planes), name="pieces")
    late = make_plan(late_plan_kernel, pivots, early, pieces)
    slices, token = doubled(slices, DISTANCES[1])
    blocks = append(cap, swap(pieces, "y"), collect(cap, room, (early, late), token, planes))
    slices, _ = doubled(slices, DISTANCES[2])
    multipliers = call(turn_kernel, (ROWS, NB), (), (slices,), [pltpu.VMEM((NB, ROWS), jnp.float32)], name="turn")
    own, multipliers = lax.optimization_barrier((swap(blocks, "x"), multipliers))
    return late[MOST], own, other_core(own), multipliers


def shards(panel, trailing, pivots):
    panel_t = panel.T

    def with_room(cap, room):
        planes, slices, plan, mine = first_phase(cap, room, panel_t, trailing, pivots)
        most, *ready = later_phases(cap, room, planes, slices, pivots, plan)
        return most, finish(cap, mine, *ready, trailing)

    def pending(carry):
        return carry[0]

    def again(carry):
        return jnp.zeros_like(carry[0]), with_room(NB, 2 * NB)[1]

    most, result = with_room(NARROW, NARROW)
    return lax.while_loop(pending, again, (most > NARROW, result))[1]


def solution(mesh):
    fine = Mesh(mesh.devices.reshape(X, Z, C, Y), ("x", "z", "c", "y"))
    split = P(("x", "z", "c"), "y")
    return jax.shard_map(shards, mesh=fine, in_specs=(split, split, P()), out_specs=split, check_vma=False)
```

```python
import functools

import jax
import jax.numpy as jnp
from jax import lax
from jax.experimental import pallas as pl
from jax.experimental.pallas import tpu as pltpu
from jax.sharding import Mesh, PartitionSpec as P

NB = 256
ORDER = 32768
LANES = 128
X, Z, C, Y = 4, 8, 2, 8
BLOCKS = X * C
ROWS = ORDER // (X * Z * C)
COLS = BLOCKS * LANES
DIAG = NB // Y
BATCH = 16
DISTANCES = (4, 2, 1)
FILLER, PLACE, TOPS = 0, NB, 2 * NB
COUNT = TOPS + NB + 8
MOST = COUNT + Z + 1
TABLE = 1024
BITS = NB.bit_length() - 1
ROW_BITS = ROWS.bit_length() - 1
PLANE_BITS = (ROWS * C).bit_length() - 1
NARROW = 56
HIGHEST = lax.Precision.HIGHEST
VMEM = pl.BlockSpec(memory_space=pltpu.VMEM)
SMEM = pl.BlockSpec(memory_space=pltpu.SMEM)
ANY = pl.BlockSpec(memory_space=pl.ANY)
HBM = pl.BlockSpec(memory_space=pltpu.HBM)
PARAMS = pltpu.CompilerParams(vmem_limit_bytes=48 * 1024 * 1024)


def loop(count, body, unroll=1):
    def step(i, carry):
        body(i)
        return carry

    lax.fori_loop(0, count, step, 0, unroll=unroll)


def tile_of(row):
    return pl.ds(pl.multiple_of(row & -8, 8), 8)


def picked(row, width):
    return lax.broadcasted_iota(jnp.int32, (8, width), 0) == (row & 7)


def load_row(ref, row):
    tile = ref[tile_of(row), :]
    return jnp.sum(jnp.where(picked(row, tile.shape[1]), tile, 0.0), axis=0, keepdims=True)


def store_row(ref, row, values):
    at = tile_of(row)
    tile = ref[at, :]
    ref[at, :] = jnp.where(picked(row, tile.shape[1]), values, tile)


def plane_of(row):
    return (row >> PLANE_BITS) & (Z - 1)


def first_row():
    return ((lax.axis_index("x") * Z + lax.axis_index("z")) * C + lax.axis_index("c")) * ROWS


def plan_kernel(pivots, table, content, fillers):
    def start(i):
        content[i] = i
        content[pivots[i]] = pivots[i]

    loop(NB, start, 8)
    for z in range(Z):
        table[COUNT + z] = 0

    def exchange(i, found):
        at = pivots[i]
        left, right = content[i], content[at]
        content[i] = right
        content[at] = left
        table[TOPS + found] = i * NB + right
        plane = plane_of(at)
        have = table[COUNT + plane]
        table[PLACE + i] = plane * NB + have
        table[COUNT + plane] = have + 1
        return found + (right != at).astype(jnp.int32)

    found = lax.fori_loop(0, NB, exchange, jnp.int32(0), unroll=4)

    def fill(i):
        row = pivots[i]
        table[FILLER + i] = jnp.where(row < NB, 0, content[row])

    if fillers:
        loop(NB, fill, 8)
    table[COUNT + Z] = found
    peak = table[COUNT]
    for z in range(1, Z):
        peak = jnp.maximum(peak, table[COUNT + z])
    table[MOST] = peak + found


def early_plan_kernel(pivots, table, content):
    @pl.when(lax.axis_index("z") == 0)
    def _():
        plan_kernel(pivots, table, content, True)


def late_plan_kernel(pivots, early, after, table, content):
    z = lax.axis_index("z")

    @pl.when(z == 0)
    def _():
        table[MOST] = early[MOST]

    @pl.when(z != 0)
    def _():
        plan_kernel(pivots, table, content, False)


def make_plan(kernel, *args):
    return pl.pallas_call(
        kernel,
        out_shape=jax.ShapeDtypeStruct((TABLE,), jnp.int32),
        in_specs=[SMEM, SMEM, VMEM][: len(args)],
        out_specs=SMEM,
        scratch_shapes=[pltpu.SMEM((ORDER,), jnp.int32)],
        compiler_params=PARAMS,
        cost_estimate=pl.CostEstimate(flops=0, bytes_accessed=16 * 1024 * 1024, transcendentals=0),
        name="plan",
    )(*args)


def invert_diagonal(panel_t, at):
    y = lax.axis_index("y")
    lanes = pl.ds(pl.multiple_of((y * DIAG) & -LANES, LANES), LANES)
    shift = (y * DIAG) & (LANES - 1)
    window = pltpu.roll(panel_t[:, lanes], (LANES - shift) & (LANES - 1), axis=1)
    rows = lax.broadcasted_iota(jnp.int32, (DIAG, LANES), 0)
    cols = lax.broadcasted_iota(jnp.int32, (DIAG, LANES), 1)
    strict = (cols > rows) & (cols < DIAG)
    values = jnp.where(strict, window, 0.0)
    inverse = jnp.where(rows == cols, 1.0, 0.0)
    for k in range(DIAG - 1, 0, -1):
        inverse = inverse - values[:, k : k + 1] * inverse[k : k + 1, :]
    window = jnp.where(strict, inverse, window)
    at[:, :] = panel_t[:, :NB]
    at[:, lanes] = pltpu.roll(window, shift, axis=1)


def local_entry(cap, entry):
    return (entry >> BITS) & (ROWS - 1), jnp.minimum(entry & (NB - 1), cap - 1)


def pack_kernel(cap, pivots, panel_t, trailing, keep, send, mine, triangle, rows, sem):
    copy = pltpu.make_async_copy(trailing, rows, sem)
    copy.start()
    z = lax.axis_index("z")
    c = lax.axis_index("c")
    first = first_row()

    device = first >> ROW_BITS

    def find(i, carry):
        rank, found = carry
        row = pivots[i]
        mine[found] = (row << BITS) + rank
        rank = jnp.where(plane_of(row) == z, rank + 1, rank)
        return rank, jnp.where(row >> ROW_BITS == device, found + 1, found)

    _, found = lax.fori_loop(0, NB, find, (jnp.int32(0), jnp.int32(0)), unroll=16)
    sides = ((keep, c), (send, 1 - c))
    for out, side in sides:
        for x in range(X):
            out[x, :cap, :] = jnp.zeros((cap, LANES), jnp.float32)

    @pl.when(first == 0)
    def _():
        invert_diagonal(panel_t, triangle)

    copy.wait()

    @pl.when(first == 0)
    def _():
        for out, side in sides:
            for x in range(X):
                lanes = pl.ds(pl.multiple_of(side * LANES, LANES), LANES)
                out[x, cap + NB :, :] = triangle[8 * x : 8 * x + 8, lanes]
                lanes = pl.ds(pl.multiple_of((x * C + side) * LANES, LANES), LANES)
                out[x, cap : cap + NB, :] = rows[:NB, lanes]

    def put(k):
        row, rank = local_entry(cap, mine[k])
        at = pl.ds(rank, 1)
        hit = picked(row, LANES)
        for out, side in sides:
            for x in range(X):
                lanes = pl.ds(pl.multiple_of((x * C + side) * LANES, LANES), LANES)
                tile = jnp.where(hit, rows[tile_of(row), lanes], 0.0)
                out[x, at, :] = jnp.sum(tile, axis=0, keepdims=True)

    loop(found, put)
    mine[NB] = found


def join_kernel(cap, keep, got, *blocks):
    x = lax.axis_index("x")
    c = lax.axis_index("c")
    for s, out in enumerate(blocks):
        at = (x + s) & (X - 1)
        out[:cap, :] = keep[at, :cap, :] + got[at, :cap, :]
        out[cap:, :] = jnp.where(c == 0, keep[at, cap:, :], got[at, cap:, :])


def spread_kernel(cap, room, table, *refs):
    blocks, panel_t, out, panel_out, former = refs[:X], *refs[X:]
    x = lax.axis_index("x")
    rows = blocks[0][:cap, :]
    for s in range(1, X):
        rows = rows + blocks[s][:cap, :]
    for z in range(Z):
        out[z, :cap, :] = rows
    panel_out[...] = panel_t[...]

    @pl.when(lax.axis_index("z") == 0)
    def _():
        rest = blocks[0][cap:, :]
        for s in range(1, X):
            rest = jnp.where(x == s, blocks[s][cap:, :], rest)
        former[...] = rest
        for z in range(Z):
            out[z, cap + room :, :] = former[NB:, :]

        def put(k):
            moves = []
            for i in range(BATCH):
                where = table[PLACE + k * BATCH + i]
                rank = jnp.minimum(where & (NB - 1), cap - 1)
                filler = table[FILLER + k * BATCH + i]
                moves.append((where >> BITS, cap + rank, former[pl.ds(filler, 1), :]))
            for plane, at, values in moves:
                out[plane, pl.ds(at, 1), :] = values

        loop(NB // BATCH, put)

        def top(k):
            values = former[pl.ds(table[TOPS + k] & (NB - 1), 1), :]
            for z in range(Z):
                at = cap + jnp.minimum(table[COUNT + z] + k, room - 1)
                out[z, pl.ds(at, 1), :] = values

        loop(table[COUNT + Z], top)


def pieces_kernel(token, got, out):
    for y in range(Y):
        out[y] = got[0, got.shape[1] - 8 :, :]


def collect_kernel(cap, room, early, late, token, got, out, block, sem):
    z = lax.axis_index("z")

    def assemble(table):
        def take(k):
            base = pl.multiple_of(k * BATCH, BATCH)
            rows = []
            for i in range(BATCH):
                where = table[PLACE + base + i]
                rank = jnp.minimum(where & (NB - 1), cap - 1)
                rows.append(got[where >> BITS, pl.ds(rank, 1), :])
            for i in range(BATCH):
                block[pl.ds(base + i, 1), :] = rows[i]

        loop(NB // BATCH, take)

        def top(k):
            at = cap + jnp.minimum(table[COUNT + z] + k, room - 1)
            block[pl.ds(table[TOPS + k] >> BITS, 1), :] = got[0, pl.ds(at, 1), :]

        loop(table[COUNT + Z], top)

    pl.when(z == 0)(lambda: assemble(early))
    pl.when(z != 0)(lambda: assemble(late))
    block[NB:, :] = got[0, cap : 2 * cap, :]
    copies = [pltpu.make_async_copy(block, out.at[x, pl.ds(0, NB + cap), :], sem.at[x]) for x in range(X)]
    for copy in copies:
        copy.start()
    for copy in copies:
        copy.wait()


def append_kernel(cap, pieces, blocks, out, rows, sem):
    for y in range(Y):
        rows[8 * y : 8 * y + 8, :] = pieces[y]
    copies = [pltpu.make_async_copy(rows, out.at[x, pl.ds(NB + cap, 8 * Y), :], sem.at[x]) for x in range(X)]
    for copy in copies:
        copy.start()
    for copy in copies:
        copy.wait()


def dot(a, b):
    return jnp.dot(a, b, precision=HIGHEST, preferred_element_type=jnp.float32)


def invert(upper):
    half = NB // 2
    rows = lax.broadcasted_iota(jnp.int32, (half, half), 0)
    cols = lax.broadcasted_iota(jnp.int32, (half, half), 1)
    parts = []
    for k in range(2):
        values = upper[k * half : (k + 1) * half, k * half : (k + 1) * half]
        part = jnp.where((rows // DIAG == cols // DIAG) & (rows < cols), values, 0.0)
        part = part + jnp.where(rows == cols, 1.0, 0.0)
        parts.append((values, part))
    size = DIAG
    while size < half:
        mask = (rows // (2 * size) == cols // (2 * size)) & (rows // size < cols // size)
        parts = [(v, p - dot(dot(p, jnp.where(mask, v, 0.0)), p)) for v, p in parts]
        size *= 2
    (_, first), (_, second) = parts
    corner = -dot(dot(first, upper[:half, half:]), second)
    left = jnp.concatenate([first.T, corner.T], axis=0)
    right = jnp.concatenate([jnp.zeros((half, half), jnp.float32), second.T], axis=0)
    return jnp.concatenate([left, right], axis=1)


def double_kernel(first, second, out, token):
    half = first.shape[0]
    out[:half] = first[...]
    out[half:] = second[...]
    token[...] = second[:8, :LANES]


def turn_kernel(slices, out, ordered):
    y = lax.axis_index("y")
    columns = [y]
    for distance in DISTANCES:
        columns += [column ^ distance for column in columns]
    for k, column in enumerate(columns):
        at = pl.ds(pl.multiple_of(column * DIAG, DIAG), DIAG)
        ordered[at, :] = slices[k * DIAG : (k + 1) * DIAG, :]
    out[...] = ordered[...].T


def finish_kernel(cap, mine, own, other, multipliers, trailing, out,
                  upper, inverse, block, current, in_sem, out_sem):
    copy = pltpu.make_async_copy(trailing, current, in_sem)
    copy.start()
    c = lax.axis_index("c")
    first = first_row()
    sides = ((pl.multiple_of(c * LANES, LANES), own), (pl.multiple_of((1 - c) * LANES, LANES), other))
    for x in range(X):
        for lane, ref in sides:
            for y in range(Y):
                at = DIAG * y + 8 * x
                upper[at : at + 8, pl.ds(lane, LANES)] = ref[x, NB + cap + 8 * y : NB + cap + 8 * y + 8, :]
    inverse[...] = invert(upper)
    copy.wait()

    def put(k):
        row, rank = local_entry(cap, mine[k])
        rank = pl.ds(NB + rank, 1)
        at = tile_of(row)
        hit = picked(row, LANES)
        for x in range(X):
            for lane, ref in sides:
                lanes = pl.ds(pl.multiple_of(x * C * LANES + lane, LANES), LANES)
                current[at, lanes] = jnp.where(hit, ref[x, rank, :], current[at, lanes])

    loop(mine[NB], put)
    width = C * LANES

    def write(x):
        lanes = pl.ds(pl.multiple_of(x * width, width), width)
        return pltpu.make_async_copy(current.at[:, lanes], out.at[:, lanes], out_sem.at[x])

    def solve(x):
        slot = x & 1
        for lane, ref in sides:
            block[slot, :, pl.ds(lane, LANES)] = ref[x, :NB, :]
        block[slot] = dot(inverse[...], block[slot])

    def update(x):
        lanes = pl.ds(pl.multiple_of(x * width, width), width)
        slot = x & 1
        current[:, lanes] = current[:, lanes] - dot(multipliers[...], block[slot])

        @pl.when(first == 0)
        def _():
            current[:NB, lanes] = block[slot]

        write(x).start()

    def both(x):
        lanes = pl.ds(pl.multiple_of(x * width, width), width)
        slot = x & 1
        for lane, ref in sides:
            block[1 - slot, :, pl.ds(lane, LANES)] = ref[x + 1, :NB, :]
        solved = dot(inverse[...], block[1 - slot])
        half = ROWS // 2
        product = [dot(multipliers[k * half : (k + 1) * half], block[slot]) for k in range(2)]
        block[1 - slot] = solved
        for k in range(2):
            current[k * half : (k + 1) * half, lanes] -= product[k]

        @pl.when(first == 0)
        def _():
            current[:NB, lanes] = block[slot]

        write(x).start()

    solve(0)
    loop(X - 1, both)
    update(X - 1)
    for x in range(X):
        write(x).wait()


def call(kernel, shape, smem, vmem, scratch=(), name=None, last=VMEM, out=VMEM, busy=2, table=None, aliases={}):
    many = isinstance(shape, list)
    shapes = [jax.ShapeDtypeStruct(s, jnp.float32) for s in (shape if many else [shape])]
    specs = [out] * len(shapes)
    if table is not None:
        shapes.append(jax.ShapeDtypeStruct((table,), jnp.int32))
        specs.append(SMEM)
    got = pl.pallas_call(
        kernel,
        out_shape=shapes,
        in_specs=[SMEM] * len(smem) + [VMEM] * (len(vmem) - 1) + [last],
        out_specs=specs,
        scratch_shapes=list(scratch),
        compiler_params=PARAMS,
        input_output_aliases=aliases,
        cost_estimate=pl.CostEstimate(flops=0, bytes_accessed=busy * 2**20, transcendentals=0),
        name=name,
    )(*smem, *vmem)
    return list(got) if many else got[0]


def pack(cap, pivots, trailing, panel_t):
    scratch = [pltpu.VMEM((DIAG, NB), jnp.float32), pltpu.VMEM((ROWS, COLS), jnp.float32), pltpu.SemaphoreType.DMA]
    return call(functools.partial(pack_kernel, cap), [(X, cap + NB + 8, LANES)] * 2,
                (pivots,), (panel_t, trailing), scratch, name="pack", last=ANY, table=NB + 8)


def join(cap, keep, got):
    return call(functools.partial(join_kernel, cap), [keep.shape[1:]] * X, (), (keep, got), name="join")


def spread(cap, room, plan, blocks, panel_t):
    return call(functools.partial(spread_kernel, cap, room), [(Z, cap + room + 8, LANES), panel_t.shape],
                (plan,), (*blocks, panel_t), [pltpu.VMEM((NB + 8, LANES), jnp.float32)], name="spread")


def collect(cap, room, plans, token, planes):
    scratch = [pltpu.VMEM((NB + cap, LANES), jnp.float32), pltpu.SemaphoreType.DMA((X,))]
    return call(functools.partial(collect_kernel, cap, room), (X, NB + cap + 8 * Y, LANES),
                plans, (token, planes), scratch, name="collect", out=HBM)


def append(cap, pieces, blocks):
    scratch = [pltpu.VMEM((8 * Y, LANES), jnp.float32), pltpu.SemaphoreType.DMA((X,))]
    return call(functools.partial(append_kernel, cap), blocks.shape, (), (pieces, blocks), scratch,
                name="append", last=HBM, out=HBM, aliases={1: 0})


def finish(cap, mine, own, other, multipliers, trailing):
    scratch = [pltpu.VMEM(s, jnp.float32) for s in ((NB, NB), (NB, NB), (2, NB, C * LANES), (ROWS, COLS))]
    scratch += [pltpu.SemaphoreType.DMA, pltpu.SemaphoreType.DMA((X,))]
    return call(functools.partial(finish_kernel, cap), (ROWS, COLS), (mine,),
                (own, other, multipliers, trailing), scratch, name="finish",
                last=ANY, out=HBM, busy=16)


swap = functools.partial(lax.all_to_all, split_axis=0, concat_axis=0, tiled=True)


def other_core(values):
    return lax.ppermute(values, "c", [(0, 1), (1, 0)])


def first_phase(cap, room, panel_t, trailing, pivots):
    keep, send, mine = pack(cap, pivots, trailing, panel_t)
    blocks = join(cap, keep, other_core(send))
    for s in range(1, X):
        blocks[s] = lax.ppermute(blocks[s], "x", [(x, (x + s) % X) for x in range(X)])
    plan = make_plan(early_plan_kernel, pivots)
    return *spread(cap, room, plan, blocks, panel_t), plan, mine


def from_column(values, distance):
    return lax.ppermute(values, "y", [(y, y ^ distance) for y in range(Y)])


def doubled(slices, distance):
    shape = (2 * slices.shape[0], ROWS)
    return call(double_kernel, [shape, (8, LANES)], (), (slices, from_column(slices, distance)), name="double")


def later_phases(cap, room, planes, slices, pivots, early):
    slices, token = doubled(slices, DISTANCES[0])
    planes = swap(planes, "z")
    pieces = call(pieces_kernel, (Y, 8, LANES), (), (token, planes), name="pieces")
    late = make_plan(late_plan_kernel, pivots, early, pieces)
    slices, token = doubled(slices, DISTANCES[1])
    blocks = append(cap, swap(pieces, "y"), collect(cap, room, (early, late), token, planes))
    slices, _ = doubled(slices, DISTANCES[2])
    multipliers = call(turn_kernel, (ROWS, NB), (), (slices,), [pltpu.VMEM((NB, ROWS), jnp.float32)], name="turn")
    own, multipliers = lax.optimization_barrier((swap(blocks, "x"), multipliers))
    return late[MOST], own, other_core(own), multipliers


def shards(panel, trailing, pivots):
    panel_t = panel.T

    def with_room(cap, room):
        planes, slices, plan, mine = first_phase(cap, room, panel_t, trailing, pivots)
        most, *ready = later_phases(cap, room, planes, slices, pivots, plan)
        return most, finish(cap, mine, *ready, trailing)

    def pending(carry):
        return carry[0]

    def again(carry):
        return jnp.zeros_like(carry[0]), with_room(NB, 2 * NB)[1]

    most, result = with_room(NARROW, NARROW)
    return lax.while_loop(pending, again, (most > NARROW, result))[1]


def solution(mesh):
    fine = Mesh(mesh.devices.reshape(X, Z, C, Y), ("x", "z", "c", "y"))
    split = P(("x", "z", "c"), "y")
    return jax.shard_map(shards, mesh=fine, in_specs=(split, split, P()), out_specs=split, check_vma=False)
```
